256 devices in a mesh: row: 8 (over z_hi, y), col: 32 (over z_lo, x, core).
Axes of the slice: x: 4, y: 4, z: 8 (z_hi: 2, z_lo: 4; z = z_hi * 4 + z_lo), core: 2. Of those that a mesh axis runs over, the one named last changes fastest.
Arguments:
- start_block: float32 [32, 16384], P(None, 'col'), may hold values from -6 to 6
- energies: float32 [16384], P('col'), may hold values from 1 to 10
- hamiltonian: float32 [32, 32, 512, 512], P('row', 'col'), may hold values from -0.09375 to 0.09375
Outputs:
- recurrence: float32 [2, 2, 32, 32], replicated
- next_block: float32 [32, 16384], P(None, 'col')
The draws below stay inside these ranges and needn't reach their ends.
All inputs are finite; a program needn't handle non-finite values.
Results may differ from the reference program's by a relative error of at most 0.0003.
Values sent between devices are 32-bit elements; how exact they have to be, the bound alone decides.
No kernel may reach another device: no remote copies, remote signals or barrier semaphores. Data moves between devices by JAX's collectives and lax.ppermute only.
A program may use at most 64 MiB of HBM per device.

```python
import math
import jax
import jax.numpy as jnp
from jax import lax

VECS = 32
BLK = 512
ITERS = 2
NBLK = 32
N = 16384
N_ROW = 8


def block_scale(own_key, dims, split, smallest, top_value):
    gain, own = 1.0, jax.random.fold_in(own_key, 6)
    for position, parts in split:
        heights = jnp.exp(jax.random.uniform(jax.random.fold_in(own, position), (parts,), jnp.float32, smallest / len(split), top_value / len(split)))
        gain = gain * jnp.repeat(heights, dims[position] // parts).reshape([-1 if axis == position else 1 for axis in range(len(dims))])
    return gain


def bell_draw(own_key, shape, deviation, reach, split=(), held_as=jnp.bfloat16):
    factor_of = block_scale(own_key, shape, split, -0.22, 0.18) if split else 1.0
    entries = jax.random.normal(own_key, shape, jnp.float32) * deviation * factor_of
    return jnp.minimum(jnp.maximum(entries, -reach), reach).astype(held_as)


def setup_inputs(seed: int = 0) -> dict:
    arg_keys = jax.random.split(jax.random.key(seed), 4)
    start_block = bell_draw(arg_keys[0], (VECS, N), 1.0, 6.0, ((1, 32),), jnp.float32)
    energies = jnp.clip(jnp.exp(math.log(10.0) - 2.3025851 * jax.random.uniform(arg_keys[1], (N,), jnp.float32) ** block_scale(arg_keys[1], (N,), ((0, 32),), -0.2, 0.2)), 1.0, 10.0)
    hamiltonian = bell_draw(arg_keys[2], (NBLK, NBLK, BLK, BLK), (N // 4) ** -0.5, 0.09375, ((0, 8), (1, 32)), jnp.float32)
    return dict(start_block=start_block, energies=energies, hamiltonian=hamiltonian)


FULL_PRECISION = lax.Precision.HIGHEST

def apply_operator(vectors, energies, hamiltonian):
    slot_count = NBLK // N_ROW
    stored = jnp.arange(NBLK, dtype=jnp.int32)
    block_of = (stored % slot_count * N_ROW + stored // slot_count).astype(jnp.int32)
    where_is = (stored % N_ROW * slot_count + stored // N_ROW).astype(jnp.int32)
    by_block = vectors.reshape(VECS, NBLK, BLK).transpose(1, 0, 2)
    in_stored = by_block[block_of]

    def column(running, column_index):
        col_blocks = lax.dynamic_index_in_dim(hamiltonian, column_index, 1, keepdims=False)
        weight = jnp.where(block_of < column_index, jnp.float32(1.0), jnp.where(block_of == column_index, jnp.float32(0.5), jnp.float32(0.0))).astype(jnp.float32)
        downward = jnp.einsum('ipk,ikl->pl', in_stored * weight[:, None, None], col_blocks, precision=FULL_PRECISION)
        own_block = lax.dynamic_index_in_dim(by_block, column_index, 0, keepdims=False)
        across = jnp.einsum('pl,ikl->ipk', own_block, col_blocks, precision=FULL_PRECISION) * weight[:, None, None]
        return (running + across, downward)
    across_total, downs = lax.scan(column, jnp.zeros((NBLK, VECS, BLK), jnp.float32), jnp.arange(NBLK, dtype=jnp.int32))
    summed = downs + across_total[where_is]
    return summed.transpose(1, 0, 2).reshape(VECS, NBLK * BLK) + energies[None, :] * vectors

def mean_inner(left, right):
    return jnp.dot(left, right.T, precision=FULL_PRECISION) / N

def normalize(block):
    factor = jnp.linalg.cholesky(mean_inner(block, block))
    return (lax.linalg.triangular_solve(factor, block, left_side=True, lower=True), factor)

def reference(start_block, energies, hamiltonian):
    current, factor = normalize(start_block)
    previous = jnp.zeros_like(current)
    last_factor = jnp.zeros((VECS, VECS), jnp.float32)
    history = []
    for iteration in range(ITERS):
        residual_block = apply_operator(current, energies, hamiltonian) - jnp.dot(last_factor.T, previous, precision=FULL_PRECISION)
        diagonal_block = mean_inner(residual_block, current)
        residual_block = residual_block - jnp.dot(diagonal_block, current, precision=FULL_PRECISION)
        following, new_factor = normalize(residual_block)
        history.append(jnp.stack([diagonal_block, new_factor]))
        previous, current, last_factor = (current, following, new_factor)
    return (jnp.stack(history), current)
```

```python
import jax
import jax.numpy as jnp
from jax import lax
from jax.sharding import Mesh
from jax.sharding import PartitionSpec as P

SHIFT = 5.5
FULL = lax.Precision.HIGHEST
BLOCKS = lax.Precision.HIGH

SIZES = (2, 4, 4, 4, 2)
NAMES = ("zh", "y", "z", "x", "co")
ROW = ("zh", "y")
COL = ("z", "x", "co")

PLACE = (
    (5, 3, 2, 4, 7, 1, 0, 6),
    (2, 4, 5, 3, 0, 6, 7, 1),
    (0, 1, 7, 6, 2, 3, 5, 4),
    (7, 0, 4, 6, 2, 3, 1, 5),
    (3, 5, 4, 2, 1, 0, 6, 7),
    (4, 2, 3, 5, 1, 0, 6, 7),
    (6, 0, 1, 7, 4, 2, 3, 5),
    (1, 7, 6, 0, 3, 5, 4, 2),
)


def to_row_group():
    pairs = []
    for row in range(8):
        for z in range(4):
            for j in range(8):
                far = (row // 4) != (j // 4)
                z_to = (z + 2) % 4 if far else z
                pairs.append((row * 32 + z * 8 + j, j * 32 + z_to * 8 + PLACE[j][row]))
    return pairs


def from_row_group():
    return [(b, a) for a, b in to_row_group()]


def far_table():
    table = [[0.0] * 8 for _ in range(8)]
    for j in range(8):
        for row in range(8):
            table[j][PLACE[j][row]] = float((row // 4) != (j // 4))
    return table


def inverse_of_lower(factor):
    eye = jnp.eye(factor.shape[0], dtype=factor.dtype)
    return lax.linalg.triangular_solve(factor, eye, left_side=True, lower=True)


def mm(a, b):
    return jnp.dot(a, b, precision=FULL)


def recurrence(gram):
    n = gram.shape[0] // 3
    eye = jnp.eye(n, dtype=jnp.float32)
    g = [[gram[i * n : (i + 1) * n, k * n : (k + 1) * n] for k in range(3)] for i in range(3)]
    lower0 = jnp.linalg.cholesky(g[0][0])
    t0 = inverse_of_lower(lower0)
    a0 = mm(mm(t0, g[1][0]), t0.T)
    zero = jnp.zeros_like(t0)
    p1 = jnp.concatenate([-mm(a0, t0), t0, zero], axis=1)
    g1 = mm(mm(p1, gram), p1.T)
    lower1 = jnp.linalg.cholesky(g1)
    t1 = inverse_of_lower(lower1)
    q1 = mm(t1, p1)
    w1 = jnp.concatenate([-mm(lower1.T, t0), q1[:, :n], q1[:, n : 2 * n]], axis=1)
    a1 = mm(mm(w1, gram), q1.T)
    w1 = w1 - mm(a1, q1)
    g2 = mm(mm(w1, gram), w1.T)
    lower2 = jnp.linalg.cholesky(g2)
    q2 = mm(inverse_of_lower(lower2), w1)
    history = jnp.stack(
        [jnp.stack([a0 + SHIFT * eye, lower1]), jnp.stack([a1 + SHIFT * eye, lower2])]
    )
    return history, q2


def on_device(start_block, energies, hamiltonian):
    vecs, width = start_block.shape
    half = width // 2
    row = lax.axis_index(ROW)
    col = lax.axis_index(COL)
    z = lax.axis_index("z")
    core = lax.axis_index("co")
    place = lax.axis_index(("x", "co"))
    blocks = hamiltonian[:, 0]
    slots = blocks.shape[0]
    block_rows = row + 8 * jnp.arange(slots, dtype=jnp.int32)
    weight = jnp.where(block_rows < col, 1.0, jnp.where(block_rows == col, 0.5, 0.0)).astype(
        jnp.float32
    )[:, None, None]
    lead = (row == 0).astype(jnp.float32) * (energies - SHIFT)
    table = jnp.array(far_table(), jnp.float32).reshape(-1)
    far = jnp.sum(table * (jnp.arange(64) == row * 8 + place).astype(jnp.float32)) > 0.5
    slot = jnp.where(far, (z + 2) % 4, z)
    in_slot = (jnp.arange(slots) == slot)[:, None, None]
    every = NAMES

    def down(four, own):
        product = jnp.einsum("spk,skl->pl", four * weight, blocks, precision=BLOCKS)
        return product + lead[None, :] * own

    def across(own):
        return jnp.einsum("pl,skl->spk", own, blocks, precision=BLOCKS) * weight

    def total(acrosses, downs):
        arrived = lax.ppermute(downs, every, to_row_group())
        part = acrosses + jnp.where(in_slot, arrived[None], 0.0)
        part = part.reshape(slots * vecs // 8, 8, width)
        low, high = part[..., :half], part[..., half:]
        mine = jnp.where(core == 0, low, high)
        other = jnp.where(core == 0, high, low)
        mine = mine + lax.ppermute(other, "co", [(0, 1), (1, 0)])
        piece = lax.all_to_all(mine, ("z", "x"), 0, 0, tiled=True).sum(axis=0)
        whole = lax.all_to_all(
            jnp.broadcast_to(piece[None], mine.shape), ("z", "x"), 0, 0, tiled=True
        )
        facing = lax.ppermute(whole, "co", [(0, 1), (1, 0)])
        low = jnp.where(core == 0, whole, facing)
        high = jnp.where(core == 0, facing, whole)
        return jnp.concatenate([low, high], axis=-1).reshape(slots, vecs, width)

    def to_column(four):
        mine = jnp.sum(jnp.where(in_slot, four, 0.0), axis=0)
        return lax.ppermute(mine, every, from_row_group())

    moved = lax.ppermute(start_block, every, to_row_group())
    x4 = lax.all_to_all(
        jnp.broadcast_to(moved[None], (slots, vecs, width)), "z", 0, 0, tiled=True
    )
    x4 = jnp.where(far, jnp.roll(x4, 2, axis=0), x4)
    x = start_block
    y4 = total(across(x), down(x4, x))
    y = to_column(y4)
    z4 = total(across(y), down(y4, y))
    zz = to_column(z4)

    basis4 = jnp.concatenate([x4, y4, z4], axis=1)
    gram = jnp.einsum("spk,sqk->pq", basis4, basis4, precision=FULL)
    gram = lax.all_to_all(
        jnp.broadcast_to(gram[None], (8, *gram.shape)), ROW, 0, 0, tiled=True
    ).sum(axis=0)
    gram = gram / (32 * width)
    history, q2 = recurrence(gram)
    following = mm(q2, jnp.concatenate([x, y, zz], axis=0))
    return history, following


def solution(mesh):
    fine = Mesh(mesh.devices.reshape(SIZES), NAMES)
    placed = (P(None, COL), P(COL), P(ROW, COL, None, None))
    return jax.shard_map(
        on_device, mesh=fine, in_specs=placed, out_specs=(P(), P(None, COL)), check_vma=False
    )
```

```python
import functools

import jax
import jax.numpy as jnp
from jax import lax
from jax.experimental import pallas as pl
from jax.experimental.pallas import tpu as pltpu
from jax.sharding import Mesh
from jax.sharding import PartitionSpec as P

SHIFT = 5.5
FULL = lax.Precision.HIGHEST
BLOCKS = lax.Precision.HIGH

SIZES = (2, 4, 4, 4, 2)
NAMES = ("zh", "y", "z", "x", "co")
ROW = ("zh", "y")
COL = ("z", "x", "co")

PLACE = (
    (5, 3, 2, 4, 7, 1, 0, 6),
    (2, 4, 5, 3, 0, 6, 7, 1),
    (0, 1, 7, 6, 2, 3, 5, 4),
    (7, 0, 4, 6, 2, 3, 1, 5),
    (3, 5, 4, 2, 1, 0, 6, 7),
    (4, 2, 3, 5, 1, 0, 6, 7),
    (6, 0, 1, 7, 4, 2, 3, 5),
    (1, 7, 6, 0, 3, 5, 4, 2),
)


def to_row_group():
    pairs = []
    for row in range(8):
        for z in range(4):
            for j in range(8):
                far = (row // 4) != (j // 4)
                z_to = (z + 2) % 4 if far else z
                pairs.append((row * 32 + z * 8 + j, j * 32 + z_to * 8 + PLACE[j][row]))
    return pairs


def from_row_group():
    return [(b, a) for a, b in to_row_group()]


def far_table():
    table = [[0.0] * 8 for _ in range(8)]
    for j in range(8):
        for row in range(8):
            table[j][PLACE[j][row]] = float((row // 4) != (j // 4))
    return table


def mm(a, b):
    return jnp.dot(a, b, precision=FULL, preferred_element_type=jnp.float32)
def mmt(a, b):
    return lax.dot_general(a, b, (((1,), (1,)), ((), ())), precision=FULL, preferred_element_type=jnp.float32)


def factor_and_inverse(g):
    n = g.shape[0]
    down = lax.broadcasted_iota(jnp.int32, (n, 2 * n), 0)
    along = lax.broadcasted_iota(jnp.int32, (n, 2 * n), 1)
    same = (down == along)[:, :n]
    diagonal = jnp.where(same, g, 0.0)
    root = jnp.sqrt(jnp.sum(diagonal, axis=0, keepdims=True))
    root_down = jnp.sqrt(jnp.sum(diagonal, axis=1, keepdims=True))
    wide = jnp.concatenate([g / root, jnp.where(same, 1.0, 0.0)], axis=1) / root_down
    for k in range(0, n - 2, 2):
        r0 = jnp.broadcast_to(wide[k : k + 1, :], (8, 2 * n))
        r1 = jnp.broadcast_to(wide[k + 1 : k + 2, :], (8, 2 * n))
        a = jnp.broadcast_to(r0[:, k : k + 1], r0.shape)
        b = jnp.broadcast_to(r0[:, k + 1 : k + 2], r0.shape)
        c = jnp.broadcast_to(r1[:, k + 1 : k + 2], r0.shape)
        c0 = jnp.broadcast_to(wide[:, k : k + 1], wide.shape)
        c1 = jnp.broadcast_to(wide[:, k + 1 : k + 2], wide.shape)
        det = 1.0 / (a * c - b * b)
        s0 = jnp.concatenate([(r0 * c - r1 * b) * det] * (n // 8), axis=0)
        s1 = jnp.concatenate([(r1 * a - r0 * b) * det] * (n // 8), axis=0)
        wide = jnp.where(down > k + 1, wide - (c0 * s0 + c1 * s1), wide)
    above = jnp.roll(wide, 1, axis=0)
    left = down - 1 == along
    b = jnp.sum(jnp.where(left, wide, 0.0), axis=1, keepdims=True)
    a = jnp.sum(jnp.where(left, above, 0.0), axis=1, keepdims=True)
    wide = jnp.where(lax.rem(down, 2) == 1, wide - (b / a) * above, wide)
    pivot = jnp.sum(jnp.where(down == along, wide, 0.0), axis=1, keepdims=True)
    wide = wide * (1.0 / jnp.sqrt(pivot))
    upper = jnp.where(down <= along, wide, 0.0)[:, :n] * root
    return jnp.transpose(upper), wide[:, n:]


def finish(scale, grams_ref, x_ref, y_ref, z_ref, hist_ref, out_ref, g_ref, p_ref, v_ref):
    n = 32
    part = jnp.sum(grams_ref[...], axis=0) * scale
    at = 0
    for i in range(3):
        for k in range(i + 1):
            block = part[:, at * n : (at + 1) * n]
            g_ref[i * n : (i + 1) * n, k * n : (k + 1) * n] = block
            if k < i:
                g_ref[k * n : (k + 1) * n, i * n : (i + 1) * n] = jnp.transpose(block)
            at += 1
    v_ref[0:n] = x_ref[...]
    v_ref[n : 2 * n] = y_ref[...]
    v_ref[2 * n :] = z_ref[...]
    eye = jnp.where(
        lax.broadcasted_iota(jnp.int32, (n, n), 0) == lax.broadcasted_iota(jnp.int32, (n, n), 1),
        SHIFT,
        0.0,
    )
    low0, t0 = factor_and_inverse(g_ref[0:n, 0:n])
    a0 = mmt(mm(t0, g_ref[n : 2 * n, 0:n]), t0)
    hist_ref[0, 0] = a0 + eye
    m0 = mm(a0, t0)
    p_ref[:, 0:n] = -m0
    p_ref[:, n : 2 * n] = t0
    p1 = p_ref[:, 0 : 2 * n]
    low1, t1 = factor_and_inverse(mmt(mm(p1, g_ref[0 : 2 * n, 0 : 2 * n]), p1))
    hist_ref[0, 1] = low1
    q1 = mm(t1, p1)
    d0 = lax.dot_general(
        low1, t0, (((0,), (0,)), ((), ())), precision=FULL, preferred_element_type=jnp.float32
    )
    p_ref[:, 0:n] = -d0
    p_ref[:, n : 3 * n] = q1
    w1 = p_ref[...]
    a1 = mmt(mm(w1, g_ref[:, 0 : 2 * n]), q1)
    hist_ref[1, 0] = a1 + eye
    p_ref[:, 0 : 2 * n] = mm(a1, q1)
    w1 = jnp.concatenate([w1[:, 0 : 2 * n] - p_ref[:, 0 : 2 * n], w1[:, 2 * n :]], axis=1)
    low2, t2 = factor_and_inverse(mmt(mm(w1, g_ref[...]), w1))
    hist_ref[1, 1] = low2
    out_ref[...] = mm(t2, mm(w1, v_ref[...]))


def close(grams, x, y, z, length):
    vecs = x.shape[0]
    return pl.pallas_call(
        functools.partial(finish, 1.0 / length),
        out_shape=(
            jax.ShapeDtypeStruct((2, 2, vecs, vecs), jnp.float32),
            jax.ShapeDtypeStruct(x.shape, jnp.float32),
        ),
        scratch_shapes=[
            pltpu.VMEM((3 * vecs, 3 * vecs), jnp.float32),
            pltpu.VMEM((vecs, 3 * vecs), jnp.float32),
            pltpu.VMEM((3 * vecs, x.shape[1]), jnp.float32),
        ],
        name="recurrence",
    )(grams, x, y, z)


def on_device(start_block, energies, hamiltonian):
    vecs, width = start_block.shape
    col_count = lax.axis_size(COL)
    half = width // 2
    row = lax.axis_index(ROW)
    col = lax.axis_index(COL)
    z = lax.axis_index("z")
    core = lax.axis_index("co")
    place = lax.axis_index(("x", "co"))
    blocks = hamiltonian[:, 0]
    slots = blocks.shape[0]
    block_rows = row + 8 * jnp.arange(slots, dtype=jnp.int32)
    weight = jnp.where(block_rows < col, 1.0, jnp.where(block_rows == col, 0.5, 0.0)).astype(
        jnp.float32
    )[:, None, None]
    lead = jnp.where(place == row, energies - SHIFT, 0.0)
    own_slot = (jnp.arange(slots) == z)[:, None, None]
    table = jnp.array(far_table(), jnp.float32).reshape(-1)
    far = jnp.sum(table * (jnp.arange(64) == row * 8 + place).astype(jnp.float32)) > 0.5
    slot = jnp.where(far, (z + 2) % 4, z)
    in_slot = (jnp.arange(slots) == slot)[:, None, None]
    every = NAMES

    def down(four):
        return jnp.einsum("spk,skl->pl", four * weight, blocks, precision=BLOCKS)

    def across(own):
        product = jnp.einsum("pl,skl->spk", own, blocks, precision=BLOCKS) * weight
        return product + jnp.where(own_slot, (lead[None, :] * own)[None], 0.0)

    def total(acrosses, downs):
        arrived = lax.ppermute(downs, every, to_row_group())
        part = acrosses + jnp.where(in_slot, arrived[None], 0.0)
        part = part.reshape(slots * vecs // 8, 8, width)
        low, high = part[..., :half], part[..., half:]
        mine = jnp.where(core == 0, low, high)
        other = jnp.where(core == 0, high, low)
        mine = mine + lax.ppermute(other, "co", [(0, 1), (1, 0)])
        piece = lax.all_to_all(mine, ("z", "x"), 0, 0, tiled=True).sum(axis=0)
        whole = lax.all_to_all(
            jnp.broadcast_to(piece[None], mine.shape), ("z", "x"), 0, 0, tiled=True
        )
        facing = lax.ppermute(whole, "co", [(0, 1), (1, 0)])
        low = jnp.where(core == 0, whole, facing)
        high = jnp.where(core == 0, facing, whole)
        return jnp.concatenate([low, high], axis=-1).reshape(slots, vecs, width)

    def slot_of(four):
        return jnp.sum(jnp.where(in_slot, four, 0.0), axis=0)

    def inner(left, right):
        return jnp.einsum("spk,sqk->pq", left, right, precision=FULL)

    moved = lax.ppermute(start_block, every, to_row_group())
    x4 = lax.all_to_all(
        jnp.broadcast_to(moved[None], (slots, vecs, width)), "z", 0, 0, tiled=True
    )
    x4 = jnp.where(far, jnp.roll(x4, 2, axis=0), x4)
    x = start_block
    y4 = total(across(x), down(x4))
    y = lax.ppermute(slot_of(y4), every, from_row_group())
    xy4 = jnp.concatenate([x4, y4], axis=1)
    z4 = total(across(y), down(y4))
    grams = jnp.concatenate([inner(x4, x4), inner(y4, xy4), inner(z4, xy4), inner(z4, z4)], axis=1)
    back = lax.ppermute(
        jnp.concatenate([slot_of(z4), grams], axis=1), every, from_row_group()
    )
    zz, grams = back[:, :width], back[:, width:]
    grams = lax.all_to_all(
        jnp.broadcast_to(grams[None], (8, *grams.shape)), ("x", "co"), 0, 0, tiled=True
    )
    return close(grams, x, y, zz, col_count * width)


def solution(mesh):
    fine = Mesh(mesh.devices.reshape(SIZES), NAMES)
    placed = (P(None, COL), P(COL), P(ROW, COL, None, None))
    return jax.shard_map(
        on_device, mesh=fine, in_specs=placed, out_specs=(P(), P(None, COL)), check_vma=False
    )
```

```python
import functools

import jax
import jax.numpy as jnp
from jax import lax
from jax.experimental import pallas as pl
from jax.experimental.pallas import tpu as pltpu
from jax.sharding import Mesh
from jax.sharding import PartitionSpec as P

SHIFT = 5.5
FULL = lax.Precision.HIGHEST
BLOCKS = lax.Precision.HIGH

SIZES = (2, 4, 4, 4, 2)
NAMES = ("zh", "y", "z", "x", "co")
ROW = ("zh", "y")
COL = ("z", "x", "co")

PLACE = (
    (5, 3, 2, 4, 7, 1, 0, 6),
    (2, 4, 5, 3, 0, 6, 7, 1),
    (0, 1, 7, 6, 2, 3, 5, 4),
    (7, 0, 4, 6, 2, 3, 1, 5),
    (3, 5, 4, 2, 1, 0, 6, 7),
    (4, 2, 3, 5, 1, 0, 6, 7),
    (6, 0, 1, 7, 4, 2, 3, 5),
    (1, 7, 6, 0, 3, 5, 4, 2),
)


def to_row_group():
    pairs = []
    for row in range(8):
        for z in range(4):
            for j in range(8):
                far = (row // 4) != (j // 4)
                z_to = (z + 2) % 4 if far else z
                pairs.append((row * 32 + z * 8 + j, j * 32 + z_to * 8 + PLACE[j][row]))
    return pairs


def from_row_group():
    return [(b, a) for a, b in to_row_group()]


def far_table():
    table = [[0.0] * 8 for _ in range(8)]
    for j in range(8):
        for row in range(8):
            table[j][PLACE[j][row]] = float((row // 4) != (j // 4))
    return table


def mm(a, b):
    return jnp.dot(a, b, precision=FULL, preferred_element_type=jnp.float32)
def mmt(a, b):
    return lax.dot_general(a, b, (((1,), (1,)), ((), ())), precision=FULL, preferred_element_type=jnp.float32)


def factor_and_inverse(g):
    n = g.shape[0]
    down = lax.broadcasted_iota(jnp.int32, (n, 2 * n), 0)
    along = lax.broadcasted_iota(jnp.int32, (n, 2 * n), 1)
    same = (down == along)[:, :n]
    diagonal = jnp.where(same, g, 0.0)
    root = jnp.sqrt(jnp.sum(diagonal, axis=0, keepdims=True))
    root_down = jnp.sqrt(jnp.sum(diagonal, axis=1, keepdims=True))
    wide = jnp.concatenate([g / root, jnp.where(same, 1.0, 0.0)], axis=1) / root_down
    for k in range(0, n - 2, 2):
        r0 = jnp.broadcast_to(wide[k : k + 1, :], (8, 2 * n))
        r1 = jnp.broadcast_to(wide[k + 1 : k + 2, :], (8, 2 * n))
        a = jnp.broadcast_to(r0[:, k : k + 1], r0.shape)
        b = jnp.broadcast_to(r0[:, k + 1 : k + 2], r0.shape)
        c = jnp.broadcast_to(r1[:, k + 1 : k + 2], r0.shape)
        c0 = jnp.broadcast_to(wide[:, k : k + 1], wide.shape)
        c1 = jnp.broadcast_to(wide[:, k + 1 : k + 2], wide.shape)
        det = 1.0 / (a * c - b * b)
        s0 = jnp.concatenate([(r0 * c - r1 * b) * det] * (n // 8), axis=0)
        s1 = jnp.concatenate([(r1 * a - r0 * b) * det] * (n // 8), axis=0)
        wide = jnp.where(down > k + 1, wide - (c0 * s0 + c1 * s1), wide)
    above = jnp.roll(wide, 1, axis=0)
    left = down - 1 == along
    b = jnp.sum(jnp.where(left, wide, 0.0), axis=1, keepdims=True)
    a = jnp.sum(jnp.where(left, above, 0.0), axis=1, keepdims=True)
    wide = jnp.where(lax.rem(down, 2) == 1, wide - (b / a) * above, wide)
    pivot = jnp.sum(jnp.where(down == along, wide, 0.0), axis=1, keepdims=True)
    wide = wide * (1.0 / jnp.sqrt(pivot))
    upper = jnp.where(down <= along, wide, 0.0)[:, :n] * root
    return jnp.transpose(upper), wide[:, n:]


def finish(scale, grams_ref, x_ref, y_ref, z_ref, hist_ref, out_ref, g_ref, p_ref, v_ref):
    n = 32
    part = grams_ref[...] * scale
    at = 0
    for i in range(3):
        for k in range(i + 1):
            block = part[:, at * n : (at + 1) * n]
            g_ref[i * n : (i + 1) * n, k * n : (k + 1) * n] = block
            if k < i:
                g_ref[k * n : (k + 1) * n, i * n : (i + 1) * n] = jnp.transpose(block)
            at += 1
    v_ref[0:n] = x_ref[...]
    v_ref[n : 2 * n] = y_ref[...]
    v_ref[2 * n :] = z_ref[...]
    eye = jnp.where(
        lax.broadcasted_iota(jnp.int32, (n, n), 0) == lax.broadcasted_iota(jnp.int32, (n, n), 1),
        SHIFT,
        0.0,
    )
    low0, t0 = factor_and_inverse(g_ref[0:n, 0:n])
    a0 = mmt(mm(t0, g_ref[n : 2 * n, 0:n]), t0)
    hist_ref[0, 0] = a0 + eye
    m0 = mm(a0, t0)
    p_ref[:, 0:n] = -m0
    p_ref[:, n : 2 * n] = t0
    p1 = p_ref[:, 0 : 2 * n]
    low1, t1 = factor_and_inverse(mmt(mm(p1, g_ref[0 : 2 * n, 0 : 2 * n]), p1))
    hist_ref[0, 1] = low1
    q1 = mm(t1, p1)
    d0 = lax.dot_general(
        low1, t0, (((0,), (0,)), ((), ())), precision=FULL, preferred_element_type=jnp.float32
    )
    p_ref[:, 0:n] = -d0
    p_ref[:, n : 3 * n] = q1
    w1 = p_ref[...]
    a1 = mmt(mm(w1, g_ref[:, 0 : 2 * n]), q1)
    hist_ref[1, 0] = a1 + eye
    p_ref[:, 0 : 2 * n] = mm(a1, q1)
    w1 = jnp.concatenate([w1[:, 0 : 2 * n] - p_ref[:, 0 : 2 * n], w1[:, 2 * n :]], axis=1)
    low2, t2 = factor_and_inverse(mmt(mm(w1, g_ref[...]), w1))
    hist_ref[1, 1] = low2
    out_ref[...] = mm(t2, mm(w1, v_ref[...]))


def close(grams, x, y, z, length):
    vecs = x.shape[0]
    return pl.pallas_call(
        functools.partial(finish, 1.0 / length),
        out_shape=(
            jax.ShapeDtypeStruct((2, 2, vecs, vecs), jnp.float32),
            jax.ShapeDtypeStruct(x.shape, jnp.float32),
        ),
        scratch_shapes=[
            pltpu.VMEM((3 * vecs, 3 * vecs), jnp.float32),
            pltpu.VMEM((vecs, 3 * vecs), jnp.float32),
            pltpu.VMEM((3 * vecs, x.shape[1]), jnp.float32),
        ],
        name="recurrence",
    )(grams, x, y, z)


def on_device(start_block, energies, hamiltonian):
    vecs, width = start_block.shape
    col_count = lax.axis_size(COL)
    half = width // 2
    row = lax.axis_index(ROW)
    col = lax.axis_index(COL)
    z = lax.axis_index("z")
    core = lax.axis_index("co")
    place = lax.axis_index(("x", "co"))
    blocks = hamiltonian[:, 0]
    slots = blocks.shape[0]
    block_rows = row + 8 * jnp.arange(slots, dtype=jnp.int32)
    weight = jnp.where(block_rows < col, 1.0, jnp.where(block_rows == col, 0.5, 0.0)).astype(
        jnp.float32
    )[:, None, None]
    lead = jnp.where(place == row, energies - SHIFT, 0.0)
    own_slot = (jnp.arange(slots) == z)[:, None, None]
    table = jnp.array(far_table(), jnp.float32).reshape(-1)
    far = jnp.sum(table * (jnp.arange(64) == row * 8 + place).astype(jnp.float32)) > 0.5
    slot = jnp.where(far, (z + 2) % 4, z)
    in_slot = (jnp.arange(slots) == slot)[:, None, None]
    every = NAMES

    def down(four):
        left = jnp.concatenate([four[s] * weight[s] for s in range(slots)], axis=1)
        return jnp.dot(left, blocks.reshape(slots * width, width), precision=BLOCKS)

    def across(own):
        product = jnp.einsum("pl,skl->spk", own, blocks, precision=BLOCKS) * weight
        return product + jnp.where(own_slot, (lead[None, :] * own)[None], 0.0)

    def total(acrosses, downs):
        arrived = lax.ppermute(downs, every, to_row_group())
        acrosses = lax.optimization_barrier(acrosses)
        part = acrosses + jnp.where(in_slot, arrived[None], 0.0)
        part = part.reshape(slots * vecs // 8, 8, width)
        low, high = part[..., :half], part[..., half:]
        mine = jnp.where(core == 0, low, high)
        other = jnp.where(core == 0, high, low)
        mine = mine + lax.ppermute(other, "co", [(0, 1), (1, 0)])
        piece = lax.all_to_all(mine, ("z", "x"), 0, 0, tiled=True).sum(axis=0)
        whole = lax.all_to_all(
            jnp.broadcast_to(piece[None], mine.shape), ("z", "x"), 0, 0, tiled=True
        )
        facing = lax.ppermute(whole, "co", [(0, 1), (1, 0)])
        low = jnp.where(core == 0, whole, facing)
        high = jnp.where(core == 0, facing, whole)
        return jnp.concatenate([low, high], axis=-1).reshape(slots, vecs, width)

    def slot_of(four):
        return jnp.sum(jnp.where(in_slot, four, 0.0), axis=0)

    def inner(left, right):
        return jnp.einsum("spk,sqk->pq", left, right, precision=FULL)

    moved = lax.ppermute(start_block, every, to_row_group())
    near = lax.ppermute(moved, "z", [(0, 1), (1, 0), (2, 3), (3, 2)])
    odd = lax.rem(z, 2) == 1
    two = jnp.stack([jnp.where(odd, near, moved), jnp.where(odd, moved, near)])
    over = lax.ppermute(two, "z", [(0, 2), (2, 0), (1, 3), (3, 1)])
    upper = (z >= 2) != far
    x4 = jnp.concatenate([jnp.where(upper, over, two), jnp.where(upper, two, over)])
    x = start_block
    y4 = total(across(x), down(x4))
    y = lax.ppermute(slot_of(y4), every, from_row_group())
    downs = down(y4)
    acrosses, gx, gy = lax.optimization_barrier(
        (across(y), inner(x4, x4), inner(y4, jnp.concatenate([x4, y4], axis=1)))
    )
    z4 = total(acrosses, downs)
    gz = inner(z4, jnp.concatenate([x4, y4, z4], axis=1))
    back = lax.ppermute(
        jnp.concatenate([slot_of(z4), gx, gy, gz], axis=1), every, from_row_group()
    )
    zz, grams = back[:, :width], back[:, width:]
    grams = grams + lax.ppermute(grams, "co", [(0, 1), (1, 0)])
    grams = grams + lax.ppermute(grams, "x", [(0, 1), (1, 0), (2, 3), (3, 2)])
    grams = grams + lax.ppermute(grams, "x", [(0, 3), (3, 0), (1, 2), (2, 1)])
    return close(grams, x, y, zz, col_count * width)


def solution(mesh):
    fine = Mesh(mesh.devices.reshape(SIZES), NAMES)
    placed = (P(None, COL), P(COL), P(ROW, COL, None, None))
    return jax.shard_map(
        on_device, mesh=fine, in_specs=placed, out_specs=(P(), P(None, COL)), check_vma=False
    )
```

```python
import functools

import jax
import jax.numpy as jnp
from jax import lax
from jax.experimental import pallas as pl
from jax.experimental.pallas import tpu as pltpu
from jax.sharding import Mesh
from jax.sharding import PartitionSpec as P

SHIFT = 5.5
FULL = lax.Precision.HIGHEST
BLOCKS = lax.Precision.HIGH

SIZES = (2, 4, 4, 4, 2)
NAMES = ("zh", "y", "z", "x", "co")
ROW = ("zh", "y")
COL = ("z", "x", "co")

PLACE = (
    (5, 3, 2, 4, 7, 1, 0, 6),
    (2, 4, 5, 3, 0, 6, 7, 1),
    (0, 1, 7, 6, 2, 3, 5, 4),
    (7, 0, 4, 6, 2, 3, 1, 5),
    (3, 5, 4, 2, 1, 0, 6, 7),
    (4, 2, 3, 5, 1, 0, 6, 7),
    (6, 0, 1, 7, 4, 2, 3, 5),
    (1, 7, 6, 0, 3, 5, 4, 2),
)


def to_row_group():
    pairs = []
    for row in range(8):
        for z in range(4):
            for j in range(8):
                far = (row // 4) != (j // 4)
                z_to = (z + 2) % 4 if far else z
                pairs.append((row * 32 + z * 8 + j, j * 32 + z_to * 8 + PLACE[j][row]))
    return pairs


def from_row_group():
    return [(b, a) for a, b in to_row_group()]


def far_table():
    table = [[0.0] * 8 for _ in range(8)]
    for j in range(8):
        for row in range(8):
            table[j][PLACE[j][row]] = float((row // 4) != (j // 4))
    return table


def mm(a, b):
    return jnp.dot(a, b, precision=FULL, preferred_element_type=jnp.float32)
def mmt(a, b):
    return lax.dot_general(a, b, (((1,), (1,)), ((), ())), precision=FULL, preferred_element_type=jnp.float32)


def factor_and_inverse(g):
    n = g.shape[0]
    down = lax.broadcasted_iota(jnp.int32, (n, 2 * n), 0)
    along = lax.broadcasted_iota(jnp.int32, (n, 2 * n), 1)
    same = (down == along)[:, :n]
    diagonal = jnp.where(same, g, 0.0)
    root = jnp.sqrt(jnp.sum(diagonal, axis=0, keepdims=True))
    root_down = jnp.sqrt(jnp.sum(diagonal, axis=1, keepdims=True))
    wide = jnp.concatenate([g / root, jnp.where(same, 1.0, 0.0)], axis=1) / root_down
    for k in range(0, n - 2, 2):
        r0 = jnp.broadcast_to(wide[k : k + 1, :], (8, 2 * n))
        r1 = jnp.broadcast_to(wide[k + 1 : k + 2, :], (8, 2 * n))
        a = jnp.broadcast_to(r0[:, k : k + 1], r0.shape)
        b = jnp.broadcast_to(r0[:, k + 1 : k + 2], r0.shape)
        c = jnp.broadcast_to(r1[:, k + 1 : k + 2], r0.shape)
        c0 = jnp.broadcast_to(wide[:, k : k + 1], wide.shape)
        c1 = jnp.broadcast_to(wide[:, k + 1 : k + 2], wide.shape)
        det = 1.0 / (a * c - b * b)
        s0 = jnp.concatenate([(r0 * c - r1 * b) * det] * (n // 8), axis=0)
        s1 = jnp.concatenate([(r1 * a - r0 * b) * det] * (n // 8), axis=0)
        wide = jnp.where(down > k + 1, wide - (c0 * s0 + c1 * s1), wide)
    above = jnp.roll(wide, 1, axis=0)
    left = down - 1 == along
    b = jnp.sum(jnp.where(left, wide, 0.0), axis=1, keepdims=True)
    a = jnp.sum(jnp.where(left, above, 0.0), axis=1, keepdims=True)
    wide = jnp.where(lax.rem(down, 2) == 1, wide - (b / a) * above, wide)
    pivot = jnp.sum(jnp.where(down == along, wide, 0.0), axis=1, keepdims=True)
    wide = wide * (1.0 / jnp.sqrt(pivot))
    upper = jnp.where(down <= along, wide, 0.0)[:, :n] * root
    return jnp.transpose(upper), wide[:, n:]


def finish(scale, grams_ref, x_ref, y_ref, z_ref, hist_ref, out_ref, g_ref, p_ref, v_ref):
    n = 32
    part = grams_ref[...] * scale
    at = 0
    for i in range(3):
        for k in range(i + 1):
            block = part[:, at * n : (at + 1) * n]
            g_ref[i * n : (i + 1) * n, k * n : (k + 1) * n] = block
            if k < i:
                g_ref[k * n : (k + 1) * n, i * n : (i + 1) * n] = jnp.transpose(block)
            at += 1
    v_ref[0:n] = x_ref[...]
    v_ref[n : 2 * n] = y_ref[...]
    v_ref[2 * n :] = z_ref[...]
    eye = jnp.where(
        lax.broadcasted_iota(jnp.int32, (n, n), 0) == lax.broadcasted_iota(jnp.int32, (n, n), 1),
        SHIFT,
        0.0,
    )
    low0, t0 = factor_and_inverse(g_ref[0:n, 0:n])
    a0 = mmt(mm(t0, g_ref[n : 2 * n, 0:n]), t0)
    hist_ref[0, 0] = a0 + eye
    m0 = mm(a0, t0)
    p_ref[:, 0:n] = -m0
    p_ref[:, n : 2 * n] = t0
    p1 = p_ref[:, 0 : 2 * n]
    low1, t1 = factor_and_inverse(mmt(mm(p1, g_ref[0 : 2 * n, 0 : 2 * n]), p1))
    hist_ref[0, 1] = low1
    q1 = mm(t1, p1)
    d0 = lax.dot_general(
        low1, t0, (((0,), (0,)), ((), ())), precision=FULL, preferred_element_type=jnp.float32
    )
    p_ref[:, 0:n] = -d0
    p_ref[:, n : 3 * n] = q1
    w1 = p_ref[...]
    a1 = mmt(mm(w1, g_ref[:, 0 : 2 * n]), q1)
    hist_ref[1, 0] = a1 + eye
    p_ref[:, 0 : 2 * n] = mm(a1, q1)
    w1 = jnp.concatenate([w1[:, 0 : 2 * n] - p_ref[:, 0 : 2 * n], w1[:, 2 * n :]], axis=1)
    low2, t2 = factor_and_inverse(mmt(mm(w1, g_ref[...]), w1))
    hist_ref[1, 1] = low2
    out_ref[...] = mm(t2, mm(w1, v_ref[...]))


def parts_of(v):
    high = v.astype(jnp.bfloat16)
    return high, (v - high.astype(jnp.float32)).astype(jnp.bfloat16)


def split_blocks(weight_ref, blocks_ref, high_ref, low_ref, held, arrived):
    slots, width = blocks_ref.shape[0], blocks_ref.shape[1]
    copies = [
        pltpu.make_async_copy(blocks_ref.at[s], held.at[s], arrived.at[s]) for s in range(slots)
    ]
    for copy in copies:
        copy.start()
    for s in range(slots):
        copies[s].wait()
        rows = pl.ds(s * width, width)
        high_ref[rows, :], low_ref[rows, :] = parts_of(held[s] * weight_ref[s])


def dot3(left, high, low, contract):
    rows = left[0].shape[0]
    dims = (((1,), (contract,)), ((), ()))
    both = lax.dot_general(
        jnp.concatenate(left, axis=0), high, dims, preferred_element_type=jnp.float32
    )
    rest = lax.dot_general(left[0], low, dims, preferred_element_type=jnp.float32)
    return both[:rows] + (both[rows:] + rest)


def down_kernel(four_ref, high_ref, low_ref, out_ref):
    slots, _, width = four_ref.shape
    total = None
    for s in range(slots):
        rows = pl.ds(s * width, width)
        term = dot3(parts_of(four_ref[s]), high_ref[rows, :], low_ref[rows, :], 0)
        total = term if total is None else total + term
    out_ref[...] = total


def across_kernel(lead_ref, own_ref, high_ref, low_ref, out_ref):
    slots, _, width = out_ref.shape
    left = parts_of(own_ref[...])
    for s in range(slots):
        rows = pl.ds(s * width, width)
        term = dot3(left, high_ref[rows, :], low_ref[rows, :], 1)
        out_ref[s] = term + lead_ref[pl.ds(s, 1), :] * own_ref[...]


def gram_kernel(*refs):
    *four_refs, out_ref, flat_ref = refs
    slots, vecs, width = four_refs[0].shape
    for i, four_ref in enumerate(four_refs):
        for s in range(slots):
            flat_ref[i * vecs : (i + 1) * vecs, s * width : (s + 1) * width] = four_ref[s]
    out_ref[...] = mmt(flat_ref[(len(four_refs) - 1) * vecs :, :], flat_ref[...])


LIMIT = pltpu.CompilerParams(vmem_limit_bytes=16 * 2**20)
IN_VMEM = pl.BlockSpec(memory_space=pltpu.VMEM)


def grams_of(*fours):
    slots, vecs, width = fours[0].shape
    return pl.pallas_call(
        gram_kernel,
        in_specs=[IN_VMEM] * len(fours),
        out_specs=IN_VMEM,
        out_shape=pltpu.VMEM((vecs, len(fours) * vecs), jnp.float32),
        scratch_shapes=[pltpu.VMEM((len(fours) * vecs, slots * width), jnp.float32)],
        compiler_params=LIMIT,
        name="gram",
    )(*fours)


def spread_kernel(parts_ref, out_ref):
    out_ref[...] = jnp.broadcast_to(jnp.sum(parts_ref[...], axis=0)[None], out_ref.shape)


def sum_spread(parts):
    return pl.pallas_call(
        spread_kernel,
        in_specs=[IN_VMEM],
        out_specs=IN_VMEM,
        out_shape=pltpu.VMEM(parts.shape, jnp.float32),
        compiler_params=LIMIT,
        name="sum_spread",
    )(parts)


def close(grams, x, y, z, length):
    vecs = x.shape[0]
    return pl.pallas_call(
        functools.partial(finish, 1.0 / length),
        out_shape=(
            jax.ShapeDtypeStruct((2, 2, vecs, vecs), jnp.float32),
            jax.ShapeDtypeStruct(x.shape, jnp.float32),
        ),
        scratch_shapes=[
            pltpu.VMEM((3 * vecs, 3 * vecs), jnp.float32),
            pltpu.VMEM((vecs, 3 * vecs), jnp.float32),
            pltpu.VMEM((3 * vecs, x.shape[1]), jnp.float32),
        ],
        compiler_params=LIMIT,
        name="recurrence",
    )(grams, x, y, z)


def on_device(start_block, energies, hamiltonian):
    vecs, width = start_block.shape
    col_count = lax.axis_size(COL)
    half = width // 2
    row = lax.axis_index(ROW)
    col = lax.axis_index(COL)
    z = lax.axis_index("z")
    core = lax.axis_index("co")
    place = lax.axis_index(("x", "co"))
    blocks = hamiltonian[:, 0]
    slots = blocks.shape[0]
    block_rows = row + 8 * jnp.arange(slots, dtype=jnp.int32)
    weight = jnp.where(block_rows < col, 1.0, jnp.where(block_rows == col, 0.5, 0.0)).astype(
        jnp.float32
    )
    own_slot = (jnp.arange(slots) == z) & (place == row)
    lead = jnp.where(own_slot[:, None], (energies - SHIFT)[None, :], 0.0)
    table = jnp.array(far_table(), jnp.float32).reshape(-1)
    far = jnp.sum(table * (jnp.arange(64) == row * 8 + place).astype(jnp.float32)) > 0.5
    slot = jnp.where(far, (z + 2) % 4, z)
    in_slot = (jnp.arange(slots) == slot)[:, None, None]
    every = NAMES

    high, low = pl.pallas_call(
        split_blocks,
        in_specs=[pl.BlockSpec(memory_space=pltpu.SMEM), pl.BlockSpec(memory_space=pl.ANY)],
        out_specs=(IN_VMEM, IN_VMEM),
        out_shape=(pltpu.VMEM((slots * width, width), jnp.bfloat16),) * 2,
        scratch_shapes=[
            pltpu.VMEM(blocks.shape, jnp.float32),
            pltpu.SemaphoreType.DMA((slots,)),
        ],
        compiler_params=LIMIT,
        name="split_blocks",
    )(weight, blocks)

    def down(four):
        return pl.pallas_call(
            down_kernel,
            in_specs=[IN_VMEM] * 3,
            out_specs=IN_VMEM,
            out_shape=pltpu.VMEM((vecs, width), jnp.float32),
            compiler_params=LIMIT,
            name="down",
        )(four, high, low)

    def across(own):
        return pl.pallas_call(
            across_kernel,
            in_specs=[IN_VMEM] * 4,
            out_specs=IN_VMEM,
            out_shape=pltpu.VMEM((slots, vecs, width), jnp.float32),
            compiler_params=LIMIT,
            name="across",
        )(lead, own, high, low)

    def total(acrosses, downs):
        arrived = lax.ppermute(downs, every, to_row_group())
        acrosses = lax.optimization_barrier(acrosses)
        part = acrosses + jnp.where(in_slot, arrived[None], 0.0)
        part = part.reshape(slots * vecs // 8, 8, width)
        low, high = part[..., :half], part[..., half:]
        mine = jnp.where(core == 0, low, high)
        other = jnp.where(core == 0, high, low)
        mine = mine + lax.ppermute(other, "co", [(0, 1), (1, 0)])
        pieces = lax.all_to_all(mine, ("z", "x"), 0, 0, tiled=True)
        whole = lax.all_to_all(sum_spread(pieces), ("z", "x"), 0, 0, tiled=True)
        facing = lax.ppermute(whole, "co", [(0, 1), (1, 0)])
        low = jnp.where(core == 0, whole, facing)
        high = jnp.where(core == 0, facing, whole)
        return jnp.concatenate([low, high], axis=-1).reshape(slots, vecs, width)

    def slot_of(four):
        return jnp.sum(jnp.where(in_slot, four, 0.0), axis=0)

    moved = lax.ppermute(start_block, every, to_row_group())
    near = lax.ppermute(moved, "z", [(0, 1), (1, 0), (2, 3), (3, 2)])
    odd = lax.rem(z, 2) == 1
    two = jnp.stack([jnp.where(odd, near, moved), jnp.where(odd, moved, near)])
    over = lax.ppermute(two, "z", [(0, 2), (2, 0), (1, 3), (3, 1)])
    upper = (z >= 2) != far
    x4 = jnp.concatenate([jnp.where(upper, over, two), jnp.where(upper, two, over)])
    x = start_block
    y4 = total(across(x), down(x4))
    y = lax.ppermute(slot_of(y4), every, from_row_group())
    downs = down(y4)
    acrosses, gx, gy = lax.optimization_barrier(
        (across(y), grams_of(x4), grams_of(x4, y4))
    )
    z4 = total(acrosses, downs)
    gz = grams_of(x4, y4, z4)
    back = lax.ppermute(
        jnp.concatenate([slot_of(z4), gx, gy, gz], axis=1), every, from_row_group()
    )
    zz, grams = back[:, :width], back[:, width:]
    grams = grams + lax.ppermute(grams, "co", [(0, 1), (1, 0)])
    grams = grams + lax.ppermute(grams, "x", [(0, 1), (1, 0), (2, 3), (3, 2)])
    grams = grams + lax.ppermute(grams, "x", [(0, 3), (3, 0), (1, 2), (2, 1)])
    return close(grams, x, y, zz, col_count * width)


def solution(mesh):
    fine = Mesh(mesh.devices.reshape(SIZES), NAMES)
    placed = (P(None, COL), P(COL), P(ROW, COL, None, None))
    return jax.shard_map(
        on_device, mesh=fine, in_specs=placed, out_specs=(P(), P(None, COL)), check_vma=False
    )
```

```python
import functools

import jax
import jax.numpy as jnp
from jax import lax
from jax.experimental import pallas as pl
from jax.experimental.pallas import tpu as pltpu
from jax.sharding import Mesh
from jax.sharding import PartitionSpec as P

SHIFT = 5.5
FULL = lax.Precision.HIGHEST
BLOCKS = lax.Precision.HIGH

SIZES = (2, 4, 4, 4, 2)
NAMES = ("zh", "y", "z", "x", "co")
ROW = ("zh", "y")
COL = ("z", "x", "co")

PLACE = (
    (5, 3, 2, 4, 7, 1, 0, 6),
    (2, 4, 5, 3, 0, 6, 7, 1),
    (0, 1, 7, 6, 2, 3, 5, 4),
    (7, 0, 4, 6, 2, 3, 1, 5),
    (3, 5, 4, 2, 1, 0, 6, 7),
    (4, 2, 3, 5, 1, 0, 6, 7),
    (6, 0, 1, 7, 4, 2, 3, 5),
    (1, 7, 6, 0, 3, 5, 4, 2),
)


def to_row_group():
    pairs = []
    for row in range(8):
        for z in range(4):
            for j in range(8):
                far = (row // 4) != (j // 4)
                z_to = (z + 2) % 4 if far else z
                pairs.append((row * 32 + z * 8 + j, j * 32 + z_to * 8 + PLACE[j][row]))
    return pairs


def from_row_group():
    return [(b, a) for a, b in to_row_group()]


def far_bits(row):
    return sum(((r // 4) != (row // 4)) << PLACE[row][r] for r in range(8))


def mm(a, b):
    return jnp.dot(a, b, precision=FULL, preferred_element_type=jnp.float32)
def mmt(a, b):
    return lax.dot_general(a, b, (((1,), (1,)), ((), ())), precision=FULL, preferred_element_type=jnp.float32)


def factor_and_inverse(g):
    n = g.shape[0]
    down = lax.broadcasted_iota(jnp.int32, (n, 2 * n), 0)
    along = lax.broadcasted_iota(jnp.int32, (n, 2 * n), 1)
    same = (down == along)[:, :n]
    diagonal = jnp.where(same, g, 0.0)
    root = jnp.sqrt(jnp.sum(diagonal, axis=0, keepdims=True))
    root_down = jnp.sqrt(jnp.sum(diagonal, axis=1, keepdims=True))
    wide = jnp.concatenate([g / root, jnp.where(same, 1.0, 0.0)], axis=1) / root_down
    for k in range(0, n - 2, 2):
        r0 = jnp.broadcast_to(wide[k : k + 1, :], (8, 2 * n))
        r1 = jnp.broadcast_to(wide[k + 1 : k + 2, :], (8, 2 * n))
        a = jnp.broadcast_to(r0[:, k : k + 1], r0.shape)
        b = jnp.broadcast_to(r0[:, k + 1 : k + 2], r0.shape)
        c = jnp.broadcast_to(r1[:, k + 1 : k + 2], r0.shape)
        c0 = jnp.broadcast_to(wide[:, k : k + 1], wide.shape)
        c1 = jnp.broadcast_to(wide[:, k + 1 : k + 2], wide.shape)
        det = 1.0 / (a * c - b * b)
        s0 = jnp.concatenate([(r0 * c - r1 * b) * det] * (n // 8), axis=0)
        s1 = jnp.concatenate([(r1 * a - r0 * b) * det] * (n // 8), axis=0)
        wide = jnp.where(down > k + 1, wide - (c0 * s0 + c1 * s1), wide)
    above = jnp.roll(wide, 1, axis=0)
    left = down - 1 == along
    b = jnp.sum(jnp.where(left, wide, 0.0), axis=1, keepdims=True)
    a = jnp.sum(jnp.where(left, above, 0.0), axis=1, keepdims=True)
    wide = jnp.where(lax.rem(down, 2) == 1, wide - (b / a) * above, wide)
    pivot = jnp.sum(jnp.where(down == along, wide, 0.0), axis=1, keepdims=True)
    wide = wide * (1.0 / jnp.sqrt(pivot))
    upper = jnp.where(down <= along, wide, 0.0)[:, :n] * root
    return jnp.transpose(upper), wide[:, n:]


def first_step(scale, gram_ref, history_ref, first_ref, second_ref):
    n = gram_ref.shape[0]
    g00 = gram_ref[:, 0:n] * scale
    g10 = gram_ref[:, n : 2 * n] * scale
    low0, t0 = factor_and_inverse(g00)
    a0 = mmt(mm(t0, g10), t0)
    history_ref[0] = a0
    second_ref[:, 0:n] = -mm(a0, t0)
    second_ref[:, n : 2 * n] = t0
    p1 = second_ref[...]
    whole = jnp.concatenate(
        [
            jnp.concatenate([g00, jnp.transpose(g10)], axis=1),
            gram_ref[:, n : 3 * n] * scale,
        ],
        axis=0,
    )
    low1, t1 = factor_and_inverse(mmt(mm(p1, whole), p1))
    history_ref[1] = low1
    q1 = mm(t1, p1)
    second_ref[...] = q1
    first_ref[:, 0:n] = -lax.dot_general(
        low1, t0, (((0,), (0,)), ((), ())), precision=FULL, preferred_element_type=jnp.float32
    )
    first_ref[:, n : 3 * n] = q1


def last_step(
    scale, gram_ref, gram2_ref, history0_ref, image_ref, second_ref, x_ref, y_ref, z_ref,
    history_ref, out_ref, g_ref, p_ref, v_ref,
):
    n = gram_ref.shape[0]
    eye = jnp.where(
        lax.broadcasted_iota(jnp.int32, (n, n), 0) == lax.broadcasted_iota(jnp.int32, (n, n), 1),
        SHIFT,
        0.0,
    )
    g_ref[0:n, 0:n] = gram_ref[:, 0:n] * scale
    g_ref[n : 2 * n, 0 : 2 * n] = gram_ref[:, n : 3 * n] * scale
    g_ref[0:n, n : 2 * n] = jnp.transpose(gram_ref[:, n : 2 * n]) * scale
    g_ref[2 * n :, :] = gram2_ref[...] * scale
    g_ref[0:n, 2 * n :] = jnp.transpose(gram2_ref[:, 0:n]) * scale
    g_ref[n : 2 * n, 2 * n :] = jnp.transpose(gram2_ref[:, n : 2 * n]) * scale
    history_ref[0, 0] = history0_ref[0] + eye
    history_ref[0, 1] = history0_ref[1]
    w1 = image_ref[...]
    q1 = second_ref[...]
    a1 = mmt(mm(w1, g_ref[:, 0 : 2 * n]), q1)
    history_ref[1, 0] = a1 + eye
    p_ref[...] = mm(a1, q1)
    w1 = jnp.concatenate([w1[:, 0 : 2 * n] - p_ref[...], w1[:, 2 * n :]], axis=1)
    low2, t2 = factor_and_inverse(mmt(mm(w1, g_ref[...]), w1))
    history_ref[1, 1] = low2
    v_ref[0:n] = x_ref[...]
    v_ref[n : 2 * n] = y_ref[...]
    v_ref[2 * n :] = z_ref[...]
    out_ref[...] = mm(t2, mm(w1, v_ref[...]))


def parts_of(v):
    high = v.astype(jnp.bfloat16)
    return high, (v - high.astype(jnp.float32)).astype(jnp.bfloat16)


def split_blocks(weight_ref, blocks_ref, high_ref, low_ref, held, arrived):
    slots, width = blocks_ref.shape[0], blocks_ref.shape[1]
    copies = [
        pltpu.make_async_copy(blocks_ref.at[s], held.at[s], arrived.at[s]) for s in range(slots)
    ]
    for copy in copies:
        copy.start()
    for s in range(slots):
        copies[s].wait()
        rows = pl.ds(s * width, width)
        high_ref[rows, :], low_ref[rows, :] = parts_of(held[s] * weight_ref[s])


def dot3(left, high, low, contract):
    rows = left[0].shape[0]
    dims = (((1,), (contract,)), ((), ()))
    both = lax.dot_general(
        jnp.concatenate(left, axis=0), high, dims, preferred_element_type=jnp.float32
    )
    rest = lax.dot_general(left[0], low, dims, preferred_element_type=jnp.float32)
    return both[:rows] + (both[rows:] + rest)


def down_kernel(four_ref, high_ref, low_ref, out_ref):
    slots, _, width = four_ref.shape
    total = None
    for s in range(slots):
        rows = pl.ds(s * width, width)
        term = dot3(parts_of(four_ref[s]), high_ref[rows, :], low_ref[rows, :], 0)
        total = term if total is None else total + term
    out_ref[...] = total


def across_kernel(leads_ref, energies_ref, own_ref, high_ref, low_ref, out_ref):
    slots, _, width = out_ref.shape
    left = parts_of(own_ref[...])
    lead = (energies_ref[...] - SHIFT) * own_ref[...]
    for s in range(slots):
        rows = pl.ds(s * width, width)
        term = dot3(left, high_ref[rows, :], low_ref[rows, :], 1)
        out_ref[s] = term + leads_ref[s] * lead


def gram_kernel(*refs):
    *four_refs, out_ref, flat_ref = refs
    slots, vecs, width = four_refs[0].shape
    for i, four_ref in enumerate(four_refs):
        for s in range(slots):
            flat_ref[i * vecs : (i + 1) * vecs, s * width : (s + 1) * width] = four_ref[s]
    out_ref[...] = mmt(flat_ref[(len(four_refs) - 1) * vecs :, :], flat_ref[...])


LIMIT = pltpu.CompilerParams(vmem_limit_bytes=16 * 2**20)
IN_VMEM = pl.BlockSpec(memory_space=pltpu.VMEM)


def grams_of(*fours):
    slots, vecs, width = fours[0].shape
    return pl.pallas_call(
        gram_kernel,
        in_specs=[IN_VMEM] * len(fours),
        out_specs=IN_VMEM,
        out_shape=pltpu.VMEM((vecs, len(fours) * vecs), jnp.float32),
        scratch_shapes=[pltpu.VMEM((len(fours) * vecs, slots * width), jnp.float32)],
        compiler_params=LIMIT,
        name="gram",
    )(*fours)


def spread_kernel(parts_ref, out_ref):
    out_ref[...] = jnp.broadcast_to(jnp.sum(parts_ref[...], axis=0)[None], out_ref.shape)


def sum_spread(parts):
    return pl.pallas_call(
        spread_kernel,
        in_specs=[IN_VMEM],
        out_specs=IN_VMEM,
        out_shape=pltpu.VMEM(parts.shape, jnp.float32),
        compiler_params=LIMIT,
        name="sum_spread",
    )(parts)


def begin(gram, length):
    vecs = gram.shape[0]
    return pl.pallas_call(
        functools.partial(first_step, 1.0 / length),
        in_specs=[IN_VMEM],
        out_specs=(IN_VMEM,) * 3,
        out_shape=(
            pltpu.VMEM((2, vecs, vecs), jnp.float32),
            pltpu.VMEM((vecs, 3 * vecs), jnp.float32),
            pltpu.VMEM((vecs, 2 * vecs), jnp.float32),
        ),
        compiler_params=LIMIT,
        cost_estimate=pl.CostEstimate(flops=6 * 10**9, bytes_accessed=10**5, transcendentals=0),
        name="first_step",
    )(gram)


def close(gram, gram2, history0, image, second, x, y, z, length):
    vecs = x.shape[0]
    return pl.pallas_call(
        functools.partial(last_step, 1.0 / length),
        out_shape=(
            jax.ShapeDtypeStruct((2, 2, vecs, vecs), jnp.float32),
            jax.ShapeDtypeStruct(x.shape, jnp.float32),
        ),
        scratch_shapes=[
            pltpu.VMEM((3 * vecs, 3 * vecs), jnp.float32),
            pltpu.VMEM((vecs, 2 * vecs), jnp.float32),
            pltpu.VMEM((3 * vecs, x.shape[1]), jnp.float32),
        ],
        compiler_params=LIMIT,
        name="last_step",
    )(gram, gram2, history0, image, second, x, y, z)


EXCHANGES = (
    ("y", [(0, 1), (1, 0), (2, 3), (3, 2)]),
    ("y", [(0, 3), (3, 0), (1, 2), (2, 1)]),
    (("zh", "z"), [(h * 4 + z, (1 - h) * 4 + (z + 2) % 4) for h in range(2) for z in range(4)]),
)


def exchanged(value, step):
    axis, pairs = EXCHANGES[step]
    return value + lax.ppermute(value, axis, pairs)


def on_device(start_block, energies, hamiltonian):
    vecs, width = start_block.shape
    col_count = lax.axis_size(COL)
    half = width // 2
    row = lax.axis_index(ROW)
    col = lax.axis_index(COL)
    z = lax.axis_index("z")
    core = lax.axis_index("co")
    place = lax.axis_index(("x", "co"))
    blocks = hamiltonian[:, 0]
    slots = blocks.shape[0]
    block_rows = row + 8 * jnp.arange(slots, dtype=jnp.int32)
    weight = jnp.where(block_rows < col, 1.0, jnp.where(block_rows == col, 0.5, 0.0)).astype(
        jnp.float32
    )
    leads = ((jnp.arange(slots) == z) & (place == row)).astype(jnp.float32)
    bits = jnp.int32(0)
    for r in range(8):
        bits = jnp.where(row == r, jnp.int32(far_bits(r)), bits)
    far = lax.shift_right_logical(bits, place) % 2 == 1
    slot = jnp.where(far, (z + 2) % 4, z)
    odd = lax.rem(z, 2) == 1
    upper = (z >= 2) != far
    weight, leads, slot, odd, upper, first = lax.optimization_barrier(
        (weight, leads, slot, odd, upper, core == 0)
    )
    in_slot = (jnp.arange(slots) == slot)[:, None, None]
    every = NAMES

    high, low = pl.pallas_call(
        split_blocks,
        in_specs=[pl.BlockSpec(memory_space=pltpu.SMEM), pl.BlockSpec(memory_space=pltpu.HBM)],
        out_specs=(IN_VMEM, IN_VMEM),
        out_shape=(pltpu.VMEM((slots * width, width), jnp.bfloat16),) * 2,
        scratch_shapes=[
            pltpu.VMEM(blocks.shape, jnp.float32),
            pltpu.SemaphoreType.DMA((slots,)),
        ],
        compiler_params=pltpu.CompilerParams(vmem_limit_bytes=58 * 2**20),
        name="split_blocks",
    )(weight, blocks)

    def down(four):
        return pl.pallas_call(
            down_kernel,
            in_specs=[IN_VMEM] * 3,
            out_specs=IN_VMEM,
            out_shape=pltpu.VMEM((vecs, width), jnp.float32),
            compiler_params=LIMIT,
            name="down",
        )(four, high, low)

    def across(own):
        return pl.pallas_call(
            across_kernel,
            in_specs=[pl.BlockSpec(memory_space=pltpu.SMEM)] + [IN_VMEM] * 4,
            out_specs=IN_VMEM,
            out_shape=pltpu.VMEM((slots, vecs, width), jnp.float32),
            compiler_params=LIMIT,
            name="across",
        )(leads, energies.reshape(1, width), own, high, low)

    def total(acrosses, downs, gram=None):
        arrived = lax.ppermute(downs, every, to_row_group())
        acrosses = lax.optimization_barrier(acrosses)
        part = acrosses + jnp.where(in_slot, arrived[None], 0.0)
        part = part.reshape(slots * vecs // 8, 8, width)
        low, high = part[..., :half], part[..., half:]
        mine = jnp.where(first, low, high)
        other = jnp.where(first, high, low)
        mine = mine + lax.ppermute(other, "co", [(0, 1), (1, 0)])
        if gram is not None:
            mine, gram = lax.optimization_barrier((mine, exchanged(gram, 0)))
        pieces = lax.all_to_all(mine, ("z", "x"), 0, 0, tiled=True)
        whole = lax.all_to_all(sum_spread(pieces), ("z", "x"), 0, 0, tiled=True)
        if gram is not None:
            whole, gram = lax.optimization_barrier((whole, gram))
            gram = exchanged(gram, 1)
        facing = lax.ppermute(whole, "co", [(0, 1), (1, 0)])
        low = jnp.where(first, whole, facing)
        high = jnp.where(first, facing, whole)
        four = jnp.concatenate([low, high], axis=-1).reshape(slots, vecs, width)
        return four, gram

    def slot_of(four):
        return jnp.sum(jnp.where(in_slot, four, 0.0), axis=0)

    moved = lax.ppermute(start_block, every, to_row_group())
    moved, high, low = lax.optimization_barrier((moved, high, low))
    near = lax.ppermute(moved, "z", [(0, 1), (1, 0), (2, 3), (3, 2)])
    two = jnp.stack([jnp.where(odd, near, moved), jnp.where(odd, moved, near)])
    over = lax.ppermute(two, "z", [(0, 2), (2, 0), (1, 3), (3, 1)])
    x4 = jnp.concatenate([jnp.where(upper, over, two), jnp.where(upper, two, over)])
    x = start_block
    y4, _ = total(across(x), down(x4))
    y = lax.ppermute(slot_of(y4), every, from_row_group())
    downs = down(y4)
    y, x4_late, y4_late = lax.optimization_barrier((y, x4, y4))
    acrosses = across(y)
    gram = jnp.concatenate([grams_of(x4_late), grams_of(x4_late, y4_late)], axis=1)
    z4, gram = total(acrosses, downs, gram)
    gram2, gram = lax.optimization_barrier((grams_of(x4, y4, z4), gram))
    gram = exchanged(gram, 2)
    zz = lax.ppermute(slot_of(z4), every, from_row_group())
    for step in range(len(EXCHANGES)):
        gram2 = exchanged(gram2, step)
    length = col_count * width
    return close(gram, gram2, *begin(gram, length), x, y, zz, length)


def solution(mesh):
    fine = Mesh(mesh.devices.reshape(SIZES), NAMES)
    placed = (P(None, COL), P(COL), P(ROW, COL, None, None))
    return jax.shard_map(
        on_device, mesh=fine, in_specs=placed, out_specs=(P(), P(None, COL)), check_vma=False
    )
```

```python
import functools

import jax
import jax.numpy as jnp
from jax import lax
from jax.experimental import pallas as pl
from jax.experimental.pallas import tpu as pltpu
from jax.sharding import Mesh
from jax.sharding import PartitionSpec as P

SHIFT = 5.5
FULL = lax.Precision.HIGHEST
BLOCKS = lax.Precision.HIGH

SIZES = (2, 4, 4, 4, 2)
NAMES = ("zh", "y", "z", "x", "co")
ROW = ("zh", "y")
COL = ("z", "x", "co")

PLACE = (
    (5, 3, 2, 4, 7, 1, 0, 6),
    (2, 4, 5, 3, 0, 6, 7, 1),
    (0, 1, 7, 6, 2, 3, 5, 4),
    (7, 0, 4, 6, 2, 3, 1, 5),
    (3, 5, 4, 2, 1, 0, 6, 7),
    (4, 2, 3, 5, 1, 0, 6, 7),
    (6, 0, 1, 7, 4, 2, 3, 5),
    (1, 7, 6, 0, 3, 5, 4, 2),
)


def to_row_group():
    pairs = []
    for row in range(8):
        for z in range(4):
            for j in range(8):
                far = (row // 4) != (j // 4)
                z_to = (z + 2) % 4 if far else z
                pairs.append((row * 32 + z * 8 + j, j * 32 + z_to * 8 + PLACE[j][row]))
    return pairs


def from_row_group():
    return [(b, a) for a, b in to_row_group()]


def far_bits(row):
    return sum(((r // 4) != (row // 4)) << PLACE[row][r] for r in range(8))


def mm(a, b):
    return jnp.dot(a, b, precision=FULL, preferred_element_type=jnp.float32)
def mmt(a, b):
    return lax.dot_general(a, b, (((1,), (1,)), ((), ())), precision=FULL, preferred_element_type=jnp.float32)


def factor_and_inverse(g):
    n = g.shape[0]
    down = lax.broadcasted_iota(jnp.int32, (n, 2 * n), 0)
    along = lax.broadcasted_iota(jnp.int32, (n, 2 * n), 1)
    same = (down == along)[:, :n]
    diagonal = jnp.where(same, g, 0.0)
    root = jnp.sqrt(jnp.sum(diagonal, axis=0, keepdims=True))
    root_down = jnp.sqrt(jnp.sum(diagonal, axis=1, keepdims=True))
    wide = jnp.concatenate([g / root, jnp.where(same, 1.0, 0.0)], axis=1) / root_down
    for k in range(0, n - 2, 2):
        r0 = jnp.broadcast_to(wide[k : k + 1, :], (8, 2 * n))
        r1 = jnp.broadcast_to(wide[k + 1 : k + 2, :], (8, 2 * n))
        a = jnp.broadcast_to(r0[:, k : k + 1], r0.shape)
        b = jnp.broadcast_to(r0[:, k + 1 : k + 2], r0.shape)
        c = jnp.broadcast_to(r1[:, k + 1 : k + 2], r0.shape)
        c0 = jnp.broadcast_to(wide[:, k : k + 1], wide.shape)
        c1 = jnp.broadcast_to(wide[:, k + 1 : k + 2], wide.shape)
        det = 1.0 / (a * c - b * b)
        s0 = jnp.concatenate([(r0 * c - r1 * b) * det] * (n // 8), axis=0)
        s1 = jnp.concatenate([(r1 * a - r0 * b) * det] * (n // 8), axis=0)
        wide = jnp.where(down > k + 1, wide - (c0 * s0 + c1 * s1), wide)
    above = jnp.roll(wide, 1, axis=0)
    left = down - 1 == along
    b = jnp.sum(jnp.where(left, wide, 0.0), axis=1, keepdims=True)
    a = jnp.sum(jnp.where(left, above, 0.0), axis=1, keepdims=True)
    wide = jnp.where(lax.rem(down, 2) == 1, wide - (b / a) * above, wide)
    pivot = jnp.sum(jnp.where(down == along, wide, 0.0), axis=1, keepdims=True)
    wide = wide * (1.0 / jnp.sqrt(pivot))
    upper = jnp.where(down <= along, wide, 0.0)[:, :n] * root
    return jnp.transpose(upper), wide[:, n:]


def first_step(scale, both_ref, history_ref, first_ref, second_ref):
    n = both_ref.shape[0]
    g00 = both_ref[:, 3 * n : 4 * n] * scale
    g10 = both_ref[:, 4 * n : 5 * n] * scale
    low0, t0 = factor_and_inverse(g00)
    a0 = mmt(mm(t0, g10), t0)
    history_ref[0] = a0
    second_ref[:, 0:n] = -mm(a0, t0)
    second_ref[:, n : 2 * n] = t0
    p1 = second_ref[...]
    whole = jnp.concatenate(
        [
            jnp.concatenate([g00, jnp.transpose(g10)], axis=1),
            both_ref[:, 4 * n :] * scale,
        ],
        axis=0,
    )
    low1, t1 = factor_and_inverse(mmt(mm(p1, whole), p1))
    history_ref[1] = low1
    q1 = mm(t1, p1)
    second_ref[...] = q1
    first_ref[:, 0:n] = -lax.dot_general(
        low1, t0, (((0,), (0,)), ((), ())), precision=FULL, preferred_element_type=jnp.float32
    )
    first_ref[:, n : 3 * n] = q1


def last_step(
    scale, both_ref, half_ref, history0_ref, image_ref, second_ref, x_ref, y_ref, z_ref,
    history_ref, out_ref, g_ref, p_ref, v_ref,
):
    n = both_ref.shape[0]
    gram2 = (both_ref[:, 0 : 3 * n] + half_ref[...]) * scale
    eye = jnp.where(
        lax.broadcasted_iota(jnp.int32, (n, n), 0) == lax.broadcasted_iota(jnp.int32, (n, n), 1),
        SHIFT,
        0.0,
    )
    g_ref[0:n, 0:n] = both_ref[:, 3 * n : 4 * n] * scale
    g_ref[n : 2 * n, 0 : 2 * n] = both_ref[:, 4 * n :] * scale
    g_ref[0:n, n : 2 * n] = jnp.transpose(both_ref[:, 4 * n : 5 * n]) * scale
    g_ref[2 * n :, :] = gram2
    g_ref[0:n, 2 * n :] = jnp.transpose(gram2[:, 0:n])
    g_ref[n : 2 * n, 2 * n :] = jnp.transpose(gram2[:, n : 2 * n])
    history_ref[0, 0] = history0_ref[0] + eye
    history_ref[0, 1] = history0_ref[1]
    w1 = image_ref[...]
    q1 = second_ref[...]
    a1 = mmt(mm(w1, g_ref[:, 0 : 2 * n]), q1)
    history_ref[1, 0] = a1 + eye
    p_ref[...] = mm(a1, q1)
    w1 = jnp.concatenate([w1[:, 0 : 2 * n] - p_ref[...], w1[:, 2 * n :]], axis=1)
    low2, t2 = factor_and_inverse(mmt(mm(w1, g_ref[...]), w1))
    history_ref[1, 1] = low2
    v_ref[0:n] = x_ref[...]
    v_ref[n : 2 * n] = y_ref[...]
    v_ref[2 * n :] = z_ref[...]
    out_ref[...] = mm(t2, mm(w1, v_ref[...]))


def parts_of(v):
    high = v.astype(jnp.bfloat16)
    return high, (v - high.astype(jnp.float32)).astype(jnp.bfloat16)


def split_blocks(weight_ref, blocks_ref, high_ref, low_ref, held, arrived):
    slots, width = blocks_ref.shape[0], blocks_ref.shape[1]
    copies = [
        pltpu.make_async_copy(blocks_ref.at[s], held.at[s], arrived.at[s]) for s in range(slots)
    ]
    for copy in copies:
        copy.start()
    for s in range(slots):
        copies[s].wait()
        rows = pl.ds(s * width, width)
        high_ref[rows, :], low_ref[rows, :] = parts_of(held[s] * weight_ref[s])


def dot3(left, high, low, contract):
    rows = left[0].shape[0]
    dims = (((1,), (contract,)), ((), ()))
    both = lax.dot_general(
        jnp.concatenate(left, axis=0), high, dims, preferred_element_type=jnp.float32
    )
    rest = lax.dot_general(left[0], low, dims, preferred_element_type=jnp.float32)
    return both[:rows] + (both[rows:] + rest)


def down_kernel(four_ref, high_ref, low_ref, out_ref):
    slots, _, width = four_ref.shape
    total = None
    for s in range(slots):
        rows = pl.ds(s * width, width)
        term = dot3(parts_of(four_ref[s]), high_ref[rows, :], low_ref[rows, :], 0)
        total = term if total is None else total + term
    out_ref[...] = total


def across_kernel(lead_ref, energies_ref, own_ref, high_ref, low_ref, out_ref):
    slots, _, width = out_ref.shape
    left = parts_of(own_ref[...])
    for s in range(slots):
        rows = pl.ds(s * width, width)
        term = dot3(left, high_ref[rows, :], low_ref[rows, :], 1)
        out_ref[s] = term

    @pl.when(lead_ref[0] == 1)
    def _():
        out_ref[lead_ref[1]] += (energies_ref[...] - SHIFT) * own_ref[...]


def gram_kernel(*refs):
    *four_refs, out_ref, flat_ref = refs
    slots, vecs, width = four_refs[0].shape
    for i, four_ref in enumerate(four_refs):
        for s in range(slots):
            flat_ref[i * vecs : (i + 1) * vecs, s * width : (s + 1) * width] = four_ref[s]
    out_ref[...] = mmt(flat_ref[(len(four_refs) - 1) * vecs :, :], flat_ref[...])


LIMIT = pltpu.CompilerParams(vmem_limit_bytes=16 * 2**20)
IN_VMEM = pl.BlockSpec(memory_space=pltpu.VMEM)


def grams_of(*fours):
    slots, vecs, width = fours[0].shape
    return pl.pallas_call(
        gram_kernel,
        in_specs=[IN_VMEM] * len(fours),
        out_specs=IN_VMEM,
        out_shape=pltpu.VMEM((vecs, len(fours) * vecs), jnp.float32),
        scratch_shapes=[pltpu.VMEM((len(fours) * vecs, slots * width), jnp.float32)],
        compiler_params=LIMIT,
        name="gram",
    )(*fours)


def spread_kernel(parts_ref, out_ref):
    out_ref[...] = jnp.broadcast_to(jnp.sum(parts_ref[...], axis=0)[None], out_ref.shape)


def sum_spread(parts):
    return pl.pallas_call(
        spread_kernel,
        in_specs=[IN_VMEM],
        out_specs=IN_VMEM,
        out_shape=pltpu.VMEM(parts.shape, jnp.float32),
        compiler_params=LIMIT,
        name="sum_spread",
    )(parts)


def begin(both, length):
    vecs = both.shape[0]
    return pl.pallas_call(
        functools.partial(first_step, 1.0 / length),
        in_specs=[IN_VMEM],
        out_specs=(IN_VMEM,) * 3,
        out_shape=(
            pltpu.VMEM((2, vecs, vecs), jnp.float32),
            pltpu.VMEM((vecs, 3 * vecs), jnp.float32),
            pltpu.VMEM((vecs, 2 * vecs), jnp.float32),
        ),
        compiler_params=LIMIT,
        cost_estimate=pl.CostEstimate(flops=6 * 10**9, bytes_accessed=10**5, transcendentals=0),
        name="first_step",
    )(both)


def close(both, half, history0, image, second, x, y, z, length):
    vecs = x.shape[0]
    return pl.pallas_call(
        functools.partial(last_step, 1.0 / length),
        out_shape=(
            jax.ShapeDtypeStruct((2, 2, vecs, vecs), jnp.float32),
            jax.ShapeDtypeStruct(x.shape, jnp.float32),
        ),
        scratch_shapes=[
            pltpu.VMEM((3 * vecs, 3 * vecs), jnp.float32),
            pltpu.VMEM((vecs, 2 * vecs), jnp.float32),
            pltpu.VMEM((3 * vecs, x.shape[1]), jnp.float32),
        ],
        compiler_params=LIMIT,
        name="last_step",
    )(both, half, history0, image, second, x, y, z)


PAIRS = ([(0, 1), (1, 0), (2, 3), (3, 2)], [(0, 3), (3, 0), (1, 2), (2, 1)])


def across_half(value):
    pairs = [(h * 4 + z, (1 - h) * 4 + (z + 2) % 4) for h in range(2) for z in range(4)]
    return lax.ppermute(value, ("zh", "z"), pairs)


def on_device(start_block, energies, hamiltonian):
    vecs, width = start_block.shape
    col_count = lax.axis_size(COL)
    half = width // 2
    row = lax.axis_index(ROW)
    col = lax.axis_index(COL)
    z = lax.axis_index("z")
    core = lax.axis_index("co")
    place = lax.axis_index(("x", "co"))
    blocks = hamiltonian[:, 0]
    slots = blocks.shape[0]
    block_rows = row + 8 * jnp.arange(slots, dtype=jnp.int32)
    weight = jnp.where(block_rows < col, 1.0, jnp.where(block_rows == col, 0.5, 0.0)).astype(
        jnp.float32
    )
    lead = jnp.stack([(place == row).astype(jnp.int32), z])
    bits = jnp.int32(0)
    for r in range(8):
        bits = jnp.where(row == r, jnp.int32(far_bits(r)), bits)
    far = lax.shift_right_logical(bits, place) % 2 == 1
    slot = jnp.where(far, (z + 2) % 4, z)
    odd = lax.rem(z, 2) == 1
    upper = (z >= 2) != far
    weight, lead, slot, odd, upper, first = lax.optimization_barrier(
        (weight, lead, slot, odd, upper, core == 0)
    )
    in_slot = (jnp.arange(slots) == slot)[:, None, None]
    every = NAMES

    high, low = pl.pallas_call(
        split_blocks,
        in_specs=[pl.BlockSpec(memory_space=pltpu.SMEM), pl.BlockSpec(memory_space=pltpu.HBM)],
        out_specs=(IN_VMEM, IN_VMEM),
        out_shape=(pltpu.VMEM((slots * width, width), jnp.bfloat16),) * 2,
        scratch_shapes=[
            pltpu.VMEM(blocks.shape, jnp.float32),
            pltpu.SemaphoreType.DMA((slots,)),
        ],
        compiler_params=pltpu.CompilerParams(vmem_limit_bytes=58 * 2**20),
        name="split_blocks",
    )(weight, blocks)

    def down(four):
        return pl.pallas_call(
            down_kernel,
            in_specs=[IN_VMEM] * 3,
            out_specs=IN_VMEM,
            out_shape=pltpu.VMEM((vecs, width), jnp.float32),
            compiler_params=LIMIT,
            name="down",
        )(four, high, low)

    def across(own):
        return pl.pallas_call(
            across_kernel,
            in_specs=[pl.BlockSpec(memory_space=pltpu.SMEM)] + [IN_VMEM] * 4,
            out_specs=IN_VMEM,
            out_shape=pltpu.VMEM((slots, vecs, width), jnp.float32),
            compiler_params=LIMIT,
            name="across",
        )(lead, energies.reshape(1, width), own, high, low)

    def total(acrosses, downs, gram=None):
        arrived = lax.ppermute(downs, every, to_row_group())
        acrosses = lax.optimization_barrier(acrosses)
        part = acrosses + jnp.where(in_slot, arrived[None], 0.0)
        part = part.reshape(slots * vecs // 8, 8, width)
        low, high = part[..., :half], part[..., half:]
        mine = jnp.where(first, low, high)
        other = jnp.where(first, high, low)
        if gram is not None:
            other_half = across_half(gram)
        mine = mine + lax.ppermute(other, "co", [(0, 1), (1, 0)])
        pieces = lax.all_to_all(mine, ("z", "x"), 0, 0, tiled=True)
        whole = lax.all_to_all(sum_spread(pieces), ("z", "x"), 0, 0, tiled=True)
        if gram is not None:
            whole, other_half = lax.optimization_barrier((whole, other_half))
            gram = gram + other_half
        facing = lax.ppermute(whole, "co", [(0, 1), (1, 0)])
        low = jnp.where(first, whole, facing)
        high = jnp.where(first, facing, whole)
        four = jnp.concatenate([low, high], axis=-1).reshape(slots, vecs, width)
        return four, gram

    def slot_of(four):
        return jnp.sum(jnp.where(in_slot, four, 0.0), axis=0)

    moved = lax.ppermute(start_block, every, to_row_group())
    moved, high, low = lax.optimization_barrier((moved, high, low))
    near = lax.ppermute(moved, "z", [(0, 1), (1, 0), (2, 3), (3, 2)])
    two = jnp.stack([jnp.where(odd, near, moved), jnp.where(odd, moved, near)])
    over = lax.ppermute(two, "z", [(0, 2), (2, 0), (1, 3), (3, 1)])
    x4 = jnp.concatenate([jnp.where(upper, over, two), jnp.where(upper, two, over)])
    x = start_block
    y4, _ = total(across(x), down(x4))
    y = lax.ppermute(slot_of(y4), every, from_row_group())
    downs = down(y4)
    y, x4_late, y4_late = lax.optimization_barrier((y, x4, y4))
    acrosses = across(y)
    gram = jnp.concatenate([grams_of(x4_late), grams_of(x4_late, y4_late)], axis=1)
    z4, gram = total(acrosses, downs, gram)
    both = jnp.concatenate([grams_of(x4, y4, z4), gram], axis=1)
    zz = lax.ppermute(slot_of(z4), every, from_row_group())
    for pairs in PAIRS:
        both = both + lax.ppermute(both, "y", pairs)
    other_half = across_half(both[:, : 3 * vecs])
    length = col_count * width
    return close(both, other_half, *begin(both, length), x, y, zz, length)


def solution(mesh):
    fine = Mesh(mesh.devices.reshape(SIZES), NAMES)
    placed = (P(None, COL), P(COL), P(ROW, COL, None, None))
    return jax.shard_map(
        on_device, mesh=fine, in_specs=placed, out_specs=(P(), P(None, COL)), check_vma=False
    )
```

```python
import functools

import jax
import jax.numpy as jnp
from jax import lax
from jax.experimental import pallas as pl
from jax.experimental.pallas import tpu as pltpu
from jax.sharding import Mesh
from jax.sharding import PartitionSpec as P

SHIFT = 5.5
FULL = lax.Precision.HIGHEST
BLOCKS = lax.Precision.HIGH

SIZES = (2, 4, 4, 4, 2)
NAMES = ("zh", "y", "z", "x", "co")
ROW = ("zh", "y")
COL = ("z", "x", "co")

PLACE = (
    (5, 3, 1, 7, 4, 2, 0, 6),
    (2, 4, 6, 0, 3, 5, 7, 1),
    (3, 1, 7, 5, 2, 0, 6, 4),
    (0, 2, 4, 6, 1, 3, 5, 7),
    (0, 2, 4, 6, 1, 3, 5, 7),
    (3, 1, 7, 5, 2, 0, 6, 4),
    (6, 0, 2, 4, 7, 1, 3, 5),
    (1, 7, 5, 3, 0, 6, 4, 2),
)


def to_row_group():
    pairs = []
    for row in range(8):
        for z in range(4):
            for j in range(8):
                far = (row // 4) != (j // 4)
                z_to = (z + 2) % 4 if far else z
                pairs.append((row * 32 + z * 8 + j, j * 32 + z_to * 8 + PLACE[j][row]))
    return pairs


def from_row_group():
    return [(b, a) for a, b in to_row_group()]


def far_bits(row):
    return sum(((r // 4) != (row // 4)) << PLACE[row][r] for r in range(8))


def mm(a, b):
    return jnp.dot(a, b, precision=FULL, preferred_element_type=jnp.float32)
def mmt(a, b):
    return lax.dot_general(a, b, (((1,), (1,)), ((), ())), precision=FULL, preferred_element_type=jnp.float32)


def factor_and_inverse(g):
    n = g.shape[0]
    down = lax.broadcasted_iota(jnp.int32, (n, 2 * n), 0)
    along = lax.broadcasted_iota(jnp.int32, (n, 2 * n), 1)
    same = (down == along)[:, :n]
    diagonal = jnp.where(same, g, 0.0)
    root = jnp.sqrt(jnp.sum(diagonal, axis=0, keepdims=True))
    root_down = jnp.sqrt(jnp.sum(diagonal, axis=1, keepdims=True))
    wide = jnp.concatenate([g / root, jnp.where(same, 1.0, 0.0)], axis=1) / root_down
    for k in range(0, n - 2, 2):
        r0 = jnp.broadcast_to(wide[k : k + 1, :], (8, 2 * n))
        r1 = jnp.broadcast_to(wide[k + 1 : k + 2, :], (8, 2 * n))
        a = jnp.broadcast_to(r0[:, k : k + 1], r0.shape)
        b = jnp.broadcast_to(r0[:, k + 1 : k + 2], r0.shape)
        c = jnp.broadcast_to(r1[:, k + 1 : k + 2], r0.shape)
        c0 = jnp.broadcast_to(wide[:, k : k + 1], wide.shape)
        c1 = jnp.broadcast_to(wide[:, k + 1 : k + 2], wide.shape)
        det = 1.0 / (a * c - b * b)
        s0 = jnp.concatenate([(r0 * c - r1 * b) * det] * (n // 8), axis=0)
        s1 = jnp.concatenate([(r1 * a - r0 * b) * det] * (n // 8), axis=0)
        wide = jnp.where(down > k + 1, wide - (c0 * s0 + c1 * s1), wide)
    above = jnp.roll(wide, 1, axis=0)
    left = down - 1 == along
    b = jnp.sum(jnp.where(left, wide, 0.0), axis=1, keepdims=True)
    a = jnp.sum(jnp.where(left, above, 0.0), axis=1, keepdims=True)
    wide = jnp.where(lax.rem(down, 2) == 1, wide - (b / a) * above, wide)
    pivot = jnp.sum(jnp.where(down == along, wide, 0.0), axis=1, keepdims=True)
    wide = wide * (1.0 / jnp.sqrt(pivot))
    upper = jnp.where(down <= along, wide, 0.0)[:, :n] * root
    return jnp.transpose(upper), wide[:, n:]


def first_step(scale, both_ref, history_ref, first_ref, second_ref):
    n = both_ref.shape[0]
    g00 = both_ref[:, 3 * n : 4 * n] * scale
    g10 = both_ref[:, 4 * n : 5 * n] * scale
    low0, t0 = factor_and_inverse(g00)
    a0 = mmt(mm(t0, g10), t0)
    history_ref[0] = a0
    second_ref[:, 0:n] = -mm(a0, t0)
    second_ref[:, n : 2 * n] = t0
    p1 = second_ref[...]
    whole = jnp.concatenate(
        [
            jnp.concatenate([g00, jnp.transpose(g10)], axis=1),
            both_ref[:, 4 * n :] * scale,
        ],
        axis=0,
    )
    low1, t1 = factor_and_inverse(mmt(mm(p1, whole), p1))
    history_ref[1] = low1
    q1 = mm(t1, p1)
    second_ref[...] = q1
    first_ref[:, 0:n] = -lax.dot_general(
        low1, t0, (((0,), (0,)), ((), ())), precision=FULL, preferred_element_type=jnp.float32
    )
    first_ref[:, n : 3 * n] = q1


def last_step(
    scale, both_ref, half_ref, history0_ref, image_ref, second_ref, x_ref, y_ref, z_ref,
    history_ref, out_ref, g_ref, p_ref, v_ref,
):
    n = both_ref.shape[0]
    gram2 = (both_ref[:, 0 : 3 * n] + half_ref[:, 0 : 3 * n]) * scale
    eye = jnp.where(
        lax.broadcasted_iota(jnp.int32, (n, n), 0) == lax.broadcasted_iota(jnp.int32, (n, n), 1),
        SHIFT,
        0.0,
    )
    g_ref[0:n, 0:n] = both_ref[:, 3 * n : 4 * n] * scale
    g_ref[n : 2 * n, 0 : 2 * n] = both_ref[:, 4 * n :] * scale
    g_ref[0:n, n : 2 * n] = jnp.transpose(both_ref[:, 4 * n : 5 * n]) * scale
    g_ref[2 * n :, :] = gram2
    g_ref[0:n, 2 * n :] = jnp.transpose(gram2[:, 0:n])
    g_ref[n : 2 * n, 2 * n :] = jnp.transpose(gram2[:, n : 2 * n])
    history_ref[0, 0] = history0_ref[0] + eye
    history_ref[0, 1] = history0_ref[1]
    w1 = image_ref[...]
    q1 = second_ref[...]
    a1 = mmt(mm(w1, g_ref[:, 0 : 2 * n]), q1)
    history_ref[1, 0] = a1 + eye
    p_ref[...] = mm(a1, q1)
    w1 = jnp.concatenate([w1[:, 0 : 2 * n] - p_ref[...], w1[:, 2 * n :]], axis=1)
    low2, t2 = factor_and_inverse(mmt(mm(w1, g_ref[...]), w1))
    history_ref[1, 1] = low2
    v_ref[0:n] = x_ref[...]
    v_ref[n : 2 * n] = y_ref[...]
    v_ref[2 * n :] = z_ref[...]
    out_ref[...] = mm(t2, mm(w1, v_ref[...]))


def parts_of(v):
    high = v.astype(jnp.bfloat16)
    return high, (v - high.astype(jnp.float32)).astype(jnp.bfloat16)


def split_blocks(weight_ref, blocks_ref, high_ref, low_ref, held, arrived):
    slots, width = blocks_ref.shape[0], blocks_ref.shape[1]
    copies = [
        pltpu.make_async_copy(blocks_ref.at[s], held.at[s], arrived.at[s]) for s in range(slots)
    ]
    for copy in copies:
        copy.start()
    for s in range(slots):
        copies[s].wait()
        rows = pl.ds(s * width, width)
        high_ref[rows, :], low_ref[rows, :] = parts_of(held[s] * weight_ref[s])


def dot3(left, high, low, contract):
    rows = left[0].shape[0]
    dims = (((1,), (contract,)), ((), ()))
    both = lax.dot_general(
        jnp.concatenate(left, axis=0), high, dims, preferred_element_type=jnp.float32
    )
    rest = lax.dot_general(left[0], low, dims, preferred_element_type=jnp.float32)
    return both[:rows] + (both[rows:] + rest)


def down_kernel(four_ref, high_ref, low_ref, out_ref):
    slots, _, width = four_ref.shape
    total = None
    for s in range(slots):
        rows = pl.ds(s * width, width)
        term = dot3(parts_of(four_ref[s]), high_ref[rows, :], low_ref[rows, :], 0)
        total = term if total is None else total + term
    out_ref[...] = total


def across_kernel(lead_ref, energies_ref, own_ref, high_ref, low_ref, out_ref):
    slots, _, width = out_ref.shape
    left = parts_of(own_ref[...])
    for s in range(slots):
        rows = pl.ds(s * width, width)
        term = dot3(left, high_ref[rows, :], low_ref[rows, :], 1)
        out_ref[s] = term

    @pl.when(lead_ref[0] == 1)
    def _():
        out_ref[lead_ref[1]] += (energies_ref[...] - SHIFT) * own_ref[...]


def gram_kernel(*refs):
    *four_refs, out_ref, flat_ref = refs
    slots, vecs, width = four_refs[0].shape
    for i, four_ref in enumerate(four_refs):
        for s in range(slots):
            flat_ref[i * vecs : (i + 1) * vecs, s * width : (s + 1) * width] = four_ref[s]
    out_ref[...] = mmt(flat_ref[(len(four_refs) - 1) * vecs :, :], flat_ref[...])


LIMIT = pltpu.CompilerParams(vmem_limit_bytes=16 * 2**20)
IN_VMEM = pl.BlockSpec(memory_space=pltpu.VMEM)


def grams_of(*fours):
    slots, vecs, width = fours[0].shape
    return pl.pallas_call(
        gram_kernel,
        in_specs=[IN_VMEM] * len(fours),
        out_specs=IN_VMEM,
        out_shape=pltpu.VMEM((vecs, len(fours) * vecs), jnp.float32),
        scratch_shapes=[pltpu.VMEM((len(fours) * vecs, slots * width), jnp.float32)],
        compiler_params=LIMIT,
        name="gram",
    )(*fours)


def spread_kernel(parts_ref, out_ref):
    out_ref[...] = jnp.broadcast_to(jnp.sum(parts_ref[...], axis=0)[None], out_ref.shape)


def sum_spread(parts):
    return pl.pallas_call(
        spread_kernel,
        in_specs=[IN_VMEM],
        out_specs=IN_VMEM,
        out_shape=pltpu.VMEM(parts.shape, jnp.float32),
        compiler_params=LIMIT,
        name="sum_spread",
    )(parts)


def begin(both, length):
    vecs = both.shape[0]
    return pl.pallas_call(
        functools.partial(first_step, 1.0 / length),
        in_specs=[IN_VMEM],
        out_specs=(IN_VMEM,) * 3,
        out_shape=(
            pltpu.VMEM((2, vecs, vecs), jnp.float32),
            pltpu.VMEM((vecs, 3 * vecs), jnp.float32),
            pltpu.VMEM((vecs, 2 * vecs), jnp.float32),
        ),
        compiler_params=LIMIT,
        cost_estimate=pl.CostEstimate(flops=6 * 10**9, bytes_accessed=10**5, transcendentals=0),
        name="first_step",
    )(both)


def close(both, half, history0, image, second, x, y, z, length):
    vecs = x.shape[0]
    return pl.pallas_call(
        functools.partial(last_step, 1.0 / length),
        out_shape=(
            jax.ShapeDtypeStruct((2, 2, vecs, vecs), jnp.float32),
            jax.ShapeDtypeStruct(x.shape, jnp.float32),
        ),
        scratch_shapes=[
            pltpu.VMEM((3 * vecs, 3 * vecs), jnp.float32),
            pltpu.VMEM((vecs, 2 * vecs), jnp.float32),
            pltpu.VMEM((3 * vecs, x.shape[1]), jnp.float32),
        ],
        compiler_params=LIMIT,
        name="last_step",
    )(both, half, history0, image, second, x, y, z)


PAIRS = ([(0, 1), (1, 0), (2, 3), (3, 2)], [(0, 3), (3, 0), (1, 2), (2, 1)])


def across_half(value):
    pairs = [(h * 4 + z, (1 - h) * 4 + (z + 2) % 4) for h in range(2) for z in range(4)]
    return lax.ppermute(value, ("zh", "z"), pairs)


def on_device(start_block, energies, hamiltonian):
    vecs, width = start_block.shape
    col_count = lax.axis_size(COL)
    half = width // 2
    row = lax.axis_index(ROW)
    col = lax.axis_index(COL)
    z = lax.axis_index("z")
    core = lax.axis_index("co")
    place = lax.axis_index(("x", "co"))
    blocks = hamiltonian[:, 0]
    slots = blocks.shape[0]
    block_rows = row + 8 * jnp.arange(slots, dtype=jnp.int32)
    weight = jnp.where(block_rows < col, 1.0, jnp.where(block_rows == col, 0.5, 0.0)).astype(
        jnp.float32
    )
    lead = jnp.stack([(place == row).astype(jnp.int32), z])
    bits = jnp.int32(0)
    for r in range(8):
        bits = jnp.where(row == r, jnp.int32(far_bits(r)), bits)
    far = lax.shift_right_logical(bits, place) % 2 == 1
    slot = jnp.where(far, (z + 2) % 4, z)
    odd = lax.rem(z, 2) == 1
    upper = (z >= 2) != far
    weight, lead, slot, odd, upper, first = lax.optimization_barrier(
        (weight, lead, slot, odd, upper, core == 0)
    )
    in_slot = (jnp.arange(slots) == slot)[:, None, None]
    every = NAMES

    high, low = pl.pallas_call(
        split_blocks,
        in_specs=[pl.BlockSpec(memory_space=pltpu.SMEM), pl.BlockSpec(memory_space=pltpu.HBM)],
        out_specs=(IN_VMEM, IN_VMEM),
        out_shape=(pltpu.VMEM((slots * width, width), jnp.bfloat16),) * 2,
        scratch_shapes=[
            pltpu.VMEM(blocks.shape, jnp.float32),
            pltpu.SemaphoreType.DMA((slots,)),
        ],
        compiler_params=pltpu.CompilerParams(vmem_limit_bytes=58 * 2**20),
        name="split_blocks",
    )(weight, blocks)

    def down(four):
        return pl.pallas_call(
            down_kernel,
            in_specs=[IN_VMEM] * 3,
            out_specs=IN_VMEM,
            out_shape=pltpu.VMEM((vecs, width), jnp.float32),
            compiler_params=LIMIT,
            name="down",
        )(four, high, low)

    def across(own):
        return pl.pallas_call(
            across_kernel,
            in_specs=[pl.BlockSpec(memory_space=pltpu.SMEM)] + [IN_VMEM] * 4,
            out_specs=IN_VMEM,
            out_shape=pltpu.VMEM((slots, vecs, width), jnp.float32),
            compiler_params=LIMIT,
            name="across",
        )(lead, energies.reshape(1, width), own, high, low)

    def total(acrosses, downs, gram=None):
        arrived = lax.ppermute(downs, every, to_row_group())
        acrosses = lax.optimization_barrier(acrosses)
        part = acrosses + jnp.where(in_slot, arrived[None], 0.0)
        part = part.reshape(slots * vecs // 8, 8, width)
        low, high = part[..., :half], part[..., half:]
        mine = jnp.where(first, low, high)
        other = jnp.where(first, high, low)
        if gram is not None:
            other_half = across_half(gram)
        mine = mine + lax.ppermute(other, "co", [(0, 1), (1, 0)])
        pieces = lax.all_to_all(mine, ("z", "x"), 0, 0, tiled=True)
        whole = lax.all_to_all(sum_spread(pieces), ("z", "x"), 0, 0, tiled=True)
        if gram is not None:
            whole, other_half = lax.optimization_barrier((whole, other_half))
            gram = gram + other_half
        facing = lax.ppermute(whole, "co", [(0, 1), (1, 0)])
        low = jnp.where(first, whole, facing)
        high = jnp.where(first, facing, whole)
        four = jnp.concatenate([low, high], axis=-1).reshape(slots, vecs, width)
        return four, gram

    def slot_of(four):
        return jnp.sum(jnp.where(in_slot, four, 0.0), axis=0)

    moved = lax.ppermute(start_block, every, to_row_group())
    moved, high, low = lax.optimization_barrier((moved, high, low))
    near = lax.ppermute(moved, "z", [(0, 1), (1, 0), (2, 3), (3, 2)])
    two = jnp.stack([jnp.where(odd, near, moved), jnp.where(odd, moved, near)])
    over = lax.ppermute(two, "co", [(0, 1), (1, 0)])
    x4 = jnp.concatenate([jnp.where(upper, over, two), jnp.where(upper, two, over)])
    x = start_block
    y4, _ = total(across(x), down(x4))
    y = lax.ppermute(slot_of(y4), every, from_row_group())
    downs = down(y4)
    y, x4_late, y4_late = lax.optimization_barrier((y, x4, y4))
    acrosses = across(y)
    gram = jnp.concatenate([grams_of(x4_late), grams_of(x4_late, y4_late)], axis=1)
    z4, gram = total(acrosses, downs, gram)
    both = jnp.concatenate([grams_of(x4, y4, z4), gram], axis=1)
    for pairs in PAIRS:
        both = both + lax.ppermute(both, "y", pairs)
    other_half = across_half(both)
    mine, both = lax.optimization_barrier((slot_of(z4), both))
    zz = lax.ppermute(mine, every, from_row_group())
    length = col_count * width
    return close(both, other_half, *begin(both, length), x, y, zz, length)


def solution(mesh):
    fine = Mesh(mesh.devices.reshape(SIZES), NAMES)
    placed = (P(None, COL), P(COL), P(ROW, COL, None, None))
    return jax.shard_map(
        on_device, mesh=fine, in_specs=placed, out_specs=(P(), P(None, COL)), check_vma=False
    )
```

```python
import functools

import jax
import jax.numpy as jnp
from jax import lax
from jax.experimental import pallas as pl
from jax.experimental.pallas import tpu as pltpu
from jax.sharding import Mesh
from jax.sharding import PartitionSpec as P

SHIFT = 5.5
FULL = lax.Precision.HIGHEST
BLOCKS = lax.Precision.HIGH

SIZES = (2, 4, 4, 4, 2)
NAMES = ("zh", "y", "z", "x", "co")
ROW = ("zh", "y")
COL = ("z", "x", "co")

PLACE = (
    (5, 3, 1, 7, 4, 2, 0, 6),
    (2, 4, 6, 0, 3, 5, 7, 1),
    (3, 1, 7, 5, 2, 0, 6, 4),
    (0, 2, 4, 6, 1, 3, 5, 7),
    (0, 2, 4, 6, 1, 3, 5, 7),
    (3, 1, 7, 5, 2, 0, 6, 4),
    (6, 0, 2, 4, 7, 1, 3, 5),
    (1, 7, 5, 3, 0, 6, 4, 2),
)


def to_row_group():
    pairs = []
    for row in range(8):
        for z in range(4):
            for j in range(8):
                far = (row // 4) != (j // 4)
                z_to = (z + 2) % 4 if far else z
                pairs.append((row * 32 + z * 8 + j, j * 32 + z_to * 8 + PLACE[j][row]))
    return pairs


def from_row_group():
    return [(b, a) for a, b in to_row_group()]


def far_bits(row):
    return sum(((r // 4) != (row // 4)) << PLACE[row][r] for r in range(8))


def mm(a, b):
    return jnp.dot(a, b, precision=FULL, preferred_element_type=jnp.float32)
def mmt(a, b):
    return lax.dot_general(a, b, (((1,), (1,)), ((), ())), precision=FULL, preferred_element_type=jnp.float32)


def factor_and_inverse(g):
    n = g.shape[0]
    same = lax.broadcasted_iota(jnp.int32, (n, n), 0) == lax.broadcasted_iota(jnp.int32, (n, n), 1)
    diagonal = jnp.where(same, g, 0.0)
    root = jnp.sqrt(jnp.sum(diagonal, axis=0, keepdims=True))
    root_down = jnp.sqrt(jnp.sum(diagonal, axis=1, keepdims=True))
    wide = jnp.concatenate([g / root, jnp.where(same, 1.0, 0.0)], axis=1) / root_down
    tiles = [wide[8 * b : 8 * b + 8, :] for b in range(n // 8)]
    solved = [jnp.zeros_like(tile) for tile in tiles]
    shape = tiles[0].shape
    down = lax.broadcasted_iota(jnp.int32, shape, 0)

    def lane(tile, k):
        return jnp.broadcast_to(tile[:, k : k + 1], shape)

    for k in range(0, n, 4):
        at, first = k // 8, k % 8
        r0, r1, r2, r3 = (
            jnp.broadcast_to(tiles[at][first + i : first + i + 1, :], shape) for i in range(4)
        )
        a10, a11 = lane(r1, k), lane(r1, k + 1)
        a20, a21, a22 = lane(r2, k), lane(r2, k + 1), lane(r2, k + 2)
        a30, a31, a32, a33 = lane(r3, k), lane(r3, k + 1), lane(r3, k + 2), lane(r3, k + 3)
        d0 = lane(r0, k)
        i0 = 1.0 / d0
        m10, m20, m30 = a10 * i0, a20 * i0, a30 * i0
        d1 = a11 - m10 * a10
        t21, t31 = a21 - m20 * a10, a31 - m30 * a10
        i1 = 1.0 / d1
        m21, m31 = t21 * i1, t31 * i1
        d2 = a22 - m20 * a20 - m21 * t21
        t32 = a32 - m30 * a20 - m31 * t21
        i2 = 1.0 / d2
        m32 = t32 * i2
        d3 = a33 - m30 * a30 - m31 * t31 - m32 * t32
        i3 = 1.0 / d3
        r1 = r1 - m10 * r0
        r2 = r2 - m20 * r0 - m21 * r1
        r3 = r3 - m30 * r0 - m31 * r1 - m32 * r2
        for i, (row, pivot) in enumerate(((r0, d0), (r1, d1), (r2, d2), (r3, d3))):
            solved[at] = jnp.where(down == first + i, row * (1.0 / jnp.sqrt(pivot)), solved[at])
        s0, s1, s2, s3 = r0 * i0, r1 * i1, r2 * i2, r3 * i3
        for b in range((k + 4) // 8, n // 8):
            c0, c1, c2, c3 = (lane(tiles[b], k + i) for i in range(4))
            c1 = c1 - m10 * c0
            c2 = c2 - m20 * c0 - m21 * c1
            c3 = c3 - m30 * c0 - m31 * c1 - m32 * c2
            less = tiles[b] - (c0 * s0 + c1 * s1) - (c2 * s2 + c3 * s3)
            tiles[b] = jnp.where(down >= 4, less, tiles[b]) if b == at else less
    wide = jnp.concatenate(solved, axis=0)
    keep = lax.broadcasted_iota(jnp.int32, (n, n), 0) <= lax.broadcasted_iota(jnp.int32, (n, n), 1)
    upper = jnp.where(keep, wide[:, :n], 0.0) * root
    return jnp.transpose(upper), wide[:, n:]


def first_step(scale, both_ref, history_ref, first_ref, second_ref):
    n = both_ref.shape[0]
    g00 = both_ref[:, 3 * n : 4 * n] * scale
    g10 = both_ref[:, 4 * n : 5 * n] * scale
    low0, t0 = factor_and_inverse(g00)
    a0 = mmt(mm(t0, g10), t0)
    history_ref[0] = a0
    second_ref[:, 0:n] = -mm(a0, t0)
    second_ref[:, n : 2 * n] = t0
    p1 = second_ref[...]
    whole = jnp.concatenate(
        [
            jnp.concatenate([g00, jnp.transpose(g10)], axis=1),
            both_ref[:, 4 * n :] * scale,
        ],
        axis=0,
    )
    low1, t1 = factor_and_inverse(mmt(mm(p1, whole), p1))
    history_ref[1] = low1
    q1 = mm(t1, p1)
    second_ref[...] = q1
    first_ref[:, 0:n] = -lax.dot_general(
        low1, t0, (((0,), (0,)), ((), ())), precision=FULL, preferred_element_type=jnp.float32
    )
    first_ref[:, n : 3 * n] = q1


def last_step(
    scale, both_ref, half_ref, history0_ref, image_ref, second_ref, x_ref, y_ref, z_ref,
    history_ref, out_ref, g_ref, p_ref, v_ref,
):
    n = both_ref.shape[0]
    gram2 = (both_ref[:, 0 : 3 * n] + half_ref[:, 0 : 3 * n]) * scale
    eye = jnp.where(
        lax.broadcasted_iota(jnp.int32, (n, n), 0) == lax.broadcasted_iota(jnp.int32, (n, n), 1),
        SHIFT,
        0.0,
    )
    g_ref[0:n, 0:n] = both_ref[:, 3 * n : 4 * n] * scale
    g_ref[n : 2 * n, 0 : 2 * n] = both_ref[:, 4 * n :] * scale
    g_ref[0:n, n : 2 * n] = jnp.transpose(both_ref[:, 4 * n : 5 * n]) * scale
    g_ref[2 * n :, :] = gram2
    g_ref[0:n, 2 * n :] = jnp.transpose(gram2[:, 0:n])
    g_ref[n : 2 * n, 2 * n :] = jnp.transpose(gram2[:, n : 2 * n])
    history_ref[0, 0] = history0_ref[0] + eye
    history_ref[0, 1] = history0_ref[1]
    w1 = image_ref[...]
    q1 = second_ref[...]
    a1 = mmt(mm(w1, g_ref[:, 0 : 2 * n]), q1)
    history_ref[1, 0] = a1 + eye
    p_ref[...] = mm(a1, q1)
    w1 = jnp.concatenate([w1[:, 0 : 2 * n] - p_ref[...], w1[:, 2 * n :]], axis=1)
    low2, t2 = factor_and_inverse(mmt(mm(w1, g_ref[...]), w1))
    history_ref[1, 1] = low2
    v_ref[0:n] = x_ref[...]
    v_ref[n : 2 * n] = y_ref[...]
    v_ref[2 * n :] = z_ref[...]
    out_ref[...] = mm(t2, mm(w1, v_ref[...]))


def parts_of(v):
    high = v.astype(jnp.bfloat16)
    return high, (v - high.astype(jnp.float32)).astype(jnp.bfloat16)


def split_blocks(energies_ref, blocks_ref, high_ref, low_ref, lead_ref, held, arrived):
    slots, width = blocks_ref.shape[0], blocks_ref.shape[1]
    copies = [
        pltpu.make_async_copy(blocks_ref.at[s], held.at[s], arrived.at[s]) for s in range(slots)
    ]
    for copy in copies:
        copy.start()
    row, col = lax.axis_index(ROW), lax.axis_index(COL)
    for s in range(slots):
        block_row = row + 8 * s
        shifted = energies_ref[...] - SHIFT
        lead_ref[s : s + 1, :] = shifted * jnp.where(block_row == col, 1.0, 0.0)
        weight = jnp.where(block_row < col, 1.0, jnp.where(block_row == col, 0.5, 0.0))
        copies[s].wait()
        rows = pl.ds(s * width, width)
        high_ref[rows, :], low_ref[rows, :] = parts_of(held[s] * weight)


def dot3(left, high, low, contract):
    rows = left[0].shape[0]
    dims = (((1,), (contract,)), ((), ()))
    both = lax.dot_general(
        jnp.concatenate(left, axis=0), high, dims, preferred_element_type=jnp.float32
    )
    rest = lax.dot_general(left[0], low, dims, preferred_element_type=jnp.float32)
    return both[:rows] + (both[rows:] + rest)


def down_kernel(four_ref, high_ref, low_ref, out_ref):
    slots, _, width = four_ref.shape
    total = None
    for s in range(slots):
        rows = pl.ds(s * width, width)
        term = dot3(parts_of(four_ref[s]), high_ref[rows, :], low_ref[rows, :], 0)
        total = term if total is None else total + term
    out_ref[...] = total


def across_kernel(lead_ref, own_ref, high_ref, low_ref, out_ref):
    slots, _, width = out_ref.shape
    left = parts_of(own_ref[...])
    for s in range(slots):
        rows = pl.ds(s * width, width)
        term = dot3(left, high_ref[rows, :], low_ref[rows, :], 1)
        out_ref[s] = term + lead_ref[s : s + 1, :] * own_ref[...]


def gram_kernel(*refs):
    *four_refs, out_ref, flat_ref = refs
    slots, vecs, width = four_refs[0].shape
    for i, four_ref in enumerate(four_refs):
        for s in range(slots):
            flat_ref[i * vecs : (i + 1) * vecs, s * width : (s + 1) * width] = four_ref[s]
    out_ref[...] = mmt(flat_ref[(len(four_refs) - 1) * vecs :, :], flat_ref[...])


LIMIT = pltpu.CompilerParams(vmem_limit_bytes=16 * 2**20)
IN_VMEM = pl.BlockSpec(memory_space=pltpu.VMEM)


def grams_of(*fours):
    slots, vecs, width = fours[0].shape
    return pl.pallas_call(
        gram_kernel,
        in_specs=[IN_VMEM] * len(fours),
        out_specs=IN_VMEM,
        out_shape=pltpu.VMEM((vecs, len(fours) * vecs), jnp.float32),
        scratch_shapes=[pltpu.VMEM((len(fours) * vecs, slots * width), jnp.float32)],
        compiler_params=LIMIT,
        name="gram",
    )(*fours)


def spread_kernel(parts_ref, out_ref):
    out_ref[...] = jnp.broadcast_to(jnp.sum(parts_ref[...], axis=0)[None], out_ref.shape)


def sum_spread(parts):
    return pl.pallas_call(
        spread_kernel,
        in_specs=[IN_VMEM],
        out_specs=IN_VMEM,
        out_shape=pltpu.VMEM(parts.shape, jnp.float32),
        compiler_params=LIMIT,
        name="sum_spread",
    )(parts)


def begin(both, length):
    vecs = both.shape[0]
    return pl.pallas_call(
        functools.partial(first_step, 1.0 / length),
        in_specs=[IN_VMEM],
        out_specs=(IN_VMEM,) * 3,
        out_shape=(
            pltpu.VMEM((2, vecs, vecs), jnp.float32),
            pltpu.VMEM((vecs, 3 * vecs), jnp.float32),
            pltpu.VMEM((vecs, 2 * vecs), jnp.float32),
        ),
        compiler_params=LIMIT,
        cost_estimate=pl.CostEstimate(flops=6 * 10**9, bytes_accessed=10**5, transcendentals=0),
        name="first_step",
    )(both)


def close(both, half, history0, image, second, x, y, z, length):
    vecs = x.shape[0]
    return pl.pallas_call(
        functools.partial(last_step, 1.0 / length),
        out_shape=(
            jax.ShapeDtypeStruct((2, 2, vecs, vecs), jnp.float32),
            jax.ShapeDtypeStruct(x.shape, jnp.float32),
        ),
        scratch_shapes=[
            pltpu.VMEM((3 * vecs, 3 * vecs), jnp.float32),
            pltpu.VMEM((vecs, 2 * vecs), jnp.float32),
            pltpu.VMEM((3 * vecs, x.shape[1]), jnp.float32),
        ],
        compiler_params=LIMIT,
        name="last_step",
    )(both, half, history0, image, second, x, y, z)


PAIRS = ([(0, 1), (1, 0), (2, 3), (3, 2)], [(0, 3), (3, 0), (1, 2), (2, 1)])


def across_half(value):
    pairs = [(h * 4 + z, (1 - h) * 4 + (z + 2) % 4) for h in range(2) for z in range(4)]
    return lax.ppermute(value, ("zh", "z"), pairs)


def on_device(start_block, energies, hamiltonian):
    vecs, width = start_block.shape
    col_count = lax.axis_size(COL)
    half = width // 2
    row = lax.axis_index(ROW)
    col = lax.axis_index(COL)
    z = lax.axis_index("z")
    core = lax.axis_index("co")
    place = lax.axis_index(("x", "co"))
    blocks = hamiltonian[:, 0]
    slots = blocks.shape[0]
    bits = jnp.int32(0)
    for r in range(8):
        bits = jnp.where(row == r, jnp.int32(far_bits(r)), bits)
    far = lax.shift_right_logical(bits, place) % 2 == 1
    slot = jnp.where(far, (z + 2) % 4, z)
    odd = lax.rem(z, 2) == 1
    upper = (z >= 2) != far
    energies, slot, odd, upper, first = lax.optimization_barrier(
        (energies, slot, odd, upper, core == 0)
    )
    in_slot = (jnp.arange(slots) == slot)[:, None, None]
    every = NAMES

    high, low, lead = pl.pallas_call(
        split_blocks,
        in_specs=[IN_VMEM, pl.BlockSpec(memory_space=pltpu.HBM)],
        out_specs=(IN_VMEM, IN_VMEM, IN_VMEM),
        out_shape=(
            pltpu.VMEM((slots * width, width), jnp.bfloat16),
            pltpu.VMEM((slots * width, width), jnp.bfloat16),
            pltpu.VMEM((slots, width), jnp.float32),
        ),
        scratch_shapes=[
            pltpu.VMEM(blocks.shape, jnp.float32),
            pltpu.SemaphoreType.DMA((slots,)),
        ],
        compiler_params=pltpu.CompilerParams(vmem_limit_bytes=58 * 2**20),
        name="split_blocks",
    )(energies.reshape(1, width), blocks)

    def down(four):
        return pl.pallas_call(
            down_kernel,
            in_specs=[IN_VMEM] * 3,
            out_specs=IN_VMEM,
            out_shape=pltpu.VMEM((vecs, width), jnp.float32),
            compiler_params=LIMIT,
            name="down",
        )(four, high, low)

    def across(own):
        return pl.pallas_call(
            across_kernel,
            in_specs=[IN_VMEM] * 4,
            out_specs=IN_VMEM,
            out_shape=pltpu.VMEM((slots, vecs, width), jnp.float32),
            compiler_params=LIMIT,
            name="across",
        )(lead, own, high, low)

    def total(acrosses, downs, gram=None):
        arrived = lax.ppermute(downs, every, to_row_group())
        acrosses = lax.optimization_barrier(acrosses)
        part = acrosses + jnp.where(in_slot, arrived[None], 0.0)
        part = part.reshape(slots * vecs // 8, 8, width)
        low, high = part[..., :half], part[..., half:]
        mine = jnp.where(first, low, high)
        other = jnp.where(first, high, low)
        if gram is not None:
            other_half = across_half(gram)
        mine = mine + lax.ppermute(other, "co", [(0, 1), (1, 0)])
        pieces = lax.all_to_all(mine, ("z", "x"), 0, 0, tiled=True)
        whole = lax.all_to_all(sum_spread(pieces), ("z", "x"), 0, 0, tiled=True)
        if gram is not None:
            whole, other_half = lax.optimization_barrier((whole, other_half))
            gram = gram + other_half
        facing = lax.ppermute(whole, "co", [(0, 1), (1, 0)])
        low = jnp.where(first, whole, facing)
        high = jnp.where(first, facing, whole)
        four = jnp.concatenate([low, high], axis=-1).reshape(slots, vecs, width)
        return four, gram

    def slot_of(four):
        return jnp.sum(jnp.where(in_slot, four, 0.0), axis=0)

    moved = lax.ppermute(start_block, every, to_row_group())
    moved, high, low = lax.optimization_barrier((moved, high, low))
    near = lax.ppermute(moved, "z", [(0, 1), (1, 0), (2, 3), (3, 2)])
    two = jnp.stack([jnp.where(odd, near, moved), jnp.where(odd, moved, near)])
    over = lax.ppermute(two, "co", [(0, 1), (1, 0)])
    x4 = jnp.concatenate([jnp.where(upper, over, two), jnp.where(upper, two, over)])
    x = start_block
    y4, _ = total(across(x), down(x4))
    y = lax.ppermute(slot_of(y4), every, from_row_group())
    downs = down(y4)
    y, x4_late, y4_late = lax.optimization_barrier((y, x4, y4))
    acrosses = across(y)
    gram = jnp.concatenate([grams_of(x4_late), grams_of(x4_late, y4_late)], axis=1)
    z4, gram = total(acrosses, downs, gram)
    both = jnp.concatenate([grams_of(x4, y4, z4), gram], axis=1)
    zz = lax.ppermute(slot_of(z4), every, from_row_group())
    for pairs in PAIRS:
        both = both + lax.ppermute(both, "y", pairs)
    other_half = across_half(both)
    length = col_count * width
    return close(both, other_half, *begin(both, length), x, y, zz, length)


def solution(mesh):
    fine = Mesh(mesh.devices.reshape(SIZES), NAMES)
    placed = (P(None, COL), P(COL), P(ROW, COL, None, None))
    return jax.shard_map(
        on_device, mesh=fine, in_specs=placed, out_specs=(P(), P(None, COL)), check_vma=False
    )
```

```python
import functools

import jax
import jax.numpy as jnp
from jax import lax
from jax.experimental import pallas as pl
from jax.experimental.pallas import tpu as pltpu
from jax.sharding import Mesh
from jax.sharding import PartitionSpec as P

SHIFT = 5.5
FULL = lax.Precision.HIGHEST
BLOCKS = lax.Precision.HIGH

SIZES = (2, 4, 4, 4, 2)
NAMES = ("zh", "y", "z", "x", "co")
ROW = ("zh", "y")
COL = ("z", "x", "co")

PLACE = (
    (5, 3, 1, 7, 4, 2, 0, 6),
    (2, 4, 6, 0, 3, 5, 7, 1),
    (3, 1, 7, 5, 2, 0, 6, 4),
    (0, 2, 4, 6, 1, 3, 5, 7),
    (0, 2, 4, 6, 1, 3, 5, 7),
    (3, 1, 7, 5, 2, 0, 6, 4),
    (6, 0, 2, 4, 7, 1, 3, 5),
    (1, 7, 5, 3, 0, 6, 4, 2),
)


def to_row_group():
    pairs = []
    for row in range(8):
        for z in range(4):
            for j in range(8):
                far = (row // 4) != (j // 4)
                z_to = (z + 2) % 4 if far else z
                pairs.append((row * 32 + z * 8 + j, j * 32 + z_to * 8 + PLACE[j][row]))
    return pairs


def from_row_group():
    return [(b, a) for a, b in to_row_group()]


def far_bits(row):
    return sum(((r // 4) != (row // 4)) << PLACE[row][r] for r in range(8))


def mm(a, b):
    return jnp.dot(a, b, precision=FULL, preferred_element_type=jnp.float32)
def mmt(a, b):
    return lax.dot_general(a, b, (((1,), (1,)), ((), ())), precision=FULL, preferred_element_type=jnp.float32)


def factor_and_inverse(g):
    n = g.shape[0]
    same = lax.broadcasted_iota(jnp.int32, (n, n), 0) == lax.broadcasted_iota(jnp.int32, (n, n), 1)
    diagonal = jnp.where(same, g, 0.0)
    root = jnp.sqrt(jnp.sum(diagonal, axis=0, keepdims=True))
    root_down = jnp.sqrt(jnp.sum(diagonal, axis=1, keepdims=True))
    wide = jnp.concatenate([g / root, jnp.where(same, 1.0, 0.0)], axis=1) / root_down
    tiles = [wide[8 * b : 8 * b + 8, :] for b in range(n // 8)]
    solved = [jnp.zeros_like(tile) for tile in tiles]
    shape = tiles[0].shape
    down = lax.broadcasted_iota(jnp.int32, shape, 0)

    def lane(tile, k):
        return jnp.broadcast_to(tile[:, k : k + 1], shape)

    for k in range(0, n, 4):
        at, first = k // 8, k % 8
        r0, r1, r2, r3 = (
            jnp.broadcast_to(tiles[at][first + i : first + i + 1, :], shape) for i in range(4)
        )
        a10, a11 = lane(r1, k), lane(r1, k + 1)
        a20, a21, a22 = lane(r2, k), lane(r2, k + 1), lane(r2, k + 2)
        a30, a31, a32, a33 = lane(r3, k), lane(r3, k + 1), lane(r3, k + 2), lane(r3, k + 3)
        d0 = lane(r0, k)
        i0 = 1.0 / d0
        m10, m20, m30 = a10 * i0, a20 * i0, a30 * i0
        d1 = a11 - m10 * a10
        t21, t31 = a21 - m20 * a10, a31 - m30 * a10
        i1 = 1.0 / d1
        m21, m31 = t21 * i1, t31 * i1
        d2 = a22 - m20 * a20 - m21 * t21
        t32 = a32 - m30 * a20 - m31 * t21
        i2 = 1.0 / d2
        m32 = t32 * i2
        d3 = a33 - m30 * a30 - m31 * t31 - m32 * t32
        i3 = 1.0 / d3
        r1 = r1 - m10 * r0
        r2 = r2 - m20 * r0 - m21 * r1
        r3 = r3 - m30 * r0 - m31 * r1 - m32 * r2
        for i, (row, pivot) in enumerate(((r0, d0), (r1, d1), (r2, d2), (r3, d3))):
            solved[at] = jnp.where(down == first + i, row * (1.0 / jnp.sqrt(pivot)), solved[at])
        s0, s1, s2, s3 = r0 * i0, r1 * i1, r2 * i2, r3 * i3
        for b in range((k + 4) // 8, n // 8):
            c0, c1, c2, c3 = (lane(tiles[b], k + i) for i in range(4))
            c1 = c1 - m10 * c0
            c2 = c2 - m20 * c0 - m21 * c1
            c3 = c3 - m30 * c0 - m31 * c1 - m32 * c2
            less = tiles[b] - (c0 * s0 + c1 * s1) - (c2 * s2 + c3 * s3)
            tiles[b] = jnp.where(down >= 4, less, tiles[b]) if b == at else less
    wide = jnp.concatenate(solved, axis=0)
    keep = lax.broadcasted_iota(jnp.int32, (n, n), 0) <= lax.broadcasted_iota(jnp.int32, (n, n), 1)
    upper = jnp.where(keep, wide[:, :n], 0.0) * root
    return jnp.transpose(upper), wide[:, n:]


def first_step(scale, both_ref, history_ref, first_ref, second_ref, own_ref):
    n = both_ref.shape[0]
    g00 = both_ref[:, 3 * n : 4 * n] * scale
    g10 = both_ref[:, 4 * n : 5 * n] * scale
    low0, t0 = factor_and_inverse(g00)
    a0 = mmt(mm(t0, g10), t0)
    history_ref[0] = a0
    second_ref[:, 0:n] = -mm(a0, t0)
    second_ref[:, n : 2 * n] = t0
    p1 = second_ref[...]
    whole = jnp.concatenate(
        [
            jnp.concatenate([g00, jnp.transpose(g10)], axis=1),
            both_ref[:, 4 * n :] * scale,
        ],
        axis=0,
    )
    low1, t1 = factor_and_inverse(mmt(mm(p1, whole), p1))
    history_ref[1] = low1
    q1 = mm(t1, p1)
    second_ref[...] = q1
    own_ref[...] = mmt(mm(q1, whole), q1)
    first_ref[:, 0:n] = -lax.dot_general(
        low1, t0, (((0,), (0,)), ((), ())), precision=FULL, preferred_element_type=jnp.float32
    )
    first_ref[:, n : 3 * n] = q1


def last_step(
    scale, both_ref, half_ref, history0_ref, image_ref, second_ref, own_ref, x_ref, y_ref, z_ref,
    history_ref, out_ref, g_ref, p_ref, v_ref, s_ref,
):
    n = both_ref.shape[0]
    gram2 = (both_ref[:, 0 : 3 * n] + half_ref[:, 0 : 3 * n]) * scale
    eye = jnp.where(
        lax.broadcasted_iota(jnp.int32, (n, n), 0) == lax.broadcasted_iota(jnp.int32, (n, n), 1),
        SHIFT,
        0.0,
    )
    g_ref[0:n, 0:n] = both_ref[:, 3 * n : 4 * n] * scale
    g_ref[n : 2 * n, 0 : 2 * n] = both_ref[:, 4 * n :] * scale
    g_ref[0:n, n : 2 * n] = jnp.transpose(both_ref[:, 4 * n : 5 * n]) * scale
    g_ref[2 * n :, :] = gram2
    g_ref[0:n, 2 * n :] = jnp.transpose(gram2[:, 0:n])
    g_ref[n : 2 * n, 2 * n :] = jnp.transpose(gram2[:, n : 2 * n])
    history_ref[0, 0] = history0_ref[0] + eye
    history_ref[0, 1] = history0_ref[1]
    w1 = image_ref[...]
    q1 = second_ref[...]
    against = mm(w1, g_ref[...])
    a1 = mmt(against[:, 0 : 2 * n], q1)
    history_ref[1, 0] = a1 + eye
    s_ref[0:n] = mmt(against, w1)
    s_ref[n : 2 * n] = mm(a1, own_ref[...])
    s_ref[2 * n :] = mmt(a1 + a1 - s_ref[n : 2 * n], a1)
    low2, t2 = factor_and_inverse(s_ref[0:n] - s_ref[2 * n :])
    history_ref[1, 1] = low2
    p_ref[...] = mm(a1, q1)
    w1 = jnp.concatenate([w1[:, 0 : 2 * n] - p_ref[...], w1[:, 2 * n :]], axis=1)
    v_ref[0:n] = x_ref[...]
    v_ref[n : 2 * n] = y_ref[...]
    v_ref[2 * n :] = z_ref[...]
    out_ref[...] = mm(t2, mm(w1, v_ref[...]))


def parts_of(v):
    high = v.astype(jnp.bfloat16)
    return high, (v - high.astype(jnp.float32)).astype(jnp.bfloat16)


def split_blocks(energies_ref, blocks_ref, high_ref, low_ref, lead_ref, held, arrived):
    slots, width = blocks_ref.shape[0], blocks_ref.shape[1]
    copies = [
        pltpu.make_async_copy(blocks_ref.at[s], held.at[s], arrived.at[s]) for s in range(slots)
    ]
    for copy in copies:
        copy.start()
    row, col = lax.axis_index(ROW), lax.axis_index(COL)
    for s in range(slots):
        block_row = row + 8 * s
        shifted = energies_ref[...] - SHIFT
        lead_ref[s : s + 1, :] = shifted * jnp.where(block_row == col, 1.0, 0.0)
        weight = jnp.where(block_row < col, 1.0, jnp.where(block_row == col, 0.5, 0.0))
        copies[s].wait()
        rows = pl.ds(s * width, width)
        high_ref[rows, :], low_ref[rows, :] = parts_of(held[s] * weight)


def dot3(left, high, low, contract):
    rows = left[0].shape[0]
    dims = (((1,), (contract,)), ((), ()))
    both = lax.dot_general(
        jnp.concatenate(left, axis=0), high, dims, preferred_element_type=jnp.float32
    )
    rest = lax.dot_general(left[0], low, dims, preferred_element_type=jnp.float32)
    return both[:rows] + (both[rows:] + rest)


def down_kernel(four_ref, high_ref, low_ref, out_ref):
    slots, _, width = four_ref.shape
    total = None
    for s in range(slots):
        rows = pl.ds(s * width, width)
        term = dot3(parts_of(four_ref[s]), high_ref[rows, :], low_ref[rows, :], 0)
        total = term if total is None else total + term
    out_ref[...] = total


def across_kernel(lead_ref, own_ref, high_ref, low_ref, out_ref):
    slots, _, width = out_ref.shape
    left = parts_of(own_ref[...])
    for s in range(slots):
        rows = pl.ds(s * width, width)
        term = dot3(left, high_ref[rows, :], low_ref[rows, :], 1)
        out_ref[s] = term + lead_ref[s : s + 1, :] * own_ref[...]


def gram_kernel(*refs):
    *four_refs, out_ref, flat_ref = refs
    slots, vecs, width = four_refs[0].shape
    for i, four_ref in enumerate(four_refs):
        for s in range(slots):
            flat_ref[i * vecs : (i + 1) * vecs, s * width : (s + 1) * width] = four_ref[s]
    out_ref[...] = mmt(flat_ref[(len(four_refs) - 1) * vecs :, :], flat_ref[...])


LIMIT = pltpu.CompilerParams(vmem_limit_bytes=16 * 2**20)
IN_VMEM = pl.BlockSpec(memory_space=pltpu.VMEM)


def grams_of(*fours):
    slots, vecs, width = fours[0].shape
    return pl.pallas_call(
        gram_kernel,
        in_specs=[IN_VMEM] * len(fours),
        out_specs=IN_VMEM,
        out_shape=pltpu.VMEM((vecs, len(fours) * vecs), jnp.float32),
        scratch_shapes=[pltpu.VMEM((len(fours) * vecs, slots * width), jnp.float32)],
        compiler_params=LIMIT,
        name="gram",
    )(*fours)


def spread_kernel(parts_ref, out_ref):
    out_ref[...] = jnp.broadcast_to(jnp.sum(parts_ref[...], axis=0)[None], out_ref.shape)


def sum_spread(parts):
    return pl.pallas_call(
        spread_kernel,
        in_specs=[IN_VMEM],
        out_specs=IN_VMEM,
        out_shape=pltpu.VMEM(parts.shape, jnp.float32),
        compiler_params=LIMIT,
        name="sum_spread",
    )(parts)


def plus_kernel(left_ref, right_ref, out_ref):
    out_ref[...] = left_ref[...] + right_ref[...]


def plus(left, right):
    return pl.pallas_call(
        plus_kernel,
        in_specs=[IN_VMEM] * 2,
        out_specs=IN_VMEM,
        out_shape=pltpu.VMEM(left.shape, jnp.float32),
        compiler_params=LIMIT,
        name="plus",
    )(left, right)


def begin(both, length):
    vecs = both.shape[0]
    return pl.pallas_call(
        functools.partial(first_step, 1.0 / length),
        in_specs=[IN_VMEM],
        out_specs=(IN_VMEM,) * 4,
        out_shape=(
            pltpu.VMEM((2, vecs, vecs), jnp.float32),
            pltpu.VMEM((vecs, 3 * vecs), jnp.float32),
            pltpu.VMEM((vecs, 2 * vecs), jnp.float32),
            pltpu.VMEM((vecs, vecs), jnp.float32),
        ),
        compiler_params=LIMIT,
        cost_estimate=pl.CostEstimate(flops=6 * 10**9, bytes_accessed=10**5, transcendentals=0),
        name="first_step",
    )(both)


def close(both, half, history0, image, second, own, x, y, z, length):
    vecs = x.shape[0]
    return pl.pallas_call(
        functools.partial(last_step, 1.0 / length),
        out_shape=(
            jax.ShapeDtypeStruct((2, 2, vecs, vecs), jnp.float32),
            jax.ShapeDtypeStruct(x.shape, jnp.float32),
        ),
        scratch_shapes=[
            pltpu.VMEM((3 * vecs, 3 * vecs), jnp.float32),
            pltpu.VMEM((vecs, 2 * vecs), jnp.float32),
            pltpu.VMEM((3 * vecs, x.shape[1]), jnp.float32),
            pltpu.VMEM((3 * vecs, vecs), jnp.float32),
        ],
        compiler_params=LIMIT,
        name="last_step",
    )(both, half, history0, image, second, own, x, y, z)


PAIRS = ([(0, 1), (1, 0), (2, 3), (3, 2)], [(0, 3), (3, 0), (1, 2), (2, 1)])


def across_half(value):
    pairs = [(h * 4 + z, (1 - h) * 4 + (z + 2) % 4) for h in range(2) for z in range(4)]
    return lax.ppermute(value, ("zh", "z"), pairs)


def on_device(start_block, energies, hamiltonian):
    vecs, width = start_block.shape
    col_count = lax.axis_size(COL)
    half = width // 2
    row = lax.axis_index(ROW)
    col = lax.axis_index(COL)
    z = lax.axis_index("z")
    core = lax.axis_index("co")
    place = lax.axis_index(("x", "co"))
    blocks = hamiltonian[:, 0]
    slots = blocks.shape[0]
    bits = jnp.int32(0)
    for r in range(8):
        bits = jnp.where(row == r, jnp.int32(far_bits(r)), bits)
    far = lax.shift_right_logical(bits, place) % 2 == 1
    slot = jnp.where(far, (z + 2) % 4, z)
    odd = lax.rem(z, 2) == 1
    upper = (z >= 2) != far
    energies, slot, odd, upper, first = lax.optimization_barrier(
        (energies, slot, odd, upper, core == 0)
    )
    in_slot = (jnp.arange(slots) == slot)[:, None, None]
    every = NAMES

    high, low, lead = pl.pallas_call(
        split_blocks,
        in_specs=[IN_VMEM, pl.BlockSpec(memory_space=pltpu.HBM)],
        out_specs=(IN_VMEM, IN_VMEM, IN_VMEM),
        out_shape=(
            pltpu.VMEM((slots * width, width), jnp.bfloat16),
            pltpu.VMEM((slots * width, width), jnp.bfloat16),
            pltpu.VMEM((slots, width), jnp.float32),
        ),
        scratch_shapes=[
            pltpu.VMEM(blocks.shape, jnp.float32),
            pltpu.SemaphoreType.DMA((slots,)),
        ],
        compiler_params=pltpu.CompilerParams(vmem_limit_bytes=58 * 2**20),
        name="split_blocks",
    )(energies.reshape(1, width), blocks)

    def down(four):
        return pl.pallas_call(
            down_kernel,
            in_specs=[IN_VMEM] * 3,
            out_specs=IN_VMEM,
            out_shape=pltpu.VMEM((vecs, width), jnp.float32),
            compiler_params=LIMIT,
            name="down",
        )(four, high, low)

    def across(own):
        return pl.pallas_call(
            across_kernel,
            in_specs=[IN_VMEM] * 4,
            out_specs=IN_VMEM,
            out_shape=pltpu.VMEM((slots, vecs, width), jnp.float32),
            compiler_params=LIMIT,
            name="across",
        )(lead, own, high, low)

    def total(acrosses, downs, gram=None):
        arrived = lax.ppermute(downs, every, to_row_group())
        acrosses = lax.optimization_barrier(acrosses)
        part = acrosses + jnp.where(in_slot, arrived[None], 0.0)
        part = part.reshape(slots * vecs // 8, 8, width)
        low, high = part[..., :half], part[..., half:]
        mine = jnp.where(first, low, high)
        other = jnp.where(first, high, low)
        if gram is not None:
            other_half = across_half(gram)
        mine = mine + lax.ppermute(other, "co", [(0, 1), (1, 0)])
        pieces = lax.all_to_all(mine, ("z", "x"), 0, 0, tiled=True)
        whole = lax.all_to_all(sum_spread(pieces), ("z", "x"), 0, 0, tiled=True)
        if gram is not None:
            whole, other_half = lax.optimization_barrier((whole, other_half))
            gram = gram + other_half
        facing = lax.ppermute(whole, "co", [(0, 1), (1, 0)])
        low = jnp.where(first, whole, facing)
        high = jnp.where(first, facing, whole)
        four = jnp.concatenate([low, high], axis=-1).reshape(slots, vecs, width)
        return four, gram

    def slot_of(four):
        return jnp.sum(jnp.where(in_slot, four, 0.0), axis=0)

    moved = lax.ppermute(start_block, every, to_row_group())
    moved, high, low = lax.optimization_barrier((moved, high, low))
    near = lax.ppermute(moved, "z", [(0, 1), (1, 0), (2, 3), (3, 2)])
    two = jnp.stack([jnp.where(odd, near, moved), jnp.where(odd, moved, near)])
    over = lax.ppermute(two, "co", [(0, 1), (1, 0)])
    x4 = jnp.concatenate([jnp.where(upper, over, two), jnp.where(upper, two, over)])
    x = start_block
    y4, _ = total(across(x), down(x4))
    y = lax.ppermute(slot_of(y4), every, from_row_group())
    downs = down(y4)
    y, x4_late, y4_late = lax.optimization_barrier((y, x4, y4))
    acrosses = across(y)
    gram = jnp.concatenate([grams_of(x4_late), grams_of(x4_late, y4_late)], axis=1)
    z4, gram = total(acrosses, downs, gram)
    both = jnp.concatenate([grams_of(x4, y4, z4), gram], axis=1)
    zz = lax.ppermute(slot_of(z4), every, from_row_group())
    for pairs in PAIRS:
        both = plus(both, lax.ppermute(both, "y", pairs))
    other_half = across_half(both)
    length = col_count * width
    return close(both, other_half, *begin(both, length), x, y, zz, length)


def solution(mesh):
    fine = Mesh(mesh.devices.reshape(SIZES), NAMES)
    placed = (P(None, COL), P(COL), P(ROW, COL, None, None))
    return jax.shard_map(
        on_device, mesh=fine, in_specs=placed, out_specs=(P(), P(None, COL)), check_vma=False
    )
```

```python
import functools

import jax
import jax.numpy as jnp
from jax import lax
from jax.experimental import pallas as pl
from jax.experimental.pallas import tpu as pltpu
from jax.sharding import Mesh
from jax.sharding import PartitionSpec as P

SHIFT = 5.5
FULL = lax.Precision.HIGHEST
BLOCKS = lax.Precision.HIGH

SIZES = (2, 4, 4, 4, 2)
NAMES = ("zh", "y", "z", "x", "co")
ROW = ("zh", "y")
COL = ("z", "x", "co")

PLACE = (
    (5, 3, 1, 7, 4, 2, 0, 6),
    (2, 4, 6, 0, 3, 5, 7, 1),
    (3, 1, 7, 5, 2, 0, 6, 4),
    (0, 2, 4, 6, 1, 3, 5, 7),
    (0, 2, 4, 6, 1, 3, 5, 7),
    (3, 1, 7, 5, 2, 0, 6, 4),
    (6, 0, 2, 4, 7, 1, 3, 5),
    (1, 7, 5, 3, 0, 6, 4, 2),
)


def to_row_group():
    pairs = []
    for row in range(8):
        for z in range(4):
            for j in range(8):
                far = (row // 4) != (j // 4)
                z_to = (z + 2) % 4 if far else z
                pairs.append((row * 32 + z * 8 + j, j * 32 + z_to * 8 + PLACE[j][row]))
    return pairs


def from_row_group():
    return [(b, a) for a, b in to_row_group()]


def far_bits(row):
    return sum(((r // 4) != (row // 4)) << PLACE[row][r] for r in range(8))


def mm(a, b):
    return jnp.dot(a, b, precision=FULL, preferred_element_type=jnp.float32)
def mmt(a, b):
    return lax.dot_general(a, b, (((1,), (1,)), ((), ())), precision=FULL, preferred_element_type=jnp.float32)


def factor_and_inverse(g):
    n = g.shape[0]
    same = lax.broadcasted_iota(jnp.int32, (n, n), 0) == lax.broadcasted_iota(jnp.int32, (n, n), 1)
    diagonal = jnp.where(same, g, 0.0)
    root = jnp.sqrt(jnp.sum(diagonal, axis=0, keepdims=True))
    root_down = jnp.sqrt(jnp.sum(diagonal, axis=1, keepdims=True))
    wide = jnp.concatenate([g / root, jnp.where(same, 1.0, 0.0)], axis=1) / root_down
    tiles = [wide[8 * b : 8 * b + 8, :] for b in range(n // 8)]
    solved = [jnp.zeros_like(tile) for tile in tiles]
    shape = tiles[0].shape
    down = lax.broadcasted_iota(jnp.int32, shape, 0)

    def lane(tile, k):
        return jnp.broadcast_to(tile[:, k : k + 1], shape)

    for k in range(0, n, 4):
        at, first = k // 8, k % 8
        r0, r1, r2, r3 = (
            jnp.broadcast_to(tiles[at][first + i : first + i + 1, :], shape) for i in range(4)
        )
        a10, a11 = lane(r1, k), lane(r1, k + 1)
        a20, a21, a22 = lane(r2, k), lane(r2, k + 1), lane(r2, k + 2)
        a30, a31, a32, a33 = lane(r3, k), lane(r3, k + 1), lane(r3, k + 2), lane(r3, k + 3)
        d0 = lane(r0, k)
        i0 = 1.0 / d0
        m10, m20, m30 = a10 * i0, a20 * i0, a30 * i0
        d1 = a11 - m10 * a10
        t21, t31 = a21 - m20 * a10, a31 - m30 * a10
        i1 = 1.0 / d1
        m21, m31 = t21 * i1, t31 * i1
        d2 = a22 - m20 * a20 - m21 * t21
        t32 = a32 - m30 * a20 - m31 * t21
        i2 = 1.0 / d2
        m32 = t32 * i2
        d3 = a33 - m30 * a30 - m31 * t31 - m32 * t32
        i3 = 1.0 / d3
        r1 = r1 - m10 * r0
        r2 = r2 - m20 * r0 - m21 * r1
        r3 = r3 - m30 * r0 - m31 * r1 - m32 * r2
        for i, (row, pivot) in enumerate(((r0, d0), (r1, d1), (r2, d2), (r3, d3))):
            solved[at] = jnp.where(down == first + i, row * (1.0 / jnp.sqrt(pivot)), solved[at])
        s0, s1, s2, s3 = r0 * i0, r1 * i1, r2 * i2, r3 * i3
        for b in range((k + 4) // 8, n // 8):
            c0, c1, c2, c3 = (lane(tiles[b], k + i) for i in range(4))
            c1 = c1 - m10 * c0
            c2 = c2 - m20 * c0 - m21 * c1
            c3 = c3 - m30 * c0 - m31 * c1 - m32 * c2
            less = tiles[b] - (c0 * s0 + c1 * s1) - (c2 * s2 + c3 * s3)
            tiles[b] = jnp.where(down >= 4, less, tiles[b]) if b == at else less
    wide = jnp.concatenate(solved, axis=0)
    keep = lax.broadcasted_iota(jnp.int32, (n, n), 0) <= lax.broadcasted_iota(jnp.int32, (n, n), 1)
    upper = jnp.where(keep, wide[:, :n], 0.0) * root
    return jnp.transpose(upper), wide[:, n:]


def first_step(scale, both_ref, history_ref, first_ref, second_ref, own_ref):
    n = both_ref.shape[0]
    g00 = both_ref[:, 3 * n : 4 * n] * scale
    g10 = both_ref[:, 4 * n : 5 * n] * scale
    low0, t0 = factor_and_inverse(g00)
    a0 = mmt(mm(t0, g10), t0)
    history_ref[0] = a0
    second_ref[:, 0:n] = -mm(a0, t0)
    second_ref[:, n : 2 * n] = t0
    p1 = second_ref[...]
    whole = jnp.concatenate(
        [
            jnp.concatenate([g00, jnp.transpose(g10)], axis=1),
            both_ref[:, 4 * n :] * scale,
        ],
        axis=0,
    )
    low1, t1 = factor_and_inverse(mmt(mm(p1, whole), p1))
    history_ref[1] = low1
    q1 = mm(t1, p1)
    second_ref[...] = q1
    own_ref[...] = mmt(mm(q1, whole), q1)
    first_ref[:, 0:n] = -lax.dot_general(
        low1, t0, (((0,), (0,)), ((), ())), precision=FULL, preferred_element_type=jnp.float32
    )
    first_ref[:, n : 3 * n] = q1


def last_step(
    scale, both_ref, half_ref, history0_ref, image_ref, second_ref, own_ref, x_ref, y_ref, z_ref,
    history_ref, out_ref, g_ref, p_ref, v_ref, s_ref,
):
    n = both_ref.shape[0]
    gram2 = (both_ref[:, 0 : 3 * n] + half_ref[:, 0 : 3 * n]) * scale
    eye = jnp.where(
        lax.broadcasted_iota(jnp.int32, (n, n), 0) == lax.broadcasted_iota(jnp.int32, (n, n), 1),
        SHIFT,
        0.0,
    )
    g_ref[0:n, 0:n] = both_ref[:, 3 * n : 4 * n] * scale
    g_ref[n : 2 * n, 0 : 2 * n] = both_ref[:, 4 * n :] * scale
    g_ref[0:n, n : 2 * n] = jnp.transpose(both_ref[:, 4 * n : 5 * n]) * scale
    g_ref[2 * n :, :] = gram2
    g_ref[0:n, 2 * n :] = jnp.transpose(gram2[:, 0:n])
    g_ref[n : 2 * n, 2 * n :] = jnp.transpose(gram2[:, n : 2 * n])
    history_ref[0, 0] = history0_ref[0] + eye
    history_ref[0, 1] = history0_ref[1]
    w1 = image_ref[...]
    q1 = second_ref[...]
    against = mm(w1, g_ref[...])
    a1 = mmt(against[:, 0 : 2 * n], q1)
    history_ref[1, 0] = a1 + eye
    s_ref[0:n] = mmt(against, w1)
    s_ref[n : 2 * n] = mm(a1, own_ref[...])
    s_ref[2 * n :] = mmt(a1 + a1 - s_ref[n : 2 * n], a1)
    low2, t2 = factor_and_inverse(s_ref[0:n] - s_ref[2 * n :])
    history_ref[1, 1] = low2
    p_ref[...] = mm(a1, q1)
    w1 = jnp.concatenate([w1[:, 0 : 2 * n] - p_ref[...], w1[:, 2 * n :]], axis=1)
    v_ref[0:n] = x_ref[...]
    v_ref[n : 2 * n] = y_ref[...]
    v_ref[2 * n :] = z_ref[...]
    out_ref[...] = mm(t2, mm(w1, v_ref[...]))


def parts_of(v):
    high = v.astype(jnp.bfloat16)
    return high, (v - high.astype(jnp.float32)).astype(jnp.bfloat16)


def split_blocks(energies_ref, blocks_ref, high_ref, low_ref, lead_ref, held, arrived):
    slots, width = blocks_ref.shape[0], blocks_ref.shape[1]
    copies = [
        pltpu.make_async_copy(blocks_ref.at[s], held.at[s], arrived.at[s]) for s in range(slots)
    ]
    for copy in copies:
        copy.start()
    row, col = lax.axis_index(ROW), lax.axis_index(COL)
    for s in range(slots):
        block_row = row + 8 * s
        shifted = energies_ref[...] - SHIFT
        lead_ref[s : s + 1, :] = shifted * jnp.where(block_row == col, 1.0, 0.0)
        weight = jnp.where(block_row < col, 1.0, jnp.where(block_row == col, 0.5, 0.0))
        copies[s].wait()
        rows = pl.ds(s * width, width)
        high_ref[rows, :], low_ref[rows, :] = parts_of(held[s] * weight)


def dot3(left, high, low, contract):
    rows = left[0].shape[0]
    dims = (((1,), (contract,)), ((), ()))
    both = lax.dot_general(
        jnp.concatenate(left, axis=0), high, dims, preferred_element_type=jnp.float32
    )
    rest = lax.dot_general(left[0], low, dims, preferred_element_type=jnp.float32)
    return both[:rows] + (both[rows:] + rest)


def down_kernel(four_ref, high_ref, low_ref, out_ref):
    slots, _, width = four_ref.shape
    total = None
    for s in range(slots):
        rows = pl.ds(s * width, width)
        term = dot3(parts_of(four_ref[s]), high_ref[rows, :], low_ref[rows, :], 0)
        total = term if total is None else total + term
    out_ref[...] = total


def across_kernel(lead_ref, own_ref, high_ref, low_ref, out_ref):
    slots, _, width = out_ref.shape
    left = parts_of(own_ref[...])
    for s in range(slots):
        rows = pl.ds(s * width, width)
        term = dot3(left, high_ref[rows, :], low_ref[rows, :], 1)
        out_ref[s] = term + lead_ref[s : s + 1, :] * own_ref[...]


def gram_kernel(*refs):
    *four_refs, out_ref, flat_ref = refs
    slots, vecs, width = four_refs[0].shape
    for i, four_ref in enumerate(four_refs):
        for s in range(slots):
            flat_ref[i * vecs : (i + 1) * vecs, s * width : (s + 1) * width] = four_ref[s]
    out_ref[...] = mmt(flat_ref[(len(four_refs) - 1) * vecs :, :], flat_ref[...])


LIMIT = pltpu.CompilerParams(vmem_limit_bytes=16 * 2**20)
IN_VMEM = pl.BlockSpec(memory_space=pltpu.VMEM)


def grams_of(*fours):
    slots, vecs, width = fours[0].shape
    return pl.pallas_call(
        gram_kernel,
        in_specs=[IN_VMEM] * len(fours),
        out_specs=IN_VMEM,
        out_shape=pltpu.VMEM((vecs, len(fours) * vecs), jnp.float32),
        scratch_shapes=[pltpu.VMEM((len(fours) * vecs, slots * width), jnp.float32)],
        compiler_params=LIMIT,
        name="gram",
    )(*fours)


def spread_kernel(parts_ref, out_ref):
    out_ref[...] = jnp.broadcast_to(jnp.sum(parts_ref[...], axis=0)[None], out_ref.shape)


def sum_spread(parts):
    return pl.pallas_call(
        spread_kernel,
        in_specs=[IN_VMEM],
        out_specs=IN_VMEM,
        out_shape=pltpu.VMEM(parts.shape, jnp.float32),
        compiler_params=LIMIT,
        name="sum_spread",
    )(parts)


def plus_kernel(left_ref, right_ref, out_ref):
    out_ref[...] = left_ref[...] + right_ref[...]


def plus(left, right):
    return pl.pallas_call(
        plus_kernel,
        in_specs=[IN_VMEM] * 2,
        out_specs=IN_VMEM,
        out_shape=pltpu.VMEM(left.shape, jnp.float32),
        compiler_params=LIMIT,
        name="plus",
    )(left, right)


def begin(both, length):
    vecs = both.shape[0]
    return pl.pallas_call(
        functools.partial(first_step, 1.0 / length),
        in_specs=[IN_VMEM],
        out_specs=(IN_VMEM,) * 4,
        out_shape=(
            pltpu.VMEM((2, vecs, vecs), jnp.float32),
            pltpu.VMEM((vecs, 3 * vecs), jnp.float32),
            pltpu.VMEM((vecs, 2 * vecs), jnp.float32),
            pltpu.VMEM((vecs, vecs), jnp.float32),
        ),
        compiler_params=LIMIT,
        cost_estimate=pl.CostEstimate(flops=6 * 10**9, bytes_accessed=10**5, transcendentals=0),
        name="first_step",
    )(both)


def close(both, half, history0, image, second, own, x, y, z, length):
    vecs = x.shape[0]
    return pl.pallas_call(
        functools.partial(last_step, 1.0 / length),
        out_shape=(
            jax.ShapeDtypeStruct((2, 2, vecs, vecs), jnp.float32),
            jax.ShapeDtypeStruct(x.shape, jnp.float32),
        ),
        scratch_shapes=[
            pltpu.VMEM((3 * vecs, 3 * vecs), jnp.float32),
            pltpu.VMEM((vecs, 2 * vecs), jnp.float32),
            pltpu.VMEM((3 * vecs, x.shape[1]), jnp.float32),
            pltpu.VMEM((3 * vecs, vecs), jnp.float32),
        ],
        compiler_params=LIMIT,
        name="last_step",
    )(both, half, history0, image, second, own, x, y, z)


PAIRS = ([(0, 1), (1, 0), (2, 3), (3, 2)], [(0, 3), (3, 0), (1, 2), (2, 1)])


def across_half(value):
    pairs = [(h * 4 + z, (1 - h) * 4 + (z + 2) % 4) for h in range(2) for z in range(4)]
    return lax.ppermute(value, ("zh", "z"), pairs)


def on_device(start_block, energies, hamiltonian):
    vecs, width = start_block.shape
    col_count = lax.axis_size(COL)
    half = width // 2
    row = lax.axis_index(ROW)
    col = lax.axis_index(COL)
    z = lax.axis_index("z")
    core = lax.axis_index("co")
    place = lax.axis_index(("x", "co"))
    blocks = hamiltonian[:, 0]
    slots = blocks.shape[0]
    bits = jnp.int32(0)
    for r in range(8):
        bits = jnp.where(row == r, jnp.int32(far_bits(r)), bits)
    far = lax.shift_right_logical(bits, place) % 2 == 1
    slot = jnp.where(far, (z + 2) % 4, z)
    odd = lax.rem(z, 2) == 1
    upper = (z >= 2) != far
    energies, slot, odd, upper, first = lax.optimization_barrier(
        (energies, slot, odd, upper, core == 0)
    )
    in_slot = (jnp.arange(slots) == slot)[:, None, None]
    every = NAMES

    high, low, lead = pl.pallas_call(
        split_blocks,
        in_specs=[IN_VMEM, pl.BlockSpec(memory_space=pltpu.HBM)],
        out_specs=(IN_VMEM, IN_VMEM, IN_VMEM),
        out_shape=(
            pltpu.VMEM((slots * width, width), jnp.bfloat16),
            pltpu.VMEM((slots * width, width), jnp.bfloat16),
            pltpu.VMEM((slots, width), jnp.float32),
        ),
        scratch_shapes=[
            pltpu.VMEM(blocks.shape, jnp.float32),
            pltpu.SemaphoreType.DMA((slots,)),
        ],
        compiler_params=pltpu.CompilerParams(vmem_limit_bytes=58 * 2**20),
        name="split_blocks",
    )(energies.reshape(1, width), blocks)

    def down(four):
        return pl.pallas_call(
            down_kernel,
            in_specs=[IN_VMEM] * 3,
            out_specs=IN_VMEM,
            out_shape=pltpu.VMEM((vecs, width), jnp.float32),
            compiler_params=LIMIT,
            name="down",
        )(four, high, low)

    def across(own):
        return pl.pallas_call(
            across_kernel,
            in_specs=[IN_VMEM] * 4,
            out_specs=IN_VMEM,
            out_shape=pltpu.VMEM((slots, vecs, width), jnp.float32),
            compiler_params=LIMIT,
            name="across",
        )(lead, own, high, low)

    def total(acrosses, downs, gram=None):
        arrived = lax.ppermute(downs, every, to_row_group())
        acrosses, gram = lax.optimization_barrier((acrosses, gram))
        part = acrosses + jnp.where(in_slot, arrived[None], 0.0)
        part = part.reshape(slots * vecs // 8, 8, width)
        low, high = part[..., :half], part[..., half:]
        mine = jnp.where(first, low, high)
        other = jnp.where(first, high, low)
        if gram is not None:
            other_half = across_half(gram)
        mine = mine + lax.ppermute(other, "co", [(0, 1), (1, 0)])
        pieces = lax.all_to_all(mine, ("z", "x"), 0, 0, tiled=True)
        whole = lax.all_to_all(sum_spread(pieces), ("z", "x"), 0, 0, tiled=True)
        if gram is not None:
            whole, other_half = lax.optimization_barrier((whole, other_half))
            gram = gram + other_half
        facing = lax.ppermute(whole, "co", [(0, 1), (1, 0)])
        low = jnp.where(first, whole, facing)
        high = jnp.where(first, facing, whole)
        four = jnp.concatenate([low, high], axis=-1).reshape(slots, vecs, width)
        return four, gram

    def slot_of(four):
        return jnp.sum(jnp.where(in_slot, four, 0.0), axis=0)

    moved = lax.ppermute(start_block, every, to_row_group())
    moved, high, low = lax.optimization_barrier((moved, high, low))
    near = lax.ppermute(moved, "z", [(0, 1), (1, 0), (2, 3), (3, 2)])
    two = jnp.stack([jnp.where(odd, near, moved), jnp.where(odd, moved, near)])
    over = lax.ppermute(two, "co", [(0, 1), (1, 0)])
    x4 = jnp.concatenate([jnp.where(upper, over, two), jnp.where(upper, two, over)])
    x = start_block
    y4, _ = total(across(x), down(x4))
    y = lax.ppermute(slot_of(y4), every, from_row_group())
    downs = down(y4)
    y, x4_late, y4_late = lax.optimization_barrier((y, x4, y4))
    acrosses = across(y)
    gram = jnp.concatenate([grams_of(x4_late), grams_of(x4_late, y4_late)], axis=1)
    z4, gram = total(acrosses, downs, gram)
    both = jnp.concatenate([grams_of(x4, y4, z4), gram], axis=1)
    zz = lax.ppermute(slot_of(z4), every, from_row_group())
    for pairs in PAIRS:
        both = plus(both, lax.ppermute(both, "y", pairs))
    other_half = across_half(both)
    length = col_count * width
    return close(both, other_half, *begin(both, length), x, y, zz, length)


def solution(mesh):
    fine = Mesh(mesh.devices.reshape(SIZES), NAMES)
    placed = (P(None, COL), P(COL), P(ROW, COL, None, None))
    return jax.shard_map(
        on_device, mesh=fine, in_specs=placed, out_specs=(P(), P(None, COL)), check_vma=False
    )
```

```python
import functools

import jax
import jax.numpy as jnp
from jax import lax
from jax.experimental import pallas as pl
from jax.experimental.pallas import tpu as pltpu
from jax.sharding import Mesh
from jax.sharding import PartitionSpec as P

SHIFT = 5.5
FULL = lax.Precision.HIGHEST
BLOCKS = lax.Precision.HIGH

SIZES = (2, 4, 4, 4, 2)
NAMES = ("zh", "y", "z", "x", "co")
ROW = ("zh", "y")
COL = ("z", "x", "co")

PLACE = (
    (5, 3, 1, 7, 4, 2, 0, 6),
    (2, 4, 6, 0, 3, 5, 7, 1),
    (3, 1, 7, 5, 2, 0, 6, 4),
    (0, 2, 4, 6, 1, 3, 5, 7),
    (0, 2, 4, 6, 1, 3, 5, 7),
    (3, 1, 7, 5, 2, 0, 6, 4),
    (6, 0, 2, 4, 7, 1, 3, 5),
    (1, 7, 5, 3, 0, 6, 4, 2),
)


def to_row_group():
    pairs = []
    for row in range(8):
        for z in range(4):
            for j in range(8):
                far = (row // 4) != (j // 4)
                z_to = (z + 2) % 4 if far else z
                pairs.append((row * 32 + z * 8 + j, j * 32 + z_to * 8 + PLACE[j][row]))
    return pairs


def from_row_group():
    return [(b, a) for a, b in to_row_group()]


def far_bits(row):
    return sum(((r // 4) != (row // 4)) << PLACE[row][r] for r in range(8))


def mm(a, b):
    return jnp.dot(a, b, precision=FULL, preferred_element_type=jnp.float32)
def mmt(a, b):
    return lax.dot_general(a, b, (((1,), (1,)), ((), ())), precision=FULL, preferred_element_type=jnp.float32)


def factor_and_inverse(g):
    n = g.shape[0]
    same = lax.broadcasted_iota(jnp.int32, (n, n), 0) == lax.broadcasted_iota(jnp.int32, (n, n), 1)
    diagonal = jnp.where(same, g, 0.0)
    root = jnp.sqrt(jnp.sum(diagonal, axis=0, keepdims=True))
    root_down = jnp.sqrt(jnp.sum(diagonal, axis=1, keepdims=True))
    wide = jnp.concatenate([g / root, jnp.where(same, 1.0, 0.0)], axis=1) / root_down
    tiles = [wide[8 * b : 8 * b + 8, :] for b in range(n // 8)]
    solved = [jnp.zeros_like(tile) for tile in tiles]
    shape = tiles[0].shape
    down = lax.broadcasted_iota(jnp.int32, shape, 0)

    def lane(tile, k):
        return jnp.broadcast_to(tile[:, k : k + 1], shape)

    for k in range(0, n, 4):
        at, first = k // 8, k % 8
        r0, r1, r2, r3 = (
            jnp.broadcast_to(tiles[at][first + i : first + i + 1, :], shape) for i in range(4)
        )
        a10, a11 = lane(r1, k), lane(r1, k + 1)
        a20, a21, a22 = lane(r2, k), lane(r2, k + 1), lane(r2, k + 2)
        a30, a31, a32, a33 = lane(r3, k), lane(r3, k + 1), lane(r3, k + 2), lane(r3, k + 3)
        d0 = lane(r0, k)
        i0 = 1.0 / d0
        m10, m20, m30 = a10 * i0, a20 * i0, a30 * i0
        d1 = a11 - m10 * a10
        t21, t31 = a21 - m20 * a10, a31 - m30 * a10
        i1 = 1.0 / d1
        m21, m31 = t21 * i1, t31 * i1
        d2 = a22 - m20 * a20 - m21 * t21
        t32 = a32 - m30 * a20 - m31 * t21
        i2 = 1.0 / d2
        m32 = t32 * i2
        d3 = a33 - m30 * a30 - m31 * t31 - m32 * t32
        i3 = 1.0 / d3
        r1 = r1 - m10 * r0
        r2 = r2 - m20 * r0 - m21 * r1
        r3 = r3 - m30 * r0 - m31 * r1 - m32 * r2
        for i, (row, pivot) in enumerate(((r0, d0), (r1, d1), (r2, d2), (r3, d3))):
            solved[at] = jnp.where(down == first + i, row * (1.0 / jnp.sqrt(pivot)), solved[at])
        s0, s1, s2, s3 = r0 * i0, r1 * i1, r2 * i2, r3 * i3
        for b in range((k + 4) // 8, n // 8):
            c0, c1, c2, c3 = (lane(tiles[b], k + i) for i in range(4))
            c1 = c1 - m10 * c0
            c2 = c2 - m20 * c0 - m21 * c1
            c3 = c3 - m30 * c0 - m31 * c1 - m32 * c2
            less = tiles[b] - (c0 * s0 + c1 * s1) - (c2 * s2 + c3 * s3)
            tiles[b] = jnp.where(down >= 4, less, tiles[b]) if b == at else less
    wide = jnp.concatenate(solved, axis=0)
    keep = lax.broadcasted_iota(jnp.int32, (n, n), 0) <= lax.broadcasted_iota(jnp.int32, (n, n), 1)
    upper = jnp.where(keep, wide[:, :n], 0.0) * root
    return jnp.transpose(upper), wide[:, n:]


def first_step(scale, both_ref, history_ref, first_ref, second_ref, own_ref):
    n = both_ref.shape[0]
    g00 = both_ref[:, 3 * n : 4 * n] * scale
    g10 = both_ref[:, 4 * n : 5 * n] * scale
    low0, t0 = factor_and_inverse(g00)
    a0 = mmt(mm(t0, g10), t0)
    history_ref[0] = a0
    second_ref[:, 0:n] = -mm(a0, t0)
    second_ref[:, n : 2 * n] = t0
    p1 = second_ref[...]
    whole = jnp.concatenate(
        [
            jnp.concatenate([g00, jnp.transpose(g10)], axis=1),
            both_ref[:, 4 * n :] * scale,
        ],
        axis=0,
    )
    low1, t1 = factor_and_inverse(mmt(mm(p1, whole), p1))
    history_ref[1] = low1
    q1 = mm(t1, p1)
    second_ref[...] = q1
    own_ref[...] = mmt(mm(q1, whole), q1)
    first_ref[:, 0:n] = -lax.dot_general(
        low1, t0, (((0,), (0,)), ((), ())), precision=FULL, preferred_element_type=jnp.float32
    )
    first_ref[:, n : 3 * n] = q1


def last_step(
    scale, mean_ref, both_ref, half_ref, history0_ref, image_ref, second_ref, own_ref, x_ref, y_ref, z_ref,
    history_ref, out_ref, g_ref, p_ref, v_ref, s_ref,
):
    n = both_ref.shape[0]
    gram2 = (both_ref[:, 0 : 3 * n] + half_ref[:, 0 : 3 * n]) * scale
    eye = jnp.where(
        lax.broadcasted_iota(jnp.int32, (n, n), 0) == lax.broadcasted_iota(jnp.int32, (n, n), 1),
        jnp.broadcast_to(mean_ref[0:1, 0:1], (n, n)),
        0.0,
    )
    g_ref[0:n, 0:n] = both_ref[:, 3 * n : 4 * n] * scale
    g_ref[n : 2 * n, 0 : 2 * n] = both_ref[:, 4 * n :] * scale
    g_ref[0:n, n : 2 * n] = jnp.transpose(both_ref[:, 4 * n : 5 * n]) * scale
    g_ref[2 * n :, :] = gram2
    g_ref[0:n, 2 * n :] = jnp.transpose(gram2[:, 0:n])
    g_ref[n : 2 * n, 2 * n :] = jnp.transpose(gram2[:, n : 2 * n])
    history_ref[0, 0] = history0_ref[0] + eye
    history_ref[0, 1] = history0_ref[1]
    w1 = image_ref[...]
    q1 = second_ref[...]
    against = mm(w1, g_ref[...])
    a1 = mmt(against[:, 0 : 2 * n], q1)
    history_ref[1, 0] = a1 + eye
    s_ref[0:n] = mmt(against, w1)
    s_ref[n : 2 * n] = mm(a1, own_ref[...])
    s_ref[2 * n :] = mmt(a1 + a1 - s_ref[n : 2 * n], a1)
    low2, t2 = factor_and_inverse(s_ref[0:n] - s_ref[2 * n :])
    history_ref[1, 1] = low2
    p_ref[...] = mm(a1, q1)
    w1 = jnp.concatenate([w1[:, 0 : 2 * n] - p_ref[...], w1[:, 2 * n :]], axis=1)
    v_ref[0:n] = x_ref[...]
    v_ref[n : 2 * n] = y_ref[...]
    v_ref[2 * n :] = z_ref[...]
    out_ref[...] = mm(t2, mm(w1, v_ref[...]))


def parts_of(v):
    high = v.astype(jnp.bfloat16)
    return high, (v - high.astype(jnp.float32)).astype(jnp.bfloat16)


def split_blocks(
    length, energies_ref, blocks_ref, high_ref, low_ref, lead_ref, mean_ref, held, arrived
):
    slots, width = blocks_ref.shape[0], blocks_ref.shape[1]
    copies = [
        pltpu.make_async_copy(blocks_ref.at[s], held.at[s], arrived.at[s]) for s in range(slots)
    ]
    for copy in copies:
        copy.start()
    mean = jnp.sum(energies_ref[...], axis=1, keepdims=True) * (1.0 / length)
    mean_ref[...] = jnp.broadcast_to(mean, mean_ref.shape)
    row, col = lax.axis_index(ROW), lax.axis_index(COL)
    for s in range(slots):
        block_row = row + 8 * s
        shifted = energies_ref[...] - SHIFT
        lead_ref[s : s + 1, :] = shifted * jnp.where(block_row == col, 1.0, 0.0)
        weight = jnp.where(block_row < col, 1.0, jnp.where(block_row == col, 0.5, 0.0))
        copies[s].wait()
        rows = pl.ds(s * width, width)
        high_ref[rows, :], low_ref[rows, :] = parts_of(held[s] * weight)


def dot3(left, high, low, contract):
    rows = left[0].shape[0]
    dims = (((1,), (contract,)), ((), ()))
    both = lax.dot_general(
        jnp.concatenate(left, axis=0), high, dims, preferred_element_type=jnp.float32
    )
    rest = lax.dot_general(left[0], low, dims, preferred_element_type=jnp.float32)
    return both[:rows] + (both[rows:] + rest)


def down_kernel(four_ref, high_ref, low_ref, out_ref):
    slots, _, width = four_ref.shape
    total = None
    for s in range(slots):
        rows = pl.ds(s * width, width)
        term = dot3(parts_of(four_ref[s]), high_ref[rows, :], low_ref[rows, :], 0)
        total = term if total is None else total + term
    out_ref[...] = total


def across_kernel(lead_ref, own_ref, high_ref, low_ref, out_ref):
    slots, _, width = out_ref.shape
    left = parts_of(own_ref[...])
    for s in range(slots):
        rows = pl.ds(s * width, width)
        term = dot3(left, high_ref[rows, :], low_ref[rows, :], 1)
        out_ref[s] = term + lead_ref[s : s + 1, :] * own_ref[...]


def gram_kernel(*refs):
    *four_refs, out_ref, flat_ref = refs
    slots, vecs, width = four_refs[0].shape
    for i, four_ref in enumerate(four_refs):
        for s in range(slots):
            flat_ref[i * vecs : (i + 1) * vecs, s * width : (s + 1) * width] = four_ref[s]
    out_ref[...] = mmt(flat_ref[(len(four_refs) - 1) * vecs :, :], flat_ref[...])


LIMIT = pltpu.CompilerParams(vmem_limit_bytes=16 * 2**20)
IN_VMEM = pl.BlockSpec(memory_space=pltpu.VMEM)


def grams_of(*fours):
    slots, vecs, width = fours[0].shape
    return pl.pallas_call(
        gram_kernel,
        in_specs=[IN_VMEM] * len(fours),
        out_specs=IN_VMEM,
        out_shape=pltpu.VMEM((vecs, len(fours) * vecs), jnp.float32),
        scratch_shapes=[pltpu.VMEM((len(fours) * vecs, slots * width), jnp.float32)],
        compiler_params=LIMIT,
        name="gram",
    )(*fours)


def spread_kernel(parts_ref, out_ref):
    out_ref[...] = jnp.broadcast_to(jnp.sum(parts_ref[...], axis=0)[None], out_ref.shape)


def sum_spread(parts):
    return pl.pallas_call(
        spread_kernel,
        in_specs=[IN_VMEM],
        out_specs=IN_VMEM,
        out_shape=pltpu.VMEM(parts.shape, jnp.float32),
        compiler_params=LIMIT,
        name="sum_spread",
    )(parts)


def plus_kernel(left_ref, right_ref, out_ref):
    out_ref[...] = left_ref[...] + right_ref[...]


def plus(left, right):
    return pl.pallas_call(
        plus_kernel,
        in_specs=[IN_VMEM] * 2,
        out_specs=IN_VMEM,
        out_shape=pltpu.VMEM(left.shape, jnp.float32),
        compiler_params=LIMIT,
        name="plus",
    )(left, right)


def begin(both, length):
    vecs = both.shape[0]
    return pl.pallas_call(
        functools.partial(first_step, 1.0 / length),
        in_specs=[IN_VMEM],
        out_specs=(IN_VMEM,) * 4,
        out_shape=(
            pltpu.VMEM((2, vecs, vecs), jnp.float32),
            pltpu.VMEM((vecs, 3 * vecs), jnp.float32),
            pltpu.VMEM((vecs, 2 * vecs), jnp.float32),
            pltpu.VMEM((vecs, vecs), jnp.float32),
        ),
        compiler_params=LIMIT,
        cost_estimate=pl.CostEstimate(flops=6 * 10**9, bytes_accessed=10**5, transcendentals=0),
        name="first_step",
    )(both)


def close(mean, both, half, history0, image, second, own, x, y, z, length):
    vecs = x.shape[0]
    return pl.pallas_call(
        functools.partial(last_step, 1.0 / length),
        out_shape=(
            jax.ShapeDtypeStruct((2, 2, vecs, vecs), jnp.float32),
            jax.ShapeDtypeStruct(x.shape, jnp.float32),
        ),
        scratch_shapes=[
            pltpu.VMEM((3 * vecs, 3 * vecs), jnp.float32),
            pltpu.VMEM((vecs, 2 * vecs), jnp.float32),
            pltpu.VMEM((3 * vecs, x.shape[1]), jnp.float32),
            pltpu.VMEM((3 * vecs, vecs), jnp.float32),
        ],
        compiler_params=LIMIT,
        name="last_step",
    )(mean, both, half, history0, image, second, own, x, y, z)


PAIRS = ([(0, 1), (1, 0), (2, 3), (3, 2)], [(0, 3), (3, 0), (1, 2), (2, 1)])


def across_half(value):
    pairs = [(h * 4 + z, (1 - h) * 4 + (z + 2) % 4) for h in range(2) for z in range(4)]
    return lax.ppermute(value, ("zh", "z"), pairs)


def on_device(start_block, energies, hamiltonian):
    vecs, width = start_block.shape
    col_count = lax.axis_size(COL)
    half = width // 2
    row = lax.axis_index(ROW)
    col = lax.axis_index(COL)
    z = lax.axis_index("z")
    core = lax.axis_index("co")
    place = lax.axis_index(("x", "co"))
    blocks = hamiltonian[:, 0]
    slots = blocks.shape[0]
    bits = jnp.int32(0)
    for r in range(8):
        bits = jnp.where(row == r, jnp.int32(far_bits(r)), bits)
    far = lax.shift_right_logical(bits, place) % 2 == 1
    slot = jnp.where(far, (z + 2) % 4, z)
    odd = lax.rem(z, 2) == 1
    upper = (z >= 2) != far
    energies, slot, odd, upper, first = lax.optimization_barrier(
        (energies, slot, odd, upper, core == 0)
    )
    in_slot = (jnp.arange(slots) == slot)[:, None, None]
    every = NAMES

    high, low, lead, mean = pl.pallas_call(
        functools.partial(split_blocks, col_count * width),
        in_specs=[IN_VMEM, pl.BlockSpec(memory_space=pltpu.HBM)],
        out_specs=(IN_VMEM,) * 4,
        out_shape=(
            pltpu.VMEM((slots * width, width), jnp.bfloat16),
            pltpu.VMEM((slots * width, width), jnp.bfloat16),
            pltpu.VMEM((slots, width), jnp.float32),
            pltpu.VMEM((8, 128), jnp.float32),
        ),
        scratch_shapes=[
            pltpu.VMEM(blocks.shape, jnp.float32),
            pltpu.SemaphoreType.DMA((slots,)),
        ],
        compiler_params=pltpu.CompilerParams(vmem_limit_bytes=58 * 2**20),
        name="split_blocks",
    )(energies.reshape(1, width), blocks)

    def down(four):
        return pl.pallas_call(
            down_kernel,
            in_specs=[IN_VMEM] * 3,
            out_specs=IN_VMEM,
            out_shape=pltpu.VMEM((vecs, width), jnp.float32),
            compiler_params=LIMIT,
            name="down",
        )(four, high, low)

    def across(own):
        return pl.pallas_call(
            across_kernel,
            in_specs=[IN_VMEM] * 4,
            out_specs=IN_VMEM,
            out_shape=pltpu.VMEM((slots, vecs, width), jnp.float32),
            compiler_params=LIMIT,
            name="across",
        )(lead, own, high, low)

    def total(acrosses, downs, before, mean, far_mean, gram=None):
        arrived = lax.ppermute(downs, every, to_row_group())
        if far_mean is not None:
            arrived, far_mean = lax.optimization_barrier((arrived, far_mean))
            mean = mean + far_mean
        acrosses, gram = lax.optimization_barrier((acrosses, gram))
        part = acrosses + jnp.where(in_slot, arrived[None], 0.0)
        part = part.reshape(slots * vecs // 8, 8, width)
        low, high = part[..., :half], part[..., half:]
        mine = jnp.where(first, low, high)
        other = jnp.where(first, high, low)
        if gram is not None:
            other_half = across_half(gram)
        mine = mine + lax.ppermute(other, "co", [(0, 1), (1, 0)])
        pieces = lax.all_to_all(mine, ("z", "x"), 0, 0, tiled=True)
        whole = lax.all_to_all(sum_spread(pieces), ("z", "x"), 0, 0, tiled=True)
        if gram is not None:
            whole, other_half = lax.optimization_barrier((whole, other_half))
            gram = gram + other_half
        facing = lax.ppermute(whole, "co", [(0, 1), (1, 0)])
        low = jnp.where(first, whole, facing)
        high = jnp.where(first, facing, whole)
        four = jnp.concatenate([low, high], axis=-1).reshape(slots, vecs, width)
        four = four - (mean[:1, :1] - SHIFT)[None] * before
        return four, gram, mean

    def slot_of(four):
        return jnp.sum(jnp.where(in_slot, four, 0.0), axis=0)

    moved = lax.ppermute(start_block, every, to_row_group())
    mean = mean + lax.ppermute(mean, "co", [(0, 1), (1, 0)])
    mean = mean + lax.ppermute(mean, "x", PAIRS[0])
    moved, high, low, mean = lax.optimization_barrier((moved, high, low, mean))
    near = lax.ppermute(moved, "z", [(0, 1), (1, 0), (2, 3), (3, 2)])
    near, near_mean = lax.optimization_barrier((near, lax.ppermute(mean, "x", PAIRS[1])))
    mean = mean + near_mean
    two = jnp.stack([jnp.where(odd, near, moved), jnp.where(odd, moved, near)])
    over = lax.ppermute(two, "co", [(0, 1), (1, 0)])
    x4 = jnp.concatenate([jnp.where(upper, over, two), jnp.where(upper, two, over)])
    x = start_block
    downs, mean = lax.optimization_barrier((down(x4), mean))
    mean = mean + lax.ppermute(mean, "z", PAIRS[0])
    far_mean = lax.ppermute(mean, "z", [(0, 2), (2, 0), (1, 3), (3, 1)])
    y4, _, mean = total(across(x), downs, x4, mean, far_mean)
    y = lax.ppermute(slot_of(y4), every, from_row_group())
    downs = down(y4)
    y, x4_late, y4_late = lax.optimization_barrier((y, x4, y4))
    acrosses = across(y)
    gram = jnp.concatenate([grams_of(x4_late), grams_of(x4_late, y4_late)], axis=1)
    z4, gram, mean = total(acrosses, downs, y4, mean, None, gram)
    both = jnp.concatenate([grams_of(x4, y4, z4), gram], axis=1)
    zz = lax.ppermute(slot_of(z4), every, from_row_group())
    for pairs in PAIRS:
        both = plus(both, lax.ppermute(both, "y", pairs))
    other_half = across_half(both)
    length = col_count * width
    return close(mean, both, other_half, *begin(both, length), x, y, zz, length)


def solution(mesh):
    fine = Mesh(mesh.devices.reshape(SIZES), NAMES)
    placed = (P(None, COL), P(COL), P(ROW, COL, None, None))
    return jax.shard_map(
        on_device, mesh=fine, in_specs=placed, out_specs=(P(), P(None, COL)), check_vma=False
    )
```

```python
import functools

import jax
import jax.numpy as jnp
from jax import lax
from jax.experimental import pallas as pl
from jax.experimental.pallas import tpu as pltpu
from jax.sharding import Mesh
from jax.sharding import PartitionSpec as P

SHIFT = 5.5
FULL = lax.Precision.HIGHEST
BLOCKS = lax.Precision.HIGH

SIZES = (2, 4, 4, 4, 2)
NAMES = ("zh", "y", "z", "x", "co")
ROW = ("zh", "y")
COL = ("z", "x", "co")

PLACE = (
    (5, 3, 1, 7, 4, 2, 0, 6),
    (2, 4, 6, 0, 3, 5, 7, 1),
    (3, 1, 7, 5, 2, 0, 6, 4),
    (0, 2, 4, 6, 1, 3, 5, 7),
    (0, 2, 4, 6, 1, 3, 5, 7),
    (3, 1, 7, 5, 2, 0, 6, 4),
    (6, 0, 2, 4, 7, 1, 3, 5),
    (1, 7, 5, 3, 0, 6, 4, 2),
)


def to_row_group():
    pairs = []
    for row in range(8):
        for z in range(4):
            for j in range(8):
                far = (row // 4) != (j // 4)
                z_to = (z + 2) % 4 if far else z
                pairs.append((row * 32 + z * 8 + j, j * 32 + z_to * 8 + PLACE[j][row]))
    return pairs


def from_row_group():
    return [(b, a) for a, b in to_row_group()]


def far_bits(row):
    return sum(((r // 4) != (row // 4)) << PLACE[row][r] for r in range(8))


def mm(a, b):
    return jnp.dot(a, b, precision=FULL, preferred_element_type=jnp.float32)
def mmt(a, b):
    return lax.dot_general(a, b, (((1,), (1,)), ((), ())), precision=FULL, preferred_element_type=jnp.float32)


def factor_and_inverse(g):
    n = g.shape[0]
    same = lax.broadcasted_iota(jnp.int32, (n, n), 0) == lax.broadcasted_iota(jnp.int32, (n, n), 1)
    diagonal = jnp.where(same, g, 0.0)
    root = jnp.sqrt(jnp.sum(diagonal, axis=0, keepdims=True))
    root_down = jnp.sqrt(jnp.sum(diagonal, axis=1, keepdims=True))
    wide = jnp.concatenate([g / root, jnp.where(same, 1.0, 0.0)], axis=1) / root_down
    tiles = [wide[8 * b : 8 * b + 8, :] for b in range(n // 8)]
    solved = [jnp.zeros_like(tile) for tile in tiles]
    shape = tiles[0].shape
    down = lax.broadcasted_iota(jnp.int32, shape, 0)

    def lane(tile, k):
        return jnp.broadcast_to(tile[:, k : k + 1], shape)

    for k in range(0, n, 4):
        at, first = k // 8, k % 8
        r0, r1, r2, r3 = (
            jnp.broadcast_to(tiles[at][first + i : first + i + 1, :], shape) for i in range(4)
        )
        a10, a11 = lane(r1, k), lane(r1, k + 1)
        a20, a21, a22 = lane(r2, k), lane(r2, k + 1), lane(r2, k + 2)
        a30, a31, a32, a33 = lane(r3, k), lane(r3, k + 1), lane(r3, k + 2), lane(r3, k + 3)
        d0 = lane(r0, k)
        i0 = 1.0 / d0
        m10, m20, m30 = a10 * i0, a20 * i0, a30 * i0
        d1 = a11 - m10 * a10
        t21, t31 = a21 - m20 * a10, a31 - m30 * a10
        i1 = 1.0 / d1
        m21, m31 = t21 * i1, t31 * i1
        d2 = a22 - m20 * a20 - m21 * t21
        t32 = a32 - m30 * a20 - m31 * t21
        i2 = 1.0 / d2
        m32 = t32 * i2
        d3 = a33 - m30 * a30 - m31 * t31 - m32 * t32
        i3 = 1.0 / d3
        r1 = r1 - m10 * r0
        r2 = r2 - m20 * r0 - m21 * r1
        r3 = r3 - m30 * r0 - m31 * r1 - m32 * r2
        for i, (row, pivot) in enumerate(((r0, d0), (r1, d1), (r2, d2), (r3, d3))):
            solved[at] = jnp.where(down == first + i, row * (1.0 / jnp.sqrt(pivot)), solved[at])
        s0, s1, s2, s3 = r0 * i0, r1 * i1, r2 * i2, r3 * i3
        for b in range((k + 4) // 8, n // 8):
            c0, c1, c2, c3 = (lane(tiles[b], k + i) for i in range(4))
            c1 = c1 - m10 * c0
            c2 = c2 - m20 * c0 - m21 * c1
            c3 = c3 - m30 * c0 - m31 * c1 - m32 * c2
            less = tiles[b] - (c0 * s0 + c1 * s1) - (c2 * s2 + c3 * s3)
            tiles[b] = jnp.where(down >= 4, less, tiles[b]) if b == at else less
    wide = jnp.concatenate(solved, axis=0)
    keep = lax.broadcasted_iota(jnp.int32, (n, n), 0) <= lax.broadcasted_iota(jnp.int32, (n, n), 1)
    upper = jnp.where(keep, wide[:, :n], 0.0) * root
    return jnp.transpose(upper), wide[:, n:]


def first_step(scale, both_ref, history_ref, first_ref, second_ref, own_ref):
    n = both_ref.shape[0]
    g00 = both_ref[:, 3 * n : 4 * n] * scale
    g10 = both_ref[:, 4 * n : 5 * n] * scale
    low0, t0 = factor_and_inverse(g00)
    a0 = mmt(mm(t0, g10), t0)
    history_ref[0] = a0
    second_ref[:, 0:n] = -mm(a0, t0)
    second_ref[:, n : 2 * n] = t0
    p1 = second_ref[...]
    whole = jnp.concatenate(
        [
            jnp.concatenate([g00, jnp.transpose(g10)], axis=1),
            both_ref[:, 4 * n :] * scale,
        ],
        axis=0,
    )
    low1, t1 = factor_and_inverse(mmt(mm(p1, whole), p1))
    history_ref[1] = low1
    q1 = mm(t1, p1)
    second_ref[...] = q1
    own_ref[...] = mmt(mm(q1, whole), q1)
    first_ref[:, 0:n] = -lax.dot_general(
        low1, t0, (((0,), (0,)), ((), ())), precision=FULL, preferred_element_type=jnp.float32
    )
    first_ref[:, n : 3 * n] = q1


def last_step(
    scale, mean_ref, both_ref, half_ref, history0_ref, image_ref, second_ref, own_ref, x_ref, y_ref, z_ref,
    history_ref, out_ref, g_ref, p_ref, v_ref, s_ref,
):
    n = both_ref.shape[0]
    gram2 = (both_ref[:, 0 : 3 * n] + half_ref[:, 0 : 3 * n]) * scale
    eye = jnp.where(
        lax.broadcasted_iota(jnp.int32, (n, n), 0) == lax.broadcasted_iota(jnp.int32, (n, n), 1),
        jnp.broadcast_to(mean_ref[0:1, 0:1], (n, n)),
        0.0,
    )
    g_ref[0:n, 0:n] = both_ref[:, 3 * n : 4 * n] * scale
    g_ref[n : 2 * n, 0 : 2 * n] = both_ref[:, 4 * n :] * scale
    g_ref[0:n, n : 2 * n] = jnp.transpose(both_ref[:, 4 * n : 5 * n]) * scale
    g_ref[2 * n :, :] = gram2
    g_ref[0:n, 2 * n :] = jnp.transpose(gram2[:, 0:n])
    g_ref[n : 2 * n, 2 * n :] = jnp.transpose(gram2[:, n : 2 * n])
    history_ref[0, 0] = history0_ref[0] + eye
    history_ref[0, 1] = history0_ref[1]
    w1 = image_ref[...]
    q1 = second_ref[...]
    against = mm(w1, g_ref[...])
    a1 = mmt(against[:, 0 : 2 * n], q1)
    history_ref[1, 0] = a1 + eye
    s_ref[0:n] = mmt(against, w1)
    s_ref[n : 2 * n] = mm(a1, own_ref[...])
    s_ref[2 * n :] = mmt(a1 + a1 - s_ref[n : 2 * n], a1)
    low2, t2 = factor_and_inverse(s_ref[0:n] - s_ref[2 * n :])
    history_ref[1, 1] = low2
    p_ref[...] = mm(a1, q1)
    w1 = jnp.concatenate([w1[:, 0 : 2 * n] - p_ref[...], w1[:, 2 * n :]], axis=1)
    v_ref[0:n] = x_ref[...]
    v_ref[n : 2 * n] = y_ref[...]
    v_ref[2 * n :] = z_ref[...]
    out_ref[...] = mm(t2, mm(w1, v_ref[...]))


def parts_of(v):
    high = v.astype(jnp.bfloat16)
    return high, (v - high.astype(jnp.float32)).astype(jnp.bfloat16)


def split_blocks(
    length, energies_ref, blocks_ref, high_ref, low_ref, lead_ref, mean_ref, held, arrived
):
    slots, width = blocks_ref.shape[0], blocks_ref.shape[1]
    copies = [
        pltpu.make_async_copy(blocks_ref.at[s], held.at[s], arrived.at[s]) for s in range(slots)
    ]
    for copy in copies:
        copy.start()
    mean = jnp.sum(energies_ref[...], axis=1, keepdims=True) * (1.0 / length)
    mean_ref[...] = jnp.broadcast_to(mean, mean_ref.shape)
    row, col = lax.axis_index(ROW), lax.axis_index(COL)
    for s in range(slots):
        block_row = row + 8 * s
        shifted = energies_ref[...] - SHIFT
        lead_ref[s : s + 1, :] = shifted * jnp.where(block_row == col, 1.0, 0.0)
        weight = jnp.where(block_row < col, 1.0, jnp.where(block_row == col, 0.5, 0.0))
        copies[s].wait()
        rows = pl.ds(s * width, width)
        high_ref[rows, :], low_ref[rows, :] = parts_of(held[s] * weight)


def dot3(left, high, low, contract):
    rows = left[0].shape[0]
    dims = (((1,), (contract,)), ((), ()))
    both = lax.dot_general(
        jnp.concatenate(left, axis=0), high, dims, preferred_element_type=jnp.float32
    )
    rest = lax.dot_general(left[0], low, dims, preferred_element_type=jnp.float32)
    return both[:rows] + (both[rows:] + rest)


def down_kernel(four_ref, high_ref, low_ref, out_ref):
    slots, _, width = four_ref.shape
    total = None
    for s in range(slots):
        rows = pl.ds(s * width, width)
        term = dot3(parts_of(four_ref[s]), high_ref[rows, :], low_ref[rows, :], 0)
        total = term if total is None else total + term
    out_ref[...] = total


def across_kernel(lead_ref, own_ref, high_ref, low_ref, out_ref):
    slots, _, width = out_ref.shape
    left = parts_of(own_ref[...])
    for s in range(slots):
        rows = pl.ds(s * width, width)
        term = dot3(left, high_ref[rows, :], low_ref[rows, :], 1)
        out_ref[s] = term + lead_ref[s : s + 1, :] * own_ref[...]


def gram_kernel(*refs):
    *four_refs, out_ref, flat_ref = refs
    slots, vecs, width = four_refs[0].shape
    for i, four_ref in enumerate(four_refs):
        for s in range(slots):
            flat_ref[i * vecs : (i + 1) * vecs, s * width : (s + 1) * width] = four_ref[s]
    out_ref[...] = mmt(flat_ref[(len(four_refs) - 1) * vecs :, :], flat_ref[...])


LIMIT = pltpu.CompilerParams(vmem_limit_bytes=16 * 2**20)
IN_VMEM = pl.BlockSpec(memory_space=pltpu.VMEM)


def grams_of(*fours):
    slots, vecs, width = fours[0].shape
    return pl.pallas_call(
        gram_kernel,
        in_specs=[IN_VMEM] * len(fours),
        out_specs=IN_VMEM,
        out_shape=pltpu.VMEM((vecs, len(fours) * vecs), jnp.float32),
        scratch_shapes=[pltpu.VMEM((len(fours) * vecs, slots * width), jnp.float32)],
        compiler_params=LIMIT,
        name="gram",
    )(*fours)


def spread_kernel(parts_ref, out_ref):
    out_ref[...] = jnp.broadcast_to(jnp.sum(parts_ref[...], axis=0)[None], out_ref.shape)


def sum_spread(parts):
    return pl.pallas_call(
        spread_kernel,
        in_specs=[IN_VMEM],
        out_specs=IN_VMEM,
        out_shape=pltpu.VMEM(parts.shape, jnp.float32),
        compiler_params=LIMIT,
        name="sum_spread",
    )(parts)


def plus_kernel(left_ref, right_ref, out_ref):
    out_ref[...] = left_ref[...] + right_ref[...]


def plus(left, right):
    return pl.pallas_call(
        plus_kernel,
        in_specs=[IN_VMEM] * 2,
        out_specs=IN_VMEM,
        out_shape=pltpu.VMEM(left.shape, jnp.float32),
        compiler_params=LIMIT,
        name="plus",
    )(left, right)


def begin(both, length):
    vecs = both.shape[0]
    return pl.pallas_call(
        functools.partial(first_step, 1.0 / length),
        in_specs=[IN_VMEM],
        out_specs=(IN_VMEM,) * 4,
        out_shape=(
            pltpu.VMEM((2, vecs, vecs), jnp.float32),
            pltpu.VMEM((vecs, 3 * vecs), jnp.float32),
            pltpu.VMEM((vecs, 2 * vecs), jnp.float32),
            pltpu.VMEM((vecs, vecs), jnp.float32),
        ),
        compiler_params=LIMIT,
        cost_estimate=pl.CostEstimate(flops=6 * 10**9, bytes_accessed=10**5, transcendentals=0),
        name="first_step",
    )(both)


def close(mean, both, half, history0, image, second, own, x, y, z, length):
    vecs = x.shape[0]
    return pl.pallas_call(
        functools.partial(last_step, 1.0 / length),
        out_shape=(
            jax.ShapeDtypeStruct((2, 2, vecs, vecs), jnp.float32),
            jax.ShapeDtypeStruct(x.shape, jnp.float32),
        ),
        scratch_shapes=[
            pltpu.VMEM((3 * vecs, 3 * vecs), jnp.float32),
            pltpu.VMEM((vecs, 2 * vecs), jnp.float32),
            pltpu.VMEM((3 * vecs, x.shape[1]), jnp.float32),
            pltpu.VMEM((3 * vecs, vecs), jnp.float32),
        ],
        compiler_params=LIMIT,
        name="last_step",
    )(mean, both, half, history0, image, second, own, x, y, z)


PAIRS = ([(0, 1), (1, 0), (2, 3), (3, 2)], [(0, 3), (3, 0), (1, 2), (2, 1)])


def across_half(value):
    pairs = [(h * 4 + z, (1 - h) * 4 + (z + 2) % 4) for h in range(2) for z in range(4)]
    return lax.ppermute(value, ("zh", "z"), pairs)


def on_device(start_block, energies, hamiltonian):
    vecs, width = start_block.shape
    col_count = lax.axis_size(COL)
    half = width // 2
    row = lax.axis_index(ROW)
    col = lax.axis_index(COL)
    z = lax.axis_index("z")
    core = lax.axis_index("co")
    place = lax.axis_index(("x", "co"))
    blocks = hamiltonian[:, 0]
    slots = blocks.shape[0]
    bits = jnp.int32(0)
    for r in range(8):
        bits = jnp.where(row == r, jnp.int32(far_bits(r)), bits)
    far = lax.shift_right_logical(bits, place) % 2 == 1
    slot = jnp.where(far, (z + 2) % 4, z)
    odd = lax.rem(z, 2) == 1
    upper = (z >= 2) != far
    energies, slot, odd, upper, first = lax.optimization_barrier(
        (energies, slot, odd, upper, core == 0)
    )
    in_slot = (jnp.arange(slots) == slot)[:, None, None]
    every = NAMES

    high, low, lead, mean = pl.pallas_call(
        functools.partial(split_blocks, col_count * width),
        in_specs=[IN_VMEM, pl.BlockSpec(memory_space=pltpu.HBM)],
        out_specs=(IN_VMEM,) * 4,
        out_shape=(
            pltpu.VMEM((slots * width, width), jnp.bfloat16),
            pltpu.VMEM((slots * width, width), jnp.bfloat16),
            pltpu.VMEM((slots, width), jnp.float32),
            pltpu.VMEM((8, 128), jnp.float32),
        ),
        scratch_shapes=[
            pltpu.VMEM(blocks.shape, jnp.float32),
            pltpu.SemaphoreType.DMA((slots,)),
        ],
        compiler_params=pltpu.CompilerParams(vmem_limit_bytes=58 * 2**20),
        name="split_blocks",
    )(energies.reshape(1, width), blocks)

    def down(four):
        return pl.pallas_call(
            down_kernel,
            in_specs=[IN_VMEM] * 3,
            out_specs=IN_VMEM,
            out_shape=pltpu.VMEM((vecs, width), jnp.float32),
            compiler_params=LIMIT,
            name="down",
        )(four, high, low)

    def across(own):
        return pl.pallas_call(
            across_kernel,
            in_specs=[IN_VMEM] * 4,
            out_specs=IN_VMEM,
            out_shape=pltpu.VMEM((slots, vecs, width), jnp.float32),
            compiler_params=LIMIT,
            name="across",
        )(lead, own, high, low)

    def total(acrosses, downs, before, mean, far_mean, tau=None, gram=None):
        arrived = lax.ppermute(downs, every, to_row_group())
        if far_mean is not None:
            mean = mean + far_mean
            tau = jnp.broadcast_to(mean[None, :1, :1] - SHIFT, (1, vecs, width))
            acrosses, mean, tau = lax.optimization_barrier((acrosses, mean, tau))
        acrosses, gram = lax.optimization_barrier((acrosses, gram))
        part = acrosses + jnp.where(in_slot, arrived[None], 0.0)
        part = part.reshape(slots * vecs // 8, 8, width)
        low, high = part[..., :half], part[..., half:]
        mine = jnp.where(first, low, high)
        other = jnp.where(first, high, low)
        if gram is not None:
            other_half = across_half(gram)
        mine = mine + lax.ppermute(other, "co", [(0, 1), (1, 0)])
        pieces = lax.all_to_all(mine, ("z", "x"), 0, 0, tiled=True)
        whole = lax.all_to_all(sum_spread(pieces), ("z", "x"), 0, 0, tiled=True)
        if gram is not None:
            whole, other_half = lax.optimization_barrier((whole, other_half))
            gram = gram + other_half
        facing = lax.ppermute(whole, "co", [(0, 1), (1, 0)])
        low = jnp.where(first, whole, facing)
        high = jnp.where(first, facing, whole)
        four = jnp.concatenate([low, high], axis=-1).reshape(slots, vecs, width)
        four = four - tau * before
        return four, gram, mean, tau

    def slot_of(four):
        return jnp.sum(jnp.where(in_slot, four, 0.0), axis=0)

    moved = lax.ppermute(start_block, every, to_row_group())
    mean = mean + lax.ppermute(mean, "co", [(0, 1), (1, 0)])
    mean = mean + lax.ppermute(mean, "x", PAIRS[0])
    moved, high, low, mean = lax.optimization_barrier((moved, high, low, mean))
    near = lax.ppermute(moved, "z", [(0, 1), (1, 0), (2, 3), (3, 2)])
    near, near_mean = lax.optimization_barrier((near, lax.ppermute(mean, "x", PAIRS[1])))
    mean = mean + near_mean
    two = jnp.stack([jnp.where(odd, near, moved), jnp.where(odd, moved, near)])
    over = lax.ppermute(two, "co", [(0, 1), (1, 0)])
    x4 = jnp.concatenate([jnp.where(upper, over, two), jnp.where(upper, two, over)])
    x = start_block
    downs, mean = lax.optimization_barrier((down(x4), mean))
    mean = mean + lax.ppermute(mean, "z", PAIRS[0])
    far_mean = lax.ppermute(mean, "z", [(0, 2), (2, 0), (1, 3), (3, 1)])
    y4, _, mean, tau = total(across(x), downs, x4, mean, far_mean)
    y = lax.ppermute(slot_of(y4), every, from_row_group())
    downs = down(y4)
    y, x4_late, y4_late = lax.optimization_barrier((y, x4, y4))
    acrosses = across(y)
    gram = jnp.concatenate([grams_of(x4_late), grams_of(x4_late, y4_late)], axis=1)
    z4, gram, mean, tau = total(acrosses, downs, y4, mean, None, tau, gram)
    both = jnp.concatenate([grams_of(x4, y4, z4), gram], axis=1)
    zz = lax.ppermute(slot_of(z4), every, from_row_group())
    for pairs in PAIRS:
        both = plus(both, lax.ppermute(both, "y", pairs))
    other_half = across_half(both)
    length = col_count * width
    return close(mean, both, other_half, *begin(both, length), x, y, zz, length)


def solution(mesh):
    fine = Mesh(mesh.devices.reshape(SIZES), NAMES)
    placed = (P(None, COL), P(COL), P(ROW, COL, None, None))
    return jax.shard_map(
        on_device, mesh=fine, in_specs=placed, out_specs=(P(), P(None, COL)), check_vma=False
    )
```
